256 devices in a mesh: lon: 16 (over z, y_lo), lat: 16 (over y_hi, x, core).
Axes of the slice: x: 4, y: 4 (y_hi: 2, y_lo: 2; y = y_hi * 2 + y_lo), z: 8, core: 2. Of those that a mesh axis runs over, the one named last changes fastest.
Arguments:
- tracers: float32 [2, 4, 256, 2048], P(None, None, 'lat', 'lon'), may hold values from -6 to 6
- land_mask: int32 [256, 2048], P('lat', 'lon'), may hold values 0 or 1
- level_counts: int32 [256, 2048], P('lat', 'lon'), may hold values from 1 to 4
- fold_partner: int32 [2048], P('lon'), may hold values from 0 to 2047, as said below
- cotangent: float32 [2, 4, 256, 2048], P(None, None, 'lat', 'lon'), may hold values from -6 to 6
- w_first: float32 [6, 128], replicated, may hold values from -2.5 to 2.5
- b_first: float32 [128], replicated, may hold values from -3 to 3
- w_second: float32 [128, 128], replicated, may hold values from -0.5 to 0.5
- b_second: float32 [128], replicated, may hold values from -3 to 3
- w_head: float32 [128], replicated, may hold values from -0.5 to 0.5
- b_head: float32 [1], replicated, may hold values from -3 to 3
Outputs:
- tracers_out: float32 [2, 4, 256, 2048], P(None, None, 'lat', 'lon')
- tracer_grad: float32 [2, 4, 256, 2048], P(None, None, 'lat', 'lon')
- w_first_grad: float32 [6, 128], replicated
- w_second_grad: float32 [128, 128], replicated
- w_head_grad: float32 [128], replicated
The draws below stay inside these ranges and needn't reach their ends.
Inputs may be any that keep to these rules, and one draw needn't show every extreme that they name: fold_partner[x] = (s - x) mod 2048 for one odd whole number s of the draw: the mirror about the fold line, so fold_partner[fold_partner[x]] = x and fold_partner[x] != x.
All inputs are finite; a program needn't handle non-finite values. No bound on the sum of `land_mask` on one device may be relied on, other than what follows from the above.
Results may differ from the reference program's by a relative error of at most 0.0003.
Values sent between devices are 32-bit elements; how exact they have to be, the bound alone decides.
A program may use at most 128 MiB of HBM per device.

```python
import math
import jax
import jax.numpy as jnp
from jax import lax

NZ = 4
HID = 128
FEAT = 6
STEPS = 2
NX = 2048
NY = 256


def draw_fold_partner(key, part):
    key = jax.random.fold_in(key, 7)
    offset = 2 * jax.random.randint(key, (), 0, NX // 2).astype(jnp.int32) + 1
    columns = jnp.arange(NX, dtype=jnp.int32)
    return jnp.mod(offset - columns, NX).astype(jnp.int32)


def with_ends(drawn, stream_key, low, top_value):
    extent = drawn.shape
    place = [jax.random.randint(jax.random.fold_in(stream_key, axis), (), 0, extent[axis]) for axis in range(len(extent))]
    drawn = drawn.at[tuple(place)].set(low)
    longest = extent.index(max(extent))
    place[longest] = (place[longest] + 1) % extent[longest]
    return drawn.at[tuple(place)].set(top_value)


def steps_of(stream_key, extent, split, smallest, high):
    level = 1.0
    for dim, parts in split:
        steps = jax.random.uniform(jax.random.fold_in(jax.random.fold_in(stream_key, 6), dim), (parts,), jnp.float32, smallest / len(split), high / len(split))
        level = level * jnp.repeat(jnp.exp(steps), extent[dim] // parts).reshape((-1,) + (1,) * (len(extent) - 1 - dim))
    return level


def noise(key, extent, width, most, cuts=(), kind=jnp.bfloat16):
    level = steps_of(key, extent, cuts, -0.22, 0.18) if cuts else 1.0
    values = jax.random.normal(key, extent, jnp.float32) * width * level
    return jnp.minimum(jnp.maximum(values, -most), most).astype(kind)


def setup_inputs(seed: int = 0) -> dict:
    seeds = jax.random.split(jax.random.key(seed), 12)
    tracers = noise(seeds[0], (2, NZ, NY, NX), 1.0, 6.0, ((2, 16), (3, 16)), jnp.float32)
    land_mask = with_ends((jax.random.randint(seeds[1], (NY, NX), 0, 5) < 4).astype(jnp.int32), jax.random.fold_in(seeds[1], 1), 0, 1)
    level_counts = with_ends(jax.random.randint(seeds[2], (NY, NX), 1, NZ + 1), jax.random.fold_in(seeds[2], 1), 1, NZ).astype(jnp.int32)
    fold_partner = draw_fold_partner(jax.random.fold_in(seeds[11], 71), 0)
    cotangent = noise(seeds[4], (2, NZ, NY, NX), 1.0, 6.0, ((2, 16), (3, 16)), jnp.float32)
    w_first = noise(seeds[5], (FEAT, HID), FEAT ** -0.5, 2.5, (), jnp.float32)
    b_first = noise(seeds[6], (HID,), 0.5, 3.0, (), jnp.float32)
    w_second = noise(seeds[7], (HID, HID), HID ** -0.5, 0.5, (), jnp.float32)
    b_second = noise(seeds[8], (HID,), 0.5, 3.0, (), jnp.float32)
    w_head = noise(seeds[9], (HID,), HID ** -0.5, 0.5, (), jnp.float32)
    b_head = noise(seeds[10], (1,), 1.0, 3.0, (), jnp.float32)
    return {"tracers": tracers, "land_mask": land_mask, "level_counts": level_counts, "fold_partner": fold_partner, "cotangent": cotangent, "w_first": w_first, "b_first": b_first, "w_second": w_second, "b_second": b_second, "w_head": w_head, "b_head": b_head}


KMAX = 0.24
HIGH = lax.Precision.HIGHEST

def features(tracer, wet_cells):
    rest = [(0, 0)] * (tracer.ndim - 2)
    vertical = (tracer[:, 1:] - tracer[:, :-1]) * (wet_cells[1:] * wet_cells[:-1])
    upward = jnp.pad(-vertical, [(0, 0), (1, 0)] + rest)
    downward = jnp.pad(vertical, [(0, 0), (0, 1)] + rest)
    return jnp.concatenate([tracer, upward, downward], 0)

def closure(flat, w_first, b_first, w_second, b_second, w_head, b_head):
    first = jnp.tanh(jnp.dot(w_first.T, flat, precision=HIGH) + b_first[:, None])
    second = jnp.tanh(jnp.dot(w_second.T, first, precision=HIGH) + b_second[:, None])
    return jnp.dot(w_head, second, precision=HIGH) + b_head[0]

def global_kappa(tracer, wet_cells, weights):
    feats = features(tracer, wet_cells)
    levels_first = jnp.moveaxis(feats, 1, 0).reshape(NZ, FEAT, NY * NX)
    runner = jax.checkpoint(lambda block: closure(block, *weights))
    output = lax.map(runner, levels_first).reshape(NZ, NY, NX)
    return KMAX * jax.nn.sigmoid(output) * wet_cells

def shifted(field, partner):
    east = jnp.roll(field, -1, -1)
    west = jnp.roll(field, 1, -1)
    top_row = jnp.take(field[..., -1:, :], partner, axis=-1)
    north = jnp.concatenate([field[..., 1:, :], top_row], -2)
    south = jnp.concatenate([jnp.zeros_like(field[..., :1, :]), field[..., :-1, :]], -2)
    return [east, west, north, south]

def advance(tracer, wet_cells, partner, weights):
    kappa = global_kappa(tracer, wet_cells, weights)
    change = jnp.zeros_like(tracer)
    for t_side, k_side, w_side in zip(shifted(tracer, partner), shifted(kappa, partner), shifted(wet_cells, partner)):
        coefficient = 0.5 * (kappa + k_side) * wet_cells * w_side
        change = change + coefficient * (t_side - tracer)
    return tracer + change

def reference(tracers, land_mask, level_counts, fold_partner, cotangent, w_first, b_first, w_second, b_second, w_head, b_head):
    below = (jnp.arange(NZ, dtype=jnp.int32)[:, None, None] < level_counts[None]).astype(jnp.float32)
    wet_cells = land_mask[None].astype(jnp.float32) * below

    def forward(start, first, second, head_row):
        weights = (first, b_first, second, b_second, head_row, b_head)
        current = start
        for number in range(STEPS):
            current = advance(current, wet_cells, fold_partner, weights)
        return current
    final, pullback = jax.vjp(forward, tracers, w_first, w_second, w_head)
    grads = pullback(cotangent)
    scale = 1.0 / math.sqrt(NX * NY * NZ)
    return (final, grads[0], grads[1] * scale, grads[2] * scale, grads[3] * scale)
```

```python
import math

import jax
import jax.numpy as jnp
from jax import lax
from jax.experimental import pallas as pl
from jax.experimental.pallas import tpu as pltpu
from jax.sharding import PartitionSpec as P

KMAX = 0.24
F32 = jnp.float32
BF16 = jnp.bfloat16
MESH = pl.DeviceIdType.MESH

NZ = 4
ROWS = 16
COLS = 128
HID = 128
FIELDS = 2 * NZ
CHUNKS = NZ * ROWS // 8
LANES = 8 * COLS
EAST, WEST, NORTH, SOUTH = 0, 1, 2, 3
OPPOSITE = (WEST, EAST, SOUTH, NORTH)


def halves(x):
    high = x.astype(BF16)
    return high, (x - high.astype(F32)).astype(BF16)


def dot(a, b):
    return jnp.dot(a, b, preferred_element_type=F32)


def dot_nt(a, b):
    return lax.dot_general(a, b, (((1,), (1,)), ((), ())), preferred_element_type=F32)


def lane_roll(x, by):
    flat = x.reshape(-1, COLS)
    return pltpu.roll(flat, by % COLS, 1).reshape(x.shape)


def column(row):
    return jnp.broadcast_to(row, (COLS, COLS)).T


def kernel(
    lat_count, lon_count, sub,
    tracers, land, levels, partner, cotangent, w_first, b_first, w_second, b_second, w_head, b_head,
    tracers_out, tracer_grad, gw_first, gw_second, gw_head,
    w1_rows, w1_fwd, w1_bwd, w2_fwd, w2_bwd, bias2, head,
    wet_ext, pair, state0, state1, adj0, adj1, kap0, kap1, contrast0, contrast1, coef0, coef1,
    slope0, slope1, direct, feats0, feats1, logits, h1_0, h1_1, h2_0, h2_1, dz2, dz1, dfeat,
    obar, acc2, acc1, acch,
    send0, send1, send2, recv0, recv1, recv2, fold0, fold1, fold2,
    parts, parts_lat, parts_lon, total, gathered,
    send_sem, recv_sem, fold_send, fold_recv, sum_send, sum_recv,
):
    lat = lax.axis_index("lat")
    lon = lax.axis_index("lon")
    at_top = lat == lat_count - 1
    at_bottom = lat == 0
    east = lax.rem(lon + 1, lon_count)
    west = lax.rem(lon + lon_count - 1, lon_count)

    barrier = pltpu.get_barrier_semaphore()
    for o in range(1, lat_count):
        pl.semaphore_signal(
            barrier, inc=1, device_id={"lat": lax.rem(lat + o, lat_count), "lon": lon},
            device_id_type=MESH,
        )
    for o in range(1, lon_count):
        pl.semaphore_signal(
            barrier, inc=1, device_id={"lat": lat, "lon": lax.rem(lon + o, lon_count)},
            device_id_type=MESH,
        )

    lane3 = lax.broadcasted_iota(jnp.int32, (FIELDS, ROWS, COLS), 2)
    lane8 = lax.broadcasted_iota(jnp.int32, (8, COLS), 1)
    sub8 = lax.broadcasted_iota(jnp.int32, (8, COLS), 0)

    def to_side(phase, side, sends, recvs):
        target = {
            EAST: {"lat": lat, "lon": east},
            WEST: {"lat": lat, "lon": west},
            NORTH: {"lat": jnp.minimum(lat + 1, lat_count - 1), "lon": lon},
            SOUTH: {"lat": jnp.maximum(lat - 1, 0), "lon": lon},
        }[side]
        back = OPPOSITE[side]
        return pltpu.make_async_remote_copy(
            src_ref=sends.at[side], dst_ref=recvs.at[back],
            send_sem=send_sem.at[phase, side], recv_sem=recv_sem.at[phase, back],
            device_id=target, device_id_type=MESH,
        )

    def start_phase(phase, sends, recvs, folds):
        to_side(phase, EAST, sends, recvs).start()
        to_side(phase, WEST, sends, recvs).start()

        @pl.when(jnp.logical_not(at_top))
        def _():
            to_side(phase, NORTH, sends, recvs).start()

        @pl.when(jnp.logical_not(at_bottom))
        def _():
            to_side(phase, SOUTH, sends, recvs).start()

        @pl.when(at_top)
        def _():
            for o in range(1, lon_count):
                pltpu.make_async_remote_copy(
                    src_ref=sends.at[NORTH], dst_ref=folds.at[lon],
                    send_sem=fold_send.at[phase], recv_sem=fold_recv.at[phase],
                    device_id={"lat": lat, "lon": lax.rem(lon + o, lon_count)},
                    device_id_type=MESH,
                ).start()
            folds[lon] = sends[NORTH]

    def wait_phase(phase, sends, recvs, folds):
        to_side(phase, WEST, sends, recvs).wait_recv()
        to_side(phase, EAST, sends, recvs).wait_recv()

        @pl.when(jnp.logical_not(at_top))
        def _():
            to_side(phase, SOUTH, sends, recvs).wait_recv()

        @pl.when(jnp.logical_not(at_bottom))
        def _():
            to_side(phase, NORTH, sends, recvs).wait_recv()

        @pl.when(at_top)
        def _():
            others = folds.at[pl.ds(0, lon_count - 1)]
            pltpu.make_async_copy(others, others, fold_recv.at[phase]).wait()
            block = jnp.broadcast_to(partner[...] >> 7, (8, COLS))
            lane = jnp.broadcast_to(partner[...] & (COLS - 1), (8, COLS))
            for g in range(sends.shape[1] // 8):
                rows = pl.ds(8 * g, 8)
                picked = jnp.zeros((8, COLS), F32)
                for j in range(lon_count):
                    taken = jnp.take_along_axis(folds[j, rows, :], lane, axis=1)
                    picked = jnp.where(block == j, taken, picked)
                recvs[NORTH, rows, :] = picked

    def finish_phase(phase, sends, recvs, folds):
        to_side(phase, EAST, sends, recvs).wait_send()
        to_side(phase, WEST, sends, recvs).wait_send()

        @pl.when(jnp.logical_not(at_top))
        def _():
            to_side(phase, NORTH, sends, recvs).wait_send()

        @pl.when(jnp.logical_not(at_bottom))
        def _():
            to_side(phase, SOUTH, sends, recvs).wait_send()

        @pl.when(at_top)
        def _():
            others = folds.at[pl.ds(0, lon_count - 1)]
            pltpu.make_async_copy(others, others, fold_send.at[phase]).wait()

    def pack(ext, sends, at):
        turned = ext[:, 8:24, :].reshape(COLS, COLS).T
        sends[EAST, at : at + 8, :] = turned[COLS - 8 :]
        sends[WEST, at : at + 8, :] = turned[:8]
        for i in range(FIELDS):
            sends[NORTH, at + i : at + i + 1, :] = ext[i, 23:24, :]
            sends[SOUTH, at + i : at + i + 1, :] = ext[i, 8:9, :]

    def unpack(ext, recvs, at):
        for i in range(FIELDS):
            ext[i, 24:25, :] = recvs[NORTH, at + i : at + i + 1, :]
            ext[i, 7:8, :] = recvs[SOUTH, at + i : at + i + 1, :]

    def edge_columns(recvs, at):
        from_east = column(recvs[EAST, at : at + 1, :]).reshape(FIELDS, ROWS, COLS)
        from_west = column(recvs[WEST, at + 7 : at + 8, :]).reshape(FIELDS, ROWS, COLS)
        return from_east, from_west

    def sides(ext, from_east, from_west):
        core = ext[:, 8:24, :]
        lane = lane3[: core.shape[0]]
        return [
            jnp.where(lane == COLS - 1, from_east, lane_roll(core, -1)),
            jnp.where(lane == 0, from_west, lane_roll(core, 1)),
            ext[:, 9:25, :],
            ext[:, 7:23, :],
        ]

    def store_feature(feats, chunk, f, value):
        feats[chunk, pl.ds(f, 8, stride=8), :] = value

    def own_features(ext, feats):
        for half in range(2):
            rows = pl.ds(8 + 8 * half, 8)
            wets = [wet_ext[k, rows, :] for k in range(NZ)]
            for t in range(2):
                cells = [ext[NZ * t + k, rows, :] for k in range(NZ)]
                vertical = [
                    (cells[k + 1] - cells[k]) * (wets[k + 1] * wets[k]) for k in range(NZ - 1)
                ]
                zero = jnp.zeros((8, COLS), F32)
                for k in range(NZ):
                    chunk = 2 * k + half
                    store_feature(feats, chunk, t, cells[k])
                    store_feature(feats, chunk, 2 + t, -vertical[k - 1] if k > 0 else zero)
                    store_feature(feats, chunk, 4 + t, vertical[k] if k < NZ - 1 else zero)

    def halo_features(recvs, feats):
        north, south = recvs[NORTH, 0:8, :], recvs[SOUTH, 0:8, :]
        first = sub8 < NZ
        wet = jnp.where(first, recv0[NORTH, 16:24, :], pltpu.roll(recv0[SOUTH, 16:24, :], 4, 0))
        joint = jnp.where(
            lax.rem(sub8, NZ) == NZ - 1, 0.0, wet * pltpu.roll(wet, 7, 0)
        )
        fields = (
            jnp.where(first, north, pltpu.roll(south, 4, 0)),
            jnp.where(first, pltpu.roll(north, 4, 0), south),
        )
        for t, cells in enumerate(fields):
            vertical = (pltpu.roll(cells, 7, 0) - cells) * joint
            store_feature(feats, CHUNKS, t, cells)
            store_feature(feats, CHUNKS, 2 + t, -pltpu.roll(vertical, 1, 0))
            store_feature(feats, CHUNKS, 4 + t, vertical)
        east_row = jnp.broadcast_to(recvs[EAST, 0:1, :], (8, COLS))
        west_row = jnp.broadcast_to(recvs[WEST, 7:8, :], (8, COLS))
        first = lane8 < NZ * ROWS
        wet_col = edge_wet()
        joint = jnp.where(
            lax.rem(lane8, NZ * ROWS) >= (NZ - 1) * ROWS, 0.0,
            wet_col * pltpu.roll(wet_col, COLS - ROWS, 1),
        )
        fields = (
            jnp.where(first, east_row, pltpu.roll(west_row, NZ * ROWS, 1)),
            jnp.where(first, pltpu.roll(east_row, NZ * ROWS, 1), west_row),
        )
        for t, cells in enumerate(fields):
            vertical = (pltpu.roll(cells, COLS - ROWS, 1) - cells) * joint
            feats[CHUNKS + 1, t : t + 1, :] = cells[0:1]
            feats[CHUNKS + 1, 2 + t : 3 + t, :] = -pltpu.roll(vertical, ROWS, 1)[0:1]
            feats[CHUNKS + 1, 4 + t : 5 + t, :] = vertical[0:1]
        return wet

    def edge_wet():
        wet_east = jnp.broadcast_to(recv0[EAST, 16:17, :], (8, COLS))
        wet_west = jnp.broadcast_to(recv0[WEST, 23:24, :], (8, COLS))
        return jnp.where(lane8 < NZ * ROWS, wet_east, wet_west)

    def wide(x, n):
        return jnp.concatenate([x] * n, axis=1) if n > 1 else x

    def closure_chunk(feats, chunk, rows, h1_ref, h2_ref):
        for s in range(0, rows, sub):
            n = min(sub, rows - s)
            f = [feats[chunk, 8 * (s + q) : 8 * (s + q) + 8, :] for q in range(n)]
            f = jnp.concatenate(f, axis=1) if n > 1 else f[0]
            high = f.astype(BF16).astype(F32)
            low = f - high
            stacked = jnp.concatenate([high, low, high, low], axis=0).astype(BF16)
            h1 = jnp.tanh(dot(w1_fwd[...], stacked))
            h1_high, h1_low = halves(h1)
            pre2 = dot(w2_fwd[...], jnp.concatenate([h1_high, h1_low, h1_high], axis=0))
            h2 = jnp.tanh(pre2 + wide(bias2[...], n))
            o = jnp.sum(h2 * wide(head[...], n), axis=0, keepdims=True)
            for q in range(n):
                logits[chunk, s + q : s + q + 1, :] = o[:, COLS * q : COLS * (q + 1)]
            if h1_ref is not None:
                lanes = slice(COLS * s, COLS * (s + n))
                h1_ref[chunk, :HID, lanes] = h1_high
                h1_ref[chunk, HID:, lanes] = h1_low
                h2_ref[chunk, :, lanes] = h2

    def closure_own(feats, h1_ref, h2_ref):
        @pl.loop(0, CHUNKS)
        def _(chunk):
            closure_chunk(feats, chunk, 8, h1_ref, h2_ref)

    def kappa_from(o, wet):
        gate = jax.nn.sigmoid(o + b_head[0])
        return KMAX * gate * wet, KMAX * gate * (1.0 - gate) * wet

    def advance(phase, state, feats, sends, recvs, folds, h1_ref, h2_ref, kap, slope, contrast, coef):
        own_features(state, feats)
        closure_own(feats, h1_ref, h2_ref)
        wait_phase(phase, sends, recvs, folds)
        unpack(state, recvs, 0)
        if phase == 0:
            unpack(adj0, recvs, 8)
            unpack(wet_ext, recvs, 16)
            wet_east, wet_west = edge_columns(recvs, 16)
            wet = wet_ext[:NZ, 8:24, :]
            around = sides(wet_ext, wet_east, wet_west)
            for n in range(4):
                pair[n] = 0.5 * wet * around[n][:NZ]
        wet_halo = halo_features(recvs, feats)
        closure_chunk(feats, CHUNKS, 8, None, None)
        closure_chunk(feats, CHUNKS + 1, 1, None, None)
        for k in range(NZ):
            for half in range(2):
                rows = pl.ds(8 + 8 * half, 8)
                value, rise = kappa_from(logits[2 * k + half], wet_ext[k, rows, :])
                kap[k, rows, :] = value
                slope[2 * k + half] = rise
        value, _ = kappa_from(logits[CHUNKS], wet_halo)
        for k in range(NZ):
            kap[k, 24:25, :] = value[k : k + 1]
            kap[k, 7:8, :] = value[NZ + k : NZ + k + 1]
        value, _ = kappa_from(logits[CHUNKS + 1], edge_wet())
        kap_edges = column(value[0:1]).reshape(2, NZ, ROWS, COLS)
        kap_sides = sides(kap, kap_edges[0], kap_edges[1])
        tracer_sides = sides(state, *edge_columns(recvs, 0))
        core = state[:, 8:24, :]
        own_kap = kap[:, 8:24, :]
        change = jnp.zeros_like(core)
        for n in range(4):
            difference = tracer_sides[n] - core
            weight = (own_kap + kap_sides[n]) * pair[n]
            contrast[n] = difference
            coef[n] = weight
            change = change + jnp.concatenate([weight, weight], 0) * difference
        return core + change

    def pull_flux(adjoint, recvs, at, contrast, coef, slope):
        core = adjoint[:, 8:24, :]
        around = sides(adjoint, *edge_columns(recvs, at))
        total_direct = core
        kappa_bar = jnp.zeros((NZ, ROWS, COLS), F32)
        for n in range(4):
            difference = around[n] - core
            weight = coef[n]
            total_direct = total_direct + jnp.concatenate([weight, weight], 0) * difference
            product = contrast[n] * difference
            kappa_bar = kappa_bar - pair[n] * (product[:NZ] + product[NZ:])
        direct[...] = total_direct
        obar[...] = kappa_bar.reshape(CHUNKS, 8, COLS) * slope[...]

    def pull_closure(h1_ref, h2_ref):
        @pl.loop(0, CHUNKS)
        def _(chunk):
            heads = jnp.zeros((HID, COLS), F32)
            for s in range(0, 8, sub):
                n = min(sub, 8 - s)
                lanes = slice(COLS * s, COLS * (s + n))
                bar = [obar[chunk, s + q : s + q + 1, :] for q in range(n)]
                bar = jnp.concatenate(bar, axis=1) if n > 1 else bar[0]
                h2 = h2_ref[chunk, :, lanes]
                weighted = h2 * bar
                for q in range(n):
                    heads = heads + weighted[:, COLS * q : COLS * (q + 1)]
                d2_high, d2_low = halves(wide(head[...], n) * (bar - weighted * h2))
                dh1 = dot(w2_bwd[...], jnp.concatenate([d2_high, d2_low, d2_high], axis=0))
                h1 = h1_ref[chunk, :HID, lanes].astype(F32) + h1_ref[chunk, HID:, lanes].astype(F32)
                d1_high, d1_low = halves(dh1 * (1.0 - h1 * h1))
                dz2[chunk, :HID, lanes] = d2_high
                dz2[chunk, HID:, lanes] = d2_low
                dz1[chunk, :HID, lanes] = d1_high
                dz1[chunk, HID:, lanes] = d1_low
            acch[...] += heads

    def pull_features():
        @pl.loop(0, CHUNKS)
        def _(chunk):
            d1 = dz1[chunk]
            d = dot(w1_bwd[...], jnp.concatenate([d1, d1[:HID]], axis=0))
            for q in range(8):
                dfeat[chunk, 8 * q : 8 * q + 8, :] = d[:8, COLS * q : COLS * (q + 1)]

    def add_weights(feats, h1_ref):
        @pl.loop(0, CHUNKS)
        def _(chunk):
            acc2[...] += dot_nt(h1_ref[chunk], dz2[chunk])
            f = jnp.concatenate([feats[chunk, 8 * q : 8 * q + 8, :] for q in range(8)], axis=1)
            high = f.astype(BF16).astype(F32)
            stacked = jnp.concatenate([high, f - high], axis=0).astype(BF16)
            acc1[...] += dot_nt(stacked, dz1[chunk])

    def pull_state(store):
        for half in range(2):
            rows = pl.ds(8 * half, 8)
            wets = [wet_ext[k, pl.ds(8 + 8 * half, 8), :] for k in range(NZ)]
            for t in range(2):
                bar = [
                    [dfeat[2 * k + half, pl.ds(f, 8, stride=8), :] for k in range(NZ)]
                    for f in (t, 2 + t, 4 + t)
                ]
                vertical = [
                    (bar[2][k] - bar[1][k + 1]) * (wets[k + 1] * wets[k]) for k in range(NZ - 1)
                ]
                for k in range(NZ):
                    value = direct[NZ * t + k, rows, :] + bar[0][k]
                    if k < NZ - 1:
                        value = value - vertical[k]
                    if k > 0:
                        value = value + vertical[k - 1]
                    store(NZ * t + k, half, value)

    depth_here = land[...] * levels[...]
    for k in range(NZ):
        wet = (k < depth_here).astype(F32)
        wet_ext[k, 8:24, :] = wet
        wet_ext[NZ + k, 8:24, :] = wet
    state0[:, 8:24, :] = tracers[...]
    adj0[:, 8:24, :] = cotangent[...]
    pack(state0, send0, 0)
    pack(adj0, send0, 8)
    pack(wet_ext, send0, 16)

    @pl.when(at_bottom)
    def _():
        for recvs in (recv0, recv1, recv2):
            recvs[SOUTH] = jnp.zeros(recvs.shape[1:], F32)

    pl.semaphore_wait(barrier, lat_count + lon_count - 2)
    start_phase(0, send0, recv0, fold0)

    w1_rows[0:6, :] = w_first[...]
    w1_rows[6:7, :] = b_first[...]
    w1_rows[7:8, :] = jnp.zeros((1, HID), F32)
    w1 = w1_rows[...]
    w1_high = w1.astype(BF16).astype(F32)
    w1_low = w1 - w1_high
    tall = jnp.concatenate(
        [w1_high, w1_high, w1_low, w1_low, jnp.zeros((HID - 32, HID), F32)], axis=0
    )
    w1_fwd[...] = tall.T[:, :32].astype(BF16)
    blank = jnp.zeros((8, HID), F32)
    w1_high = jnp.concatenate([w1_high, blank], axis=0).astype(BF16)
    w1_low = jnp.concatenate([w1_low, blank], axis=0).astype(BF16)
    w1_bwd[...] = jnp.concatenate([w1_high, w1_high, w1_low], axis=1)
    w2 = w_second[...]
    high, low = halves(w2)
    w2_bwd[...] = jnp.concatenate([high, high, low], axis=1)
    high, low = halves(w2.T)
    w2_fwd[...] = jnp.concatenate([high, high, low], axis=1)
    bias2[...] = column(b_second[...])
    head[...] = column(w_head[...])
    ones_row = jnp.where(sub8 == 6, 1.0, 0.0)
    for feats in (feats0, feats1):
        for chunk in range(CHUNKS + 1):
            feats[chunk, pl.ds(6, 8, stride=8), :] = jnp.ones((8, COLS), F32)
            feats[chunk, pl.ds(7, 8, stride=8), :] = jnp.zeros((8, COLS), F32)
        feats[CHUNKS + 1, 0:8, :] = ones_row
    logits[CHUNKS + 1] = jnp.zeros((8, COLS), F32)
    acc2[...] = jnp.zeros_like(acc2)
    acc1[...] = jnp.zeros_like(acc1)
    acch[...] = jnp.zeros_like(acch)

    state1[:, 8:24, :] = advance(
        0, state0, feats0, send0, recv0, fold0, h1_0, h2_0, kap0, slope0, contrast0, coef0
    )
    pack(state1, send1, 0)
    start_phase(1, send1, recv1, fold1)
    tracers_out[...] = advance(
        1, state1, feats1, send1, recv1, fold1, h1_1, h2_1, kap1, slope1, contrast1, coef1
    )

    pull_flux(adj0, recv0, 8, contrast1, coef1, slope1)
    pull_closure(h1_1, h2_1)
    pull_features()

    def keep(i, half, value):
        adj1[i, 8 + 8 * half : 16 + 8 * half, :] = value

    pull_state(keep)
    pack(adj1, send2, 0)
    start_phase(2, send2, recv2, fold2)
    add_weights(feats1, h1_1)
    wait_phase(2, send2, recv2, fold2)
    unpack(adj1, recv2, 0)
    pull_flux(adj1, recv2, 0, contrast0, coef0, slope0)
    pull_closure(h1_0, h2_0)
    add_weights(feats0, h1_0)

    piece = HID // lat_count
    both = piece + 8
    second = (
        (acc2[HID:, HID:] + acc2[HID:, :HID]) + acc2[:HID, HID:]
    ) + acc2[:HID, :HID]
    first = (acc1[8:, :HID] + acc1[:8, HID:]) + acc1[:8, :HID]
    head_row = jnp.sum(acch[...].T, axis=0, keepdims=True)
    extra = jnp.where(sub8 == 6, jnp.broadcast_to(head_row, (8, COLS)), first)
    for p in range(lat_count):
        parts[p, :piece, :] = second[piece * p : piece * (p + 1)]
        parts[p, piece:, :] = extra

    def lat_copy(o, src, dst, step):
        return pltpu.make_async_remote_copy(
            src_ref=src, dst_ref=dst, send_sem=sum_send.at[step], recv_sem=sum_recv.at[step],
            device_id={"lat": lax.rem(lat + o, lat_count), "lon": lon}, device_id_type=MESH,
        )

    def lon_copy(o, src, dst, step):
        return pltpu.make_async_remote_copy(
            src_ref=src, dst_ref=dst, send_sem=sum_send.at[step], recv_sem=sum_recv.at[step],
            device_id={"lat": lat, "lon": lax.rem(lon + o, lon_count)}, device_id_type=MESH,
        )

    def wait_all(ref, count, sem):
        some = ref.at[pl.ds(0, count)]
        pltpu.make_async_copy(some, some, sem).wait()

    for o in range(1, lat_count):
        lat_copy(o, parts.at[lax.rem(lat + o, lat_count)], parts_lat.at[lat], 0).start()
    parts_lat[lat] = parts[lat]

    pull_features()

    def finish(i, half, value):
        tracer_grad[i, 8 * half : 8 * half + 8, :] = value

    pull_state(finish)

    wait_all(parts_lat, lat_count - 1, sum_recv.at[0])
    summed = parts_lat[0]
    for p in range(1, lat_count):
        summed = summed + parts_lat[p]
    parts_lon[lon] = summed
    for o in range(1, lon_count):
        lon_copy(o, parts_lon.at[lon], parts_lon.at[lon], 1).start()
    wait_all(parts_lon, lon_count - 1, sum_recv.at[1])
    summed = parts_lon[0]
    for p in range(1, lon_count):
        summed = summed + parts_lon[p]
    cells_all = lat_count * ROWS * lon_count * COLS * NZ
    summed = summed * (1.0 / math.sqrt(cells_all))
    gathered[lat] = summed[:piece]
    for o in range(1, lat_count):
        lat_copy(o, gathered.at[lat], gathered.at[lat], 2).start()
    gw_first[...] = summed[piece : piece + 6]
    gw_head[...] = summed[piece + 6 : piece + 7]
    wait_all(gathered, lat_count - 1, sum_recv.at[2])
    for p in range(lat_count):
        gw_second[piece * p : piece * (p + 1), :] = gathered[p]

    finish_phase(0, send0, recv0, fold0)
    finish_phase(1, send1, recv1, fold1)
    finish_phase(2, send2, recv2, fold2)
    wait_all(parts_lat, lat_count - 1, sum_send.at[0])
    wait_all(parts_lon, lon_count - 1, sum_send.at[1])
    wait_all(gathered, lat_count - 1, sum_send.at[2])


def per_device(lat_count, lon_count, sub, tracers, land_mask, level_counts, fold_partner, cotangent,
               w_first, b_first, w_second, b_second, w_head, b_head):
    field = (FIELDS, ROWS, COLS)
    ext = pltpu.VMEM((FIELDS, 32, COLS), F32)
    kap = pltpu.VMEM((NZ, 32, COLS), F32)
    feats = pltpu.VMEM((CHUNKS + 2, 64, COLS), F32)
    stack = pltpu.VMEM((CHUNKS, 2 * HID, LANES), BF16)
    dense = pltpu.VMEM((CHUNKS, HID, LANES), F32)
    tile = pltpu.VMEM((CHUNKS, 8, COLS), F32)
    piece = HID // lat_count
    both = piece + 8
    scratch = [
        pltpu.VMEM((8, HID), F32),
        pltpu.VMEM((HID, 32), BF16),
        pltpu.VMEM((16, 3 * HID), BF16),
        pltpu.VMEM((HID, 3 * HID), BF16),
        pltpu.VMEM((HID, 3 * HID), BF16),
        pltpu.VMEM((HID, COLS), F32),
        pltpu.VMEM((HID, COLS), F32),
        ext,
        pltpu.VMEM((4, NZ, ROWS, COLS), F32),
        ext, ext, ext, ext, kap, kap,
        pltpu.VMEM((4,) + field, F32),
        pltpu.VMEM((4,) + field, F32),
        pltpu.VMEM((4, NZ, ROWS, COLS), F32),
        pltpu.VMEM((4, NZ, ROWS, COLS), F32),
        tile, tile,
        pltpu.VMEM(field, F32),
        feats, feats,
        pltpu.VMEM((CHUNKS + 2, 8, COLS), F32),
        stack, stack, dense, dense, stack, stack,
        pltpu.VMEM((CHUNKS, 64, COLS), F32),
        tile,
        pltpu.VMEM((2 * HID, 2 * HID), F32),
        pltpu.VMEM((16, 2 * HID), F32),
        pltpu.VMEM((HID, COLS), F32),
    ]
    scratch += [pltpu.VMEM((4, n, COLS), F32) for n in (24, 8, 8)] * 2
    scratch += [pltpu.VMEM((lon_count, n, COLS), F32) for n in (24, 8, 8)]
    scratch += [
        pltpu.VMEM((lat_count, both, COLS), F32),
        pltpu.VMEM((lat_count, both, COLS), F32),
        pltpu.VMEM((lon_count, both, COLS), F32),
        pltpu.VMEM((8, COLS), F32),
        pltpu.VMEM((lat_count, piece, COLS), F32),
        pltpu.SemaphoreType.DMA((3, 4)),
        pltpu.SemaphoreType.DMA((3, 4)),
        pltpu.SemaphoreType.DMA((3,)),
        pltpu.SemaphoreType.DMA((3,)),
        pltpu.SemaphoreType.DMA((3,)),
        pltpu.SemaphoreType.DMA((3,)),
    ]
    vmem = pl.BlockSpec(memory_space=pltpu.VMEM)
    run = pl.pallas_call(
        lambda *refs: kernel(lat_count, lon_count, sub, *refs),
        out_shape=[
            jax.ShapeDtypeStruct(field, F32),
            jax.ShapeDtypeStruct(field, F32),
            jax.ShapeDtypeStruct((6, HID), F32),
            jax.ShapeDtypeStruct((HID, HID), F32),
            jax.ShapeDtypeStruct((1, HID), F32),
        ],
        in_specs=[vmem] * 10 + [pl.BlockSpec(memory_space=pltpu.SMEM)],
        out_specs=[vmem] * 5,
        scratch_shapes=scratch,
        compiler_params=pltpu.CompilerParams(
            collective_id=0, has_side_effects=True, vmem_limit_bytes=56 * 2**20
        ),
        name="adjoint_steps",
    )
    out, grad, first, second, head = run(
        tracers.reshape(field), land_mask, level_counts, fold_partner.reshape(1, COLS),
        cotangent.reshape(field), w_first, b_first.reshape(1, HID), w_second,
        b_second.reshape(1, HID), w_head.reshape(1, HID), b_head,
    )
    return (
        out.reshape(tracers.shape), grad.reshape(tracers.shape), first, second, head.reshape(HID)
    )


def solution(mesh):
    lat_count, lon_count = mesh.shape["lat"], mesh.shape["lon"]
    grid = P(None, None, "lat", "lon")
    return jax.shard_map(
        lambda *args: per_device(lat_count, lon_count, 2, *args),
        mesh=mesh,
        in_specs=(
            grid, P("lat", "lon"), P("lat", "lon"), P("lon"), grid,
            P(), P(), P(), P(), P(), P(),
        ),
        out_specs=(grid, grid, P(), P(), P()),
        check_vma=False,
    )
```

```python
import math

import jax
import jax.numpy as jnp
from jax import lax
from jax.experimental import pallas as pl
from jax.experimental.pallas import tpu as pltpu
from jax.sharding import PartitionSpec as P

KMAX = 0.24
F32 = jnp.float32
BF16 = jnp.bfloat16
MESH = pl.DeviceIdType.MESH

NZ = 4
ROWS = 16
COLS = 128
HID = 128
FIELDS = 2 * NZ
CHUNKS = NZ * ROWS // 8
LANES = 8 * COLS
EAST, WEST, NORTH, SOUTH = 0, 1, 2, 3
OPPOSITE = (WEST, EAST, SOUTH, NORTH)


PLANE = ("x", "y_high", "y_low")
PILLAR = ("core", "z")


def place_sizes(lat_count, lon_count):
    if lat_count == 16 and lon_count == 16:
        return {"core": 2, "x": 4, "y_high": 2, "y_low": 2, "z": 8}
    return {"core": 1, "x": lat_count, "y_high": 1, "y_low": 1, "z": lon_count}


def offsets(dims, sizes):
    steps = [{}]
    for d in dims:
        steps = [{**s, d: o} for s in steps for o in range(sizes[d])]

    def hops(s):
        y = {(0, 0): 0, (1, 0): 2, (0, 1): 1, (1, 1): 1}[s.get("y_high", 0), s.get("y_low", 0)]
        x, z = s.get("x", 0), s.get("z", 0)
        return y + min(x, sizes["x"] - x) + min(z, sizes["z"] - z)

    return sorted([s for s in steps if any(s.values())], key=hops, reverse=True)


def piece_rows(parts):
    return HID // parts, -(-8 // parts)


def halves(x):
    high = x.astype(BF16)
    return high, (x - high.astype(F32)).astype(BF16)


def dot(a, b):
    return jnp.dot(a, b, preferred_element_type=F32)


def dot_nt(a, b):
    return lax.dot_general(a, b, (((1,), (1,)), ((), ())), preferred_element_type=F32)


def lane_roll(x, by):
    flat = x.reshape(-1, COLS)
    return pltpu.roll(flat, by % COLS, 1).reshape(x.shape)


def column(row):
    return jnp.broadcast_to(row, (COLS, COLS)).T


def kernel(
    lat_count, lon_count, sub,
    tracers, land, levels, partner, cotangent, w_first, b_first, w_second, b_second, w_head, b_head,
    tracers_out, tracer_grad, gw_first, gw_second, gw_head,
    w1_rows, w1_fwd, w1_bwd, w2_fwd, w2_bwd, bias2, head,
    wet_ext, pair, state0, state1, adj0, adj1, kap0, kap1, contrast0, contrast1, coef0, coef1,
    slope0, slope1, direct, feats0, feats1, logits, h1_0, h1_1, h2_0, h2_1, dz2, dz1, dfeat,
    obar, acc2, acc1, acch,
    send0, send1, send2, recv0, recv1, recv2, fold0, fold1, fold2,
    parts, parts_plane, parts_pillar, gathered, extras,
    send_sem, recv_sem, fold_send, fold_recv, sum_send, sum_recv, in_sem,
):
    lat = lax.axis_index("lat")
    lon = lax.axis_index("lon")
    at_top = lat == lat_count - 1
    at_bottom = lat == 0
    east = lax.rem(lon + 1, lon_count)
    west = lax.rem(lon + lon_count - 1, lon_count)

    sizes = place_sizes(lat_count, lon_count)
    core_count, x_count, y_low_count = sizes["core"], sizes["x"], sizes["y_low"]
    here = {
        "core": lax.rem(lat, core_count),
        "x": lax.rem(lax.div(lat, core_count), x_count),
        "y_high": lax.div(lat, core_count * x_count),
        "y_low": lax.rem(lon, y_low_count),
        "z": lax.div(lon, y_low_count),
    }

    def device_at(at):
        return {
            "lat": (at["y_high"] * x_count + at["x"]) * core_count + at["core"],
            "lon": at["z"] * y_low_count + at["y_low"],
        }

    def moved(offset):
        return {d: lax.rem(here[d] + offset.get(d, 0), sizes[d]) for d in here}

    def slot(dims, at):
        index = 0
        for d in dims:
            index = index * sizes[d] + at[d]
        return index

    barrier = pltpu.get_barrier_semaphore()

    def greet(device):
        pl.semaphore_signal(barrier, inc=1, device_id=device, device_id_type=MESH)

    greeted = 4
    greet({"lat": lat, "lon": east})
    greet({"lat": lat, "lon": west})
    greet({"lat": lax.rem(lat + 1, lat_count), "lon": lon})
    greet({"lat": lax.rem(lat + lat_count - 1, lat_count), "lon": lon})
    for dims in (PLANE, PILLAR):
        for offset in offsets(dims, sizes):
            greet(device_at(moved(offset)))
            greeted += 1

    @pl.when(at_top)
    def _():
        for o in range(1, lon_count):
            greet({"lat": lat, "lon": lax.rem(lon + o, lon_count)})

    loads = [
        pltpu.make_async_copy(tracers, state0.at[:, pl.ds(8, ROWS), :], in_sem.at[0]),
        pltpu.make_async_copy(cotangent, adj0.at[:, pl.ds(8, ROWS), :], in_sem.at[1]),
    ]
    for load in loads:
        load.start()

    lane3 = lax.broadcasted_iota(jnp.int32, (FIELDS, ROWS, COLS), 2)
    lane8 = lax.broadcasted_iota(jnp.int32, (8, COLS), 1)
    sub8 = lax.broadcasted_iota(jnp.int32, (8, COLS), 0)

    def to_side(phase, side, sends, recvs):
        target = {
            EAST: {"lat": lat, "lon": east},
            WEST: {"lat": lat, "lon": west},
            NORTH: {"lat": jnp.minimum(lat + 1, lat_count - 1), "lon": lon},
            SOUTH: {"lat": jnp.maximum(lat - 1, 0), "lon": lon},
        }[side]
        back = OPPOSITE[side]
        return pltpu.make_async_remote_copy(
            src_ref=sends.at[side], dst_ref=recvs.at[back],
            send_sem=send_sem.at[phase, side], recv_sem=recv_sem.at[phase, back],
            device_id=target, device_id_type=MESH,
        )

    def start_phase(phase, sends, recvs, folds):
        to_side(phase, EAST, sends, recvs).start()
        to_side(phase, WEST, sends, recvs).start()

        @pl.when(jnp.logical_not(at_top))
        def _():
            to_side(phase, NORTH, sends, recvs).start()

        @pl.when(jnp.logical_not(at_bottom))
        def _():
            to_side(phase, SOUTH, sends, recvs).start()

        @pl.when(at_top)
        def _():
            for o in range(1, lon_count):
                pltpu.make_async_remote_copy(
                    src_ref=sends.at[NORTH], dst_ref=folds.at[lon],
                    send_sem=fold_send.at[phase], recv_sem=fold_recv.at[phase],
                    device_id={"lat": lat, "lon": lax.rem(lon + o, lon_count)},
                    device_id_type=MESH,
                ).start()
            folds[lon] = sends[NORTH]

    def wait_phase(phase, sends, recvs, folds):
        to_side(phase, WEST, sends, recvs).wait_recv()
        to_side(phase, EAST, sends, recvs).wait_recv()

        @pl.when(jnp.logical_not(at_top))
        def _():
            to_side(phase, SOUTH, sends, recvs).wait_recv()

        @pl.when(jnp.logical_not(at_bottom))
        def _():
            to_side(phase, NORTH, sends, recvs).wait_recv()

        @pl.when(at_top)
        def _():
            others = folds.at[pl.ds(0, lon_count - 1)]
            pltpu.make_async_copy(others, others, fold_recv.at[phase]).wait()
            block = jnp.broadcast_to(partner[...] >> 7, (8, COLS))
            lane = jnp.broadcast_to(partner[...] & (COLS - 1), (8, COLS))
            for g in range(sends.shape[1] // 8):
                rows = pl.ds(8 * g, 8)
                picked = jnp.zeros((8, COLS), F32)
                for j in range(lon_count):
                    taken = jnp.take_along_axis(folds[j, rows, :], lane, axis=1)
                    picked = jnp.where(block == j, taken, picked)
                recvs[NORTH, rows, :] = picked

    def finish_phase(phase, sends, recvs, folds):
        to_side(phase, EAST, sends, recvs).wait_send()
        to_side(phase, WEST, sends, recvs).wait_send()

        @pl.when(jnp.logical_not(at_top))
        def _():
            to_side(phase, NORTH, sends, recvs).wait_send()

        @pl.when(jnp.logical_not(at_bottom))
        def _():
            to_side(phase, SOUTH, sends, recvs).wait_send()

        @pl.when(at_top)
        def _():
            others = folds.at[pl.ds(0, lon_count - 1)]
            pltpu.make_async_copy(others, others, fold_send.at[phase]).wait()

    def pack(ext, sends, at):
        turned = ext[:, 8:24, :].reshape(COLS, COLS).T
        sends[EAST, at : at + 8, :] = turned[COLS - 8 :]
        sends[WEST, at : at + 8, :] = turned[:8]
        sends[NORTH, at : at + 8, :] = ext[:, 23, :]
        sends[SOUTH, at : at + 8, :] = ext[:, 8, :]

    def unpack(ext, recvs, at):
        ext[:, 24, :] = recvs[NORTH, at : at + 8, :]
        ext[:, 7, :] = recvs[SOUTH, at : at + 8, :]

    def edge_columns(recvs, at):
        first = pltpu.roll(recvs[WEST, at : at + 8, :], 1, 0)
        last = pltpu.roll(recvs[EAST, at : at + 8, :], 7, 0)
        middle = jnp.zeros((COLS - 16, COLS), F32)
        return jnp.concatenate([first, middle, last], axis=0).T.reshape(FIELDS, ROWS, COLS)

    def sides(ext, edges):
        core = ext[:, 8:24, :]
        lane = lane3[: core.shape[0]]
        return [
            jnp.where(lane == COLS - 1, edges, lane_roll(core, -1)),
            jnp.where(lane == 0, edges, lane_roll(core, 1)),
            ext[:, 9:25, :],
            ext[:, 7:23, :],
        ]

    def store_feature(feats, chunk, f, value):
        feats[chunk, pl.ds(f, 8, stride=8), :] = value

    def own_features(ext, feats):
        for half in range(2):
            rows = pl.ds(8 + 8 * half, 8)
            wets = [wet_ext[k, rows, :] for k in range(NZ)]
            for t in range(2):
                cells = [ext[NZ * t + k, rows, :] for k in range(NZ)]
                vertical = [
                    (cells[k + 1] - cells[k]) * (wets[k + 1] * wets[k]) for k in range(NZ - 1)
                ]
                zero = jnp.zeros((8, COLS), F32)
                for k in range(NZ):
                    chunk = 2 * k + half
                    store_feature(feats, chunk, t, cells[k])
                    store_feature(feats, chunk, 2 + t, -vertical[k - 1] if k > 0 else zero)
                    store_feature(feats, chunk, 4 + t, vertical[k] if k < NZ - 1 else zero)

    def halo_features(recvs, feats):
        north, south = recvs[NORTH, 0:8, :], recvs[SOUTH, 0:8, :]
        first = sub8 < NZ
        wet = jnp.where(first, recv0[NORTH, 16:24, :], pltpu.roll(recv0[SOUTH, 16:24, :], 4, 0))
        joint = jnp.where(
            lax.rem(sub8, NZ) == NZ - 1, 0.0, wet * pltpu.roll(wet, 7, 0)
        )
        fields = (
            jnp.where(first, north, pltpu.roll(south, 4, 0)),
            jnp.where(first, pltpu.roll(north, 4, 0), south),
        )
        for t, cells in enumerate(fields):
            vertical = (pltpu.roll(cells, 7, 0) - cells) * joint
            store_feature(feats, CHUNKS, t, cells)
            store_feature(feats, CHUNKS, 2 + t, -pltpu.roll(vertical, 1, 0))
            store_feature(feats, CHUNKS, 4 + t, vertical)
        east_row = jnp.broadcast_to(recvs[EAST, 0:1, :], (8, COLS))
        west_row = jnp.broadcast_to(recvs[WEST, 7:8, :], (8, COLS))
        first = lane8 < NZ * ROWS
        wet_col = edge_wet()
        joint = jnp.where(
            lax.rem(lane8, NZ * ROWS) >= (NZ - 1) * ROWS, 0.0,
            wet_col * pltpu.roll(wet_col, COLS - ROWS, 1),
        )
        fields = (
            jnp.where(first, east_row, pltpu.roll(west_row, NZ * ROWS, 1)),
            jnp.where(first, pltpu.roll(east_row, NZ * ROWS, 1), west_row),
        )
        for t, cells in enumerate(fields):
            vertical = (pltpu.roll(cells, COLS - ROWS, 1) - cells) * joint
            feats[CHUNKS + 1, t : t + 1, :] = cells[0:1]
            feats[CHUNKS + 1, 2 + t : 3 + t, :] = -pltpu.roll(vertical, ROWS, 1)[0:1]
            feats[CHUNKS + 1, 4 + t : 5 + t, :] = vertical[0:1]
        return wet

    def edge_wet():
        wet_east = jnp.broadcast_to(recv0[EAST, 16:17, :], (8, COLS))
        wet_west = jnp.broadcast_to(recv0[WEST, 23:24, :], (8, COLS))
        return jnp.where(lane8 < NZ * ROWS, wet_east, wet_west)

    def wide(x, n):
        return jnp.concatenate([x] * n, axis=1) if n > 1 else x

    def closure_chunk(feats, chunk, rows, h1_ref, h2_ref):
        for s in range(0, rows, sub):
            n = min(sub, rows - s)
            f = [feats[chunk, 8 * (s + q) : 8 * (s + q) + 8, :] for q in range(n)]
            f = jnp.concatenate(f, axis=1) if n > 1 else f[0]
            high = f.astype(BF16).astype(F32)
            low = f - high
            stacked = jnp.concatenate([high, low, high, low], axis=0).astype(BF16)
            h1 = jnp.tanh(dot(w1_fwd[...], stacked))
            h1_high, h1_low = halves(h1)
            pre2 = dot(w2_fwd[...], jnp.concatenate([h1_high, h1_low, h1_high], axis=0))
            h2 = jnp.tanh(pre2 + wide(bias2[...], n))
            o = jnp.sum(h2 * wide(head[...], n), axis=0, keepdims=True)
            for q in range(n):
                logits[chunk, s + q : s + q + 1, :] = o[:, COLS * q : COLS * (q + 1)]
            if h1_ref is not None:
                lanes = slice(COLS * s, COLS * (s + n))
                h1_ref[chunk, :HID, lanes] = h1_high
                h1_ref[chunk, HID:, lanes] = h1_low
                h2_ref[chunk, :, lanes] = h2

    def closure_own(feats, h1_ref, h2_ref):
        @pl.loop(0, CHUNKS, unroll=CHUNKS)
        def _(chunk):
            closure_chunk(feats, chunk, 8, h1_ref, h2_ref)

    def kappa_from(o, wet):
        gate = jax.nn.sigmoid(o + b_head[0])
        return KMAX * gate * wet, KMAX * gate * (1.0 - gate) * wet

    def advance(phase, state, feats, sends, recvs, folds, h1_ref, h2_ref, kap, slope, contrast, coef):
        own_features(state, feats)
        closure_own(feats, h1_ref, h2_ref)
        wait_phase(phase, sends, recvs, folds)
        unpack(state, recvs, 0)
        if phase == 0:
            unpack(adj0, recvs, 8)
            unpack(wet_ext, recvs, 16)
            wet = wet_ext[:NZ, 8:24, :]
            around = sides(wet_ext, edge_columns(recvs, 16))
            for n in range(4):
                pair[n] = 0.5 * wet * around[n][:NZ]
        wet_halo = halo_features(recvs, feats)
        closure_chunk(feats, CHUNKS, 8, None, None)
        closure_chunk(feats, CHUNKS + 1, 1, None, None)
        for k in range(NZ):
            for half in range(2):
                rows = pl.ds(8 + 8 * half, 8)
                value, rise = kappa_from(logits[2 * k + half], wet_ext[k, rows, :])
                kap[k, rows, :] = value
                slope[2 * k + half] = rise
        value, _ = kappa_from(logits[CHUNKS], wet_halo)
        for k in range(NZ):
            kap[k, 24:25, :] = value[k : k + 1]
            kap[k, 7:8, :] = value[NZ + k : NZ + k + 1]
        value, _ = kappa_from(logits[CHUNKS + 1], edge_wet())
        same = jnp.broadcast_to(value[0:1], (8, COLS))
        middle = jnp.zeros((COLS - 16, COLS), F32)
        kap_edges = jnp.concatenate([pltpu.roll(same, NZ * ROWS, 1), middle, same], axis=0).T
        kap_sides = sides(kap, kap_edges[: NZ * ROWS].reshape(NZ, ROWS, COLS))
        tracer_sides = sides(state, edge_columns(recvs, 0))
        core = state[:, 8:24, :]
        own_kap = kap[:, 8:24, :]
        change = jnp.zeros_like(core)
        for n in range(4):
            difference = tracer_sides[n] - core
            weight = (own_kap + kap_sides[n]) * pair[n]
            contrast[n] = difference
            coef[n] = weight
            change = change + jnp.concatenate([weight, weight], 0) * difference
        return core + change

    def pull_flux(adjoint, recvs, at, contrast, coef, slope):
        core = adjoint[:, 8:24, :]
        around = sides(adjoint, edge_columns(recvs, at))
        total_direct = core
        kappa_bar = jnp.zeros((NZ, ROWS, COLS), F32)
        for n in range(4):
            difference = around[n] - core
            weight = coef[n]
            total_direct = total_direct + jnp.concatenate([weight, weight], 0) * difference
            product = contrast[n] * difference
            kappa_bar = kappa_bar - pair[n] * (product[:NZ] + product[NZ:])
        direct[...] = total_direct
        obar[...] = kappa_bar.reshape(CHUNKS, 8, COLS) * slope[...]

    def pull_closure(h1_ref, h2_ref):
        @pl.loop(0, CHUNKS, unroll=CHUNKS)
        def _(chunk):
            heads = jnp.zeros((HID, COLS), F32)
            for s in range(0, 8, sub):
                n = min(sub, 8 - s)
                lanes = slice(COLS * s, COLS * (s + n))
                bar = [obar[chunk, s + q : s + q + 1, :] for q in range(n)]
                bar = jnp.concatenate(bar, axis=1) if n > 1 else bar[0]
                h2 = h2_ref[chunk, :, lanes]
                weighted = h2 * bar
                for q in range(n):
                    heads = heads + weighted[:, COLS * q : COLS * (q + 1)]
                d2_high, d2_low = halves(wide(head[...], n) * (bar - weighted * h2))
                dh1 = dot(w2_bwd[...], jnp.concatenate([d2_high, d2_low, d2_high], axis=0))
                h1 = h1_ref[chunk, :HID, lanes].astype(F32) + h1_ref[chunk, HID:, lanes].astype(F32)
                d1_high, d1_low = halves(dh1 * (1.0 - h1 * h1))
                dz2[chunk, :HID, lanes] = d2_high
                dz2[chunk, HID:, lanes] = d2_low
                dz1[chunk, :HID, lanes] = d1_high
                dz1[chunk, HID:, lanes] = d1_low
            acch[...] += heads

    def pull_features():
        @pl.loop(0, CHUNKS, unroll=CHUNKS)
        def _(chunk):
            d1 = dz1[chunk]
            d = dot(w1_bwd[...], jnp.concatenate([d1, d1[:HID]], axis=0))
            for q in range(8):
                dfeat[chunk, 8 * q : 8 * q + 8, :] = d[:8, COLS * q : COLS * (q + 1)]

    def add_weights(feats, h1_ref):
        @pl.loop(0, CHUNKS, unroll=CHUNKS)
        def _(chunk):
            acc2[...] += dot_nt(h1_ref[chunk], dz2[chunk])
            f = jnp.concatenate([feats[chunk, 8 * q : 8 * q + 8, :] for q in range(8)], axis=1)
            high = f.astype(BF16).astype(F32)
            stacked = jnp.concatenate([high, f - high], axis=0).astype(BF16)
            acc1[...] += dot_nt(stacked, dz1[chunk])

    def pull_state(store):
        for half in range(2):
            rows = pl.ds(8 * half, 8)
            wets = [wet_ext[k, pl.ds(8 + 8 * half, 8), :] for k in range(NZ)]
            for t in range(2):
                bar = [
                    [dfeat[2 * k + half, pl.ds(f, 8, stride=8), :] for k in range(NZ)]
                    for f in (t, 2 + t, 4 + t)
                ]
                vertical = [
                    (bar[2][k] - bar[1][k + 1]) * (wets[k + 1] * wets[k]) for k in range(NZ - 1)
                ]
                for k in range(NZ):
                    value = direct[NZ * t + k, rows, :] + bar[0][k]
                    if k < NZ - 1:
                        value = value - vertical[k]
                    if k > 0:
                        value = value + vertical[k - 1]
                    store(NZ * t + k, half, value)

    depth_here = land[...] * levels[...]
    for k in range(NZ):
        wet = (k < depth_here).astype(F32)
        wet_ext[k, 8:24, :] = wet
        wet_ext[NZ + k, 8:24, :] = wet
    pack(wet_ext, send0, 16)
    loads[0].wait()
    pack(state0, send0, 0)
    loads[1].wait()
    pack(adj0, send0, 8)

    @pl.when(at_bottom)
    def _():
        for recvs in (recv0, recv1, recv2):
            recvs[SOUTH] = jnp.zeros(recvs.shape[1:], F32)

    @pl.when(jnp.logical_not(at_top))
    def _():
        pl.semaphore_wait(barrier, greeted)

    @pl.when(at_top)
    def _():
        pl.semaphore_wait(barrier, greeted + lon_count - 1)

    start_phase(0, send0, recv0, fold0)

    w1_rows[0:6, :] = w_first[...]
    w1_rows[6:7, :] = b_first[...]
    w1_rows[7:8, :] = jnp.zeros((1, HID), F32)
    w1 = w1_rows[...]
    w1_high = w1.astype(BF16).astype(F32)
    w1_low = w1 - w1_high
    tall = jnp.concatenate(
        [w1_high, w1_high, w1_low, w1_low, jnp.zeros((HID - 32, HID), F32)], axis=0
    )
    w1_fwd[...] = tall.T[:, :32].astype(BF16)
    blank = jnp.zeros((8, HID), F32)
    w1_high = jnp.concatenate([w1_high, blank], axis=0).astype(BF16)
    w1_low = jnp.concatenate([w1_low, blank], axis=0).astype(BF16)
    w1_bwd[...] = jnp.concatenate([w1_high, w1_high, w1_low], axis=1)
    w2 = w_second[...]
    high, low = halves(w2)
    w2_bwd[...] = jnp.concatenate([high, high, low], axis=1)
    high, low = halves(w2.T)
    w2_fwd[...] = jnp.concatenate([high, high, low], axis=1)
    bias2[...] = column(b_second[...])
    head[...] = column(w_head[...])
    ones_row = jnp.where(sub8 == 6, 1.0, 0.0)
    for feats in (feats0, feats1):
        for chunk in range(CHUNKS + 1):
            feats[chunk, pl.ds(6, 8, stride=8), :] = jnp.ones((8, COLS), F32)
            feats[chunk, pl.ds(7, 8, stride=8), :] = jnp.zeros((8, COLS), F32)
        feats[CHUNKS + 1, 0:8, :] = ones_row
    logits[CHUNKS + 1] = jnp.zeros((8, COLS), F32)
    acc2[...] = jnp.zeros_like(acc2)
    acc1[...] = jnp.zeros_like(acc1)
    acch[...] = jnp.zeros_like(acch)

    state1[:, 8:24, :] = advance(
        0, state0, feats0, send0, recv0, fold0, h1_0, h2_0, kap0, slope0, contrast0, coef0
    )
    pack(state1, send1, 0)
    start_phase(1, send1, recv1, fold1)
    tracers_out[...] = advance(
        1, state1, feats1, send1, recv1, fold1, h1_1, h2_1, kap1, slope1, contrast1, coef1
    )

    pull_flux(adj0, recv0, 8, contrast1, coef1, slope1)
    pull_closure(h1_1, h2_1)
    pull_features()

    def keep(i, half, value):
        adj1[i, 8 + 8 * half : 16 + 8 * half, :] = value

    pull_state(keep)
    pack(adj1, send2, 0)
    start_phase(2, send2, recv2, fold2)
    add_weights(feats1, h1_1)
    wait_phase(2, send2, recv2, fold2)
    unpack(adj1, recv2, 0)
    pull_flux(adj1, recv2, 0, contrast0, coef0, slope0)
    pull_closure(h1_0, h2_0)
    add_weights(feats0, h1_0)

    plane = x_count * sizes["y_high"] * y_low_count
    pillar = core_count * sizes["z"]
    piece, spare = piece_rows(plane)
    second = (
        (acc2[HID:, HID:] + acc2[HID:, :HID]) + acc2[:HID, HID:]
    ) + acc2[:HID, :HID]
    first = (acc1[8:, :HID] + acc1[:8, HID:]) + acc1[:8, :HID]
    head_row = jnp.sum(acch[...].T, axis=0, keepdims=True)
    extra = jnp.where(sub8 == 6, jnp.broadcast_to(head_row, (8, COLS)), first)
    for p in range(plane):
        parts[p, :piece, :] = second[piece * p : piece * (p + 1)]
        if spare * p < 8:
            parts[p, piece:, :] = extra[spare * p : spare * (p + 1)]
        else:
            parts[p, piece:, :] = jnp.zeros((spare, COLS), F32)

    def share(dims, step, source, target):
        me = slot(dims, here)
        for offset in offsets(dims, sizes):
            there = moved(offset)
            pltpu.make_async_remote_copy(
                src_ref=source(slot(dims, there)), dst_ref=target.at[me],
                send_sem=sum_send.at[step], recv_sem=sum_recv.at[step],
                device_id=device_at(there), device_id_type=MESH,
            ).start()
        return me

    def wait_all(ref, count, sem):
        some = ref.at[pl.ds(0, count)]
        pltpu.make_async_copy(some, some, sem).wait()

    me = share(PLANE, 0, lambda there: parts.at[there], parts_plane)
    parts_plane[me] = parts[me]

    pull_features()

    def finish(i, half, value):
        tracer_grad[i, 8 * half : 8 * half + 8, :] = value

    pull_state(finish)

    wait_all(parts_plane, plane - 1, sum_recv.at[0])
    summed = parts_plane[0]
    for p in range(1, plane):
        summed = summed + parts_plane[p]
    me = slot(PILLAR, here)
    parts_pillar[me] = summed
    share(PILLAR, 1, lambda there: parts_pillar.at[me], parts_pillar)
    wait_all(parts_pillar, pillar - 1, sum_recv.at[1])
    summed = parts_pillar[0]
    for p in range(1, pillar):
        summed = summed + parts_pillar[p]
    cells_all = lat_count * ROWS * lon_count * COLS * NZ
    me = slot(PLANE, here)
    gathered[me] = summed * (1.0 / math.sqrt(cells_all))
    share(PLANE, 2, lambda there: gathered.at[me], gathered)
    wait_all(gathered, plane - 1, sum_recv.at[2])
    for p in range(plane):
        gw_second[piece * p : piece * (p + 1), :] = gathered[p, :piece, :]
        if spare * p < 8:
            extras[spare * p : spare * (p + 1), :] = gathered[p, piece:, :]
    gw_first[...] = extras[0:6, :]
    gw_head[...] = extras[6:7, :]

    finish_phase(0, send0, recv0, fold0)
    finish_phase(1, send1, recv1, fold1)
    finish_phase(2, send2, recv2, fold2)
    wait_all(parts_plane, plane - 1, sum_send.at[0])
    wait_all(parts_pillar, pillar - 1, sum_send.at[1])
    wait_all(gathered, plane - 1, sum_send.at[2])


def hand_over(*refs):
    for source, target in zip(refs[:5], refs[5:]):
        target[...] = source[...]


def per_device(lat_count, lon_count, sub, tracers, land_mask, level_counts, fold_partner, cotangent,
               w_first, b_first, w_second, b_second, w_head, b_head):
    field = (FIELDS, ROWS, COLS)
    ext = pltpu.VMEM((FIELDS, 32, COLS), F32)
    kap = pltpu.VMEM((NZ, 32, COLS), F32)
    feats = pltpu.VMEM((CHUNKS + 2, 64, COLS), F32)
    stack = pltpu.VMEM((CHUNKS, 2 * HID, LANES), BF16)
    dense = pltpu.VMEM((CHUNKS, HID, LANES), F32)
    tile = pltpu.VMEM((CHUNKS, 8, COLS), F32)
    sizes = place_sizes(lat_count, lon_count)
    plane = sizes["x"] * sizes["y_low"] * sizes["y_high"]
    pillar = sizes["core"] * sizes["z"]
    both = sum(piece_rows(plane))
    scratch = [
        pltpu.VMEM((8, HID), F32),
        pltpu.VMEM((HID, 32), BF16),
        pltpu.VMEM((16, 3 * HID), BF16),
        pltpu.VMEM((HID, 3 * HID), BF16),
        pltpu.VMEM((HID, 3 * HID), BF16),
        pltpu.VMEM((HID, COLS), F32),
        pltpu.VMEM((HID, COLS), F32),
        ext,
        pltpu.VMEM((4, NZ, ROWS, COLS), F32),
        ext, ext, ext, ext, kap, kap,
        pltpu.VMEM((4,) + field, F32),
        pltpu.VMEM((4,) + field, F32),
        pltpu.VMEM((4, NZ, ROWS, COLS), F32),
        pltpu.VMEM((4, NZ, ROWS, COLS), F32),
        tile, tile,
        pltpu.VMEM(field, F32),
        feats, feats,
        pltpu.VMEM((CHUNKS + 2, 8, COLS), F32),
        stack, stack, dense, dense, stack, stack,
        pltpu.VMEM((CHUNKS, 64, COLS), F32),
        tile,
        pltpu.VMEM((2 * HID, 2 * HID), F32),
        pltpu.VMEM((16, 2 * HID), F32),
        pltpu.VMEM((HID, COLS), F32),
    ]
    scratch += [pltpu.VMEM((4, n, COLS), F32) for n in (24, 8, 8)] * 2
    scratch += [pltpu.VMEM((lon_count, n, COLS), F32) for n in (24, 8, 8)]
    scratch += [
        pltpu.VMEM((plane, both, COLS), F32),
        pltpu.VMEM((plane, both, COLS), F32),
        pltpu.VMEM((pillar, both, COLS), F32),
        pltpu.VMEM((plane, both, COLS), F32),
        pltpu.VMEM((8, COLS), F32),
        pltpu.SemaphoreType.DMA((3, 4)),
        pltpu.SemaphoreType.DMA((3, 4)),
        pltpu.SemaphoreType.DMA((3,)),
        pltpu.SemaphoreType.DMA((3,)),
        pltpu.SemaphoreType.DMA((3,)),
        pltpu.SemaphoreType.DMA((3,)),
        pltpu.SemaphoreType.DMA((2,)),
    ]
    vmem = pl.BlockSpec(memory_space=pltpu.VMEM)
    anywhere = pl.BlockSpec(memory_space=pl.ANY)
    run = pl.pallas_call(
        lambda *refs: kernel(lat_count, lon_count, sub, *refs),
        out_shape=[
            jax.ShapeDtypeStruct(field, F32),
            jax.ShapeDtypeStruct(field, F32),
            jax.ShapeDtypeStruct((6, HID), F32),
            jax.ShapeDtypeStruct((HID, HID), F32),
            jax.ShapeDtypeStruct((1, HID), F32),
        ],
        in_specs=[anywhere] + [vmem] * 3 + [anywhere] + [vmem] * 5
        + [pl.BlockSpec(memory_space=pltpu.SMEM)],
        out_specs=[vmem] * 5,
        scratch_shapes=scratch,
        compiler_params=pltpu.CompilerParams(
            collective_id=0, has_side_effects=True, vmem_limit_bytes=56 * 2**20
        ),
        name="adjoint_steps",
    )
    results = run(
        tracers.reshape(field), land_mask, level_counts, fold_partner.reshape(1, COLS),
        cotangent.reshape(field), w_first, b_first.reshape(1, HID), w_second,
        b_second.reshape(1, HID), w_head.reshape(1, HID), b_head,
    )
    out, grad, first, second, head = pl.pallas_call(
        hand_over,
        out_shape=[jax.ShapeDtypeStruct(r.shape, F32) for r in results],
        in_specs=[vmem] * 5,
        out_specs=[vmem] * 5,
        name="hand_over",
    )(*results)
    return (
        out.reshape(tracers.shape), grad.reshape(tracers.shape), first, second, head.reshape(HID)
    )


def solution(mesh):
    lat_count, lon_count = mesh.shape["lat"], mesh.shape["lon"]
    grid = P(None, None, "lat", "lon")
    return jax.shard_map(
        lambda *args: per_device(lat_count, lon_count, 8, *args),
        mesh=mesh,
        in_specs=(
            grid, P("lat", "lon"), P("lat", "lon"), P("lon"), grid,
            P(), P(), P(), P(), P(), P(),
        ),
        out_specs=(grid, grid, P(), P(), P()),
        check_vma=False,
    )
```

```python
import math

import jax
import jax.numpy as jnp
from jax import lax
from jax.experimental import pallas as pl
from jax.experimental.pallas import tpu as pltpu
from jax.sharding import PartitionSpec as P

KMAX = 0.24
F32 = jnp.float32
BF16 = jnp.bfloat16
MESH = pl.DeviceIdType.MESH

NZ = 4
ROWS = 16
COLS = 128
HID = 128
FIELDS = 2 * NZ
CHUNKS = NZ * ROWS // 8
LANES = 8 * COLS
EAST, WEST, NORTH, SOUTH = 0, 1, 2, 3
HALF = NZ * ROWS
OPPOSITE = (WEST, EAST, SOUTH, NORTH)


PLANE = ("x", "y_high", "y_low")
PILLAR = ("core", "z")
RIM = ("z", "y_low")


def place_sizes(lat_count, lon_count):
    if lat_count == 16 and lon_count == 16:
        return {"core": 2, "x": 4, "y_high": 2, "y_low": 2, "z": 8}
    return {"core": 1, "x": lat_count, "y_high": 1, "y_low": 1, "z": lon_count}


def offsets(dims, sizes):
    steps = [{}]
    for d in dims:
        steps = [{**s, d: o} for s in steps for o in range(sizes[d])]

    def hops(s):
        y = {(0, 0): 0, (1, 0): 2, (0, 1): 1, (1, 1): 1}[s.get("y_high", 0), s.get("y_low", 0)]
        x, z = s.get("x", 0), s.get("z", 0)
        return y + min(x, sizes["x"] - x) + min(z, sizes["z"] - z)

    return sorted([s for s in steps if any(s.values())], key=hops, reverse=True)


def piece_rows(parts):
    return HID // parts, -(-8 // parts)


def halves(x):
    high = x.astype(BF16)
    return high, (x - high.astype(F32)).astype(BF16)


def dot(a, b):
    return jnp.dot(a, b, preferred_element_type=F32)


def dot_nt(a, b):
    return lax.dot_general(a, b, (((1,), (1,)), ((), ())), preferred_element_type=F32)


def lane_roll(x, by):
    flat = x.reshape(-1, COLS)
    return pltpu.roll(flat, by % COLS, 1).reshape(x.shape)


def column(row):
    return jnp.broadcast_to(row, (COLS, COLS)).T


def kernel(
    lat_count, lon_count,
    tracers, land, levels, partner, cotangent, w_first, b_first, w_second, b_second, w_head, b_head,
    tracers_out, tracer_grad, gw_first, gw_second, gw_head,
    w1_rows, w1_fwd, w1_bwd, w2_fwd, w2_bwd, bias2, head,
    wet_ext, pair, state0, state1, adj0, adj1, kap0, kap1, contrast0, contrast1, coef0, coef1,
    slope0, slope1, direct, feats0, feats1, logits, h1_0, h1_1, h2_0, h2_1, dz2, dz1,
    h1_edge, h2_edge, dfeat,
    obar, acc2, acc1, acch,
    send0, send1, send2, recv0, recv1, recv2, fold0, fold1, fold2,
    parts, parts_plane, parts_pillar, gathered, extras,
    send_sem, recv_sem, fold_send, fold_recv, sum_send, sum_recv, in_sem,
):
    lat = lax.axis_index("lat")
    lon = lax.axis_index("lon")
    at_top = lat == lat_count - 1
    at_bottom = lat == 0
    east = lax.rem(lon + 1, lon_count)
    west = lax.rem(lon + lon_count - 1, lon_count)

    sizes = place_sizes(lat_count, lon_count)
    core_count, x_count, y_low_count = sizes["core"], sizes["x"], sizes["y_low"]
    here = {
        "core": lax.rem(lat, core_count),
        "x": lax.rem(lax.div(lat, core_count), x_count),
        "y_high": lax.div(lat, core_count * x_count),
        "y_low": lax.rem(lon, y_low_count),
        "z": lax.div(lon, y_low_count),
    }

    def device_at(at):
        return {
            "lat": (at["y_high"] * x_count + at["x"]) * core_count + at["core"],
            "lon": at["z"] * y_low_count + at["y_low"],
        }

    def moved(offset):
        return {d: lax.rem(here[d] + offset.get(d, 0), sizes[d]) for d in here}

    def slot(dims, at):
        index = 0
        for d in dims:
            index = index * sizes[d] + at[d]
        return index

    barrier = pltpu.get_barrier_semaphore()

    def greet(device):
        pl.semaphore_signal(barrier, inc=1, device_id=device, device_id_type=MESH)

    @pl.when(at_top)
    def _():
        for offset in offsets(RIM, sizes):
            greet(device_at(moved(offset)))

    greeted = 4
    for dims in (PILLAR, PLANE):
        for offset in offsets(dims, sizes):
            greet(device_at(moved(offset)))
            greeted += 1
    greet({"lat": lat, "lon": east})
    greet({"lat": lat, "lon": west})
    greet({"lat": lax.rem(lat + 1, lat_count), "lon": lon})
    greet({"lat": lax.rem(lat + lat_count - 1, lat_count), "lon": lon})

    loads = [
        pltpu.make_async_copy(tracers, state0.at[:, pl.ds(8, ROWS), :], in_sem.at[0]),
        pltpu.make_async_copy(cotangent, adj0.at[:, pl.ds(8, ROWS), :], in_sem.at[1]),
    ]
    for load in loads:
        load.start()

    lane3 = lax.broadcasted_iota(jnp.int32, (FIELDS, ROWS, COLS), 2)
    lane8 = lax.broadcasted_iota(jnp.int32, (8, COLS), 1)
    sub8 = lax.broadcasted_iota(jnp.int32, (8, COLS), 0)

    def to_side(phase, side, sends, recvs):
        target = {
            EAST: {"lat": lat, "lon": east},
            WEST: {"lat": lat, "lon": west},
            NORTH: {"lat": jnp.minimum(lat + 1, lat_count - 1), "lon": lon},
            SOUTH: {"lat": jnp.maximum(lat - 1, 0), "lon": lon},
        }[side]
        back = OPPOSITE[side]
        return pltpu.make_async_remote_copy(
            src_ref=sends.at[side], dst_ref=recvs.at[back],
            send_sem=send_sem.at[phase, side], recv_sem=recv_sem.at[phase, back],
            device_id=target, device_id_type=MESH,
        )

    def start_phase(phase, sends, recvs, folds):
        @pl.when(at_top)
        def _():
            for offset in offsets(RIM, sizes):
                pltpu.make_async_remote_copy(
                    src_ref=sends.at[NORTH], dst_ref=folds.at[lon],
                    send_sem=fold_send.at[phase], recv_sem=fold_recv.at[phase],
                    device_id=device_at(moved(offset)), device_id_type=MESH,
                ).start()

        to_side(phase, EAST, sends, recvs).start()
        to_side(phase, WEST, sends, recvs).start()

        @pl.when(jnp.logical_not(at_top))
        def _():
            to_side(phase, NORTH, sends, recvs).start()

        @pl.when(jnp.logical_not(at_bottom))
        def _():
            to_side(phase, SOUTH, sends, recvs).start()

        @pl.when(at_top)
        def _():
            folds[lon] = sends[NORTH]

    def wait_phase(phase, sends, recvs, folds):
        to_side(phase, WEST, sends, recvs).wait_recv()
        to_side(phase, EAST, sends, recvs).wait_recv()

        @pl.when(jnp.logical_not(at_top))
        def _():
            to_side(phase, SOUTH, sends, recvs).wait_recv()

        @pl.when(jnp.logical_not(at_bottom))
        def _():
            to_side(phase, NORTH, sends, recvs).wait_recv()

        @pl.when(at_top)
        def _():
            others = folds.at[pl.ds(0, lon_count - 1)]
            pltpu.make_async_copy(others, others, fold_recv.at[phase]).wait()
            block = jnp.broadcast_to(partner[...] >> 7, (8, COLS))
            lane = jnp.broadcast_to(partner[...] & (COLS - 1), (8, COLS))
            for g in range(sends.shape[1] // 8):
                rows = pl.ds(8 * g, 8)
                picked = jnp.zeros((8, COLS), F32)
                for j in range(lon_count):
                    taken = jnp.take_along_axis(folds[j, rows, :], lane, axis=1)
                    picked = jnp.where(block == j, taken, picked)
                recvs[NORTH, rows, :] = picked

    def finish_phase(phase, sends, recvs, folds):
        to_side(phase, EAST, sends, recvs).wait_send()
        to_side(phase, WEST, sends, recvs).wait_send()

        @pl.when(jnp.logical_not(at_top))
        def _():
            to_side(phase, NORTH, sends, recvs).wait_send()

        @pl.when(jnp.logical_not(at_bottom))
        def _():
            to_side(phase, SOUTH, sends, recvs).wait_send()

        @pl.when(at_top)
        def _():
            others = folds.at[pl.ds(0, lon_count - 1)]
            pltpu.make_async_copy(others, others, fold_send.at[phase]).wait()

    def pack(ext, sends, at):
        turned = ext[:, 8:24, :].reshape(COLS, COLS).T
        sends[EAST, at : at + 8, :] = turned[COLS - 8 :]
        sends[WEST, at : at + 8, :] = turned[:8]
        sends[NORTH, at : at + 8, :] = ext[:, 23, :]
        sends[SOUTH, at : at + 8, :] = ext[:, 8, :]

    def unpack(ext, recvs, at):
        ext[:, 24, :] = recvs[NORTH, at : at + 8, :]
        ext[:, 7, :] = recvs[SOUTH, at : at + 8, :]

    def edge_columns(recvs, at):
        first = pltpu.roll(recvs[WEST, at : at + 8, :], 1, 0)
        last = pltpu.roll(recvs[EAST, at : at + 8, :], 7, 0)
        middle = jnp.zeros((COLS - 16, COLS), F32)
        return jnp.concatenate([first, middle, last], axis=0).T.reshape(FIELDS, ROWS, COLS)

    def sides(ext, edges):
        core = ext[:, 8:24, :]
        lane = lane3[: core.shape[0]]
        return [
            jnp.where(lane == COLS - 1, edges, lane_roll(core, -1)),
            jnp.where(lane == 0, edges, lane_roll(core, 1)),
            ext[:, 9:25, :],
            ext[:, 7:23, :],
        ]

    def store_feature(feats, chunk, f, value):
        feats[chunk, pl.ds(f, 8, stride=8), :] = value

    def own_features(ext, feats):
        for half in range(2):
            rows = pl.ds(8 + 8 * half, 8)
            wets = [wet_ext[k, rows, :] for k in range(NZ)]
            for t in range(2):
                cells = [ext[NZ * t + k, rows, :] for k in range(NZ)]
                vertical = [
                    (cells[k + 1] - cells[k]) * (wets[k + 1] * wets[k]) for k in range(NZ - 1)
                ]
                zero = jnp.zeros((8, COLS), F32)
                for k in range(NZ):
                    chunk = 2 * k + half
                    store_feature(feats, chunk, t, cells[k])
                    store_feature(feats, chunk, 2 + t, -vertical[k - 1] if k > 0 else zero)
                    store_feature(feats, chunk, 4 + t, vertical[k] if k < NZ - 1 else zero)

    def halo_features(recvs, feats):
        north, south = recvs[NORTH, 0:8, :], recvs[SOUTH, 0:8, :]
        first = sub8 < NZ
        wet = jnp.where(first, recv0[NORTH, 16:24, :], pltpu.roll(recv0[SOUTH, 16:24, :], 4, 0))
        joint = jnp.where(
            lax.rem(sub8, NZ) == NZ - 1, 0.0, wet * pltpu.roll(wet, 7, 0)
        )
        fields = (
            jnp.where(first, north, pltpu.roll(south, 4, 0)),
            jnp.where(first, pltpu.roll(north, 4, 0), south),
        )
        for t, cells in enumerate(fields):
            vertical = (pltpu.roll(cells, 7, 0) - cells) * joint
            store_feature(feats, CHUNKS, t, cells)
            store_feature(feats, CHUNKS, 2 + t, -pltpu.roll(vertical, 1, 0))
            store_feature(feats, CHUNKS, 4 + t, vertical)
        column_features(
            recvs[EAST, 0:1, :], recvs[WEST, 7:8, :], edge_wet(), feats, CHUNKS + 1
        )
        return wet

    def paired(east_row, west_row):
        east_row = jnp.broadcast_to(east_row, (8, COLS))
        west_row = jnp.broadcast_to(west_row, (8, COLS))
        first = lane8 < HALF
        return (
            jnp.where(first, east_row, pltpu.roll(west_row, HALF, 1)),
            jnp.where(first, pltpu.roll(east_row, HALF, 1), west_row),
        )

    def joint_column(wet_col):
        below = pltpu.roll(wet_col, COLS - ROWS, 1)
        return jnp.where(lax.rem(lane8, HALF) >= HALF - ROWS, 0.0, wet_col * below)

    def column_features(east_row, west_row, wet_col, feats, chunk):
        joint = joint_column(wet_col)
        for t, cells in enumerate(paired(east_row, west_row)):
            vertical = (pltpu.roll(cells, COLS - ROWS, 1) - cells) * joint
            feats[chunk, t : t + 1, :] = cells[0:1]
            feats[chunk, 2 + t : 3 + t, :] = -pltpu.roll(vertical, ROWS, 1)[0:1]
            feats[chunk, 4 + t : 5 + t, :] = vertical[0:1]

    def edge_wet():
        return paired(recv0[EAST, 16:17, :], recv0[WEST, 23:24, :])[0]

    def own_edge_wet():
        return paired(send0[EAST, 23:24, :], send0[WEST, 16:17, :])[0]

    def wide(x, n):
        return jnp.concatenate([x] * n, axis=1) if n > 1 else x

    def closure_chunk(feats, chunk, rows, h1_ref, h2_ref, at=None):
        at = chunk if at is None else at
        n = rows
        f = [feats[chunk, 8 * q : 8 * q + 8, :] for q in range(n)]
        f = jnp.concatenate(f, axis=1) if n > 1 else f[0]
        high = f.astype(BF16).astype(F32)
        low = f - high
        stacked = jnp.concatenate([high, low, high, low], axis=0).astype(BF16)
        h1 = jnp.tanh(dot(w1_fwd[...], stacked))
        h1_high, h1_low = halves(h1)
        pre2 = dot(w2_fwd[...], jnp.concatenate([h1_high, h1_low, h1_high], axis=0))
        h2 = jnp.tanh(pre2 + wide(bias2[...], n))
        o = jnp.sum(h2 * wide(head[...], n), axis=0, keepdims=True)
        for q in range(n):
            logits[chunk, q : q + 1, :] = o[:, COLS * q : COLS * (q + 1)]
        if h1_ref is not None:
            h1_ref[at, :HID, :] = h1_high
            h1_ref[at, HID:, :] = h1_low
            h2_ref[at] = h2

    def closure_own(feats, h1_ref, h2_ref):
        @pl.loop(0, CHUNKS, unroll=CHUNKS)
        def _(chunk):
            closure_chunk(feats, chunk, 8, h1_ref, h2_ref)

    def kappa_from(o, wet):
        gate = jax.nn.sigmoid(o + b_head[0])
        return KMAX * gate * wet, KMAX * gate * (1.0 - gate) * wet

    def advance(phase, state, feats, sends, recvs, folds, h1_ref, h2_ref, kap, slope, contrast, coef):
        own_features(state, feats)
        closure_own(feats, h1_ref, h2_ref)
        if phase == 1:
            column_features(
                sends[EAST, 7:8, :], sends[WEST, 0:1, :], own_edge_wet(), feats, CHUNKS + 2
            )
            closure_chunk(feats, CHUNKS + 2, 1, h1_edge, h2_edge, 0)
        wait_phase(phase, sends, recvs, folds)
        unpack(state, recvs, 0)
        if phase == 0:
            unpack(adj0, recvs, 8)
            unpack(wet_ext, recvs, 16)
            wet = wet_ext[:NZ, 8:24, :]
            around = sides(wet_ext, edge_columns(recvs, 16))
            for n in range(4):
                pair[n] = 0.5 * wet * around[n][:NZ]
        wet_halo = halo_features(recvs, feats)
        closure_chunk(feats, CHUNKS, 8, None, None)
        closure_chunk(feats, CHUNKS + 1, 1, None, None)
        for k in range(NZ):
            for half in range(2):
                rows = pl.ds(8 + 8 * half, 8)
                value, rise = kappa_from(logits[2 * k + half], wet_ext[k, rows, :])
                kap[k, rows, :] = value
                slope[2 * k + half] = rise
        value, _ = kappa_from(logits[CHUNKS], wet_halo)
        for k in range(NZ):
            kap[k, 24:25, :] = value[k : k + 1]
            kap[k, 7:8, :] = value[NZ + k : NZ + k + 1]
        value, _ = kappa_from(logits[CHUNKS + 1], edge_wet())
        same = jnp.broadcast_to(value[0:1], (8, COLS))
        middle = jnp.zeros((COLS - 16, COLS), F32)
        kap_edges = jnp.concatenate([pltpu.roll(same, NZ * ROWS, 1), middle, same], axis=0).T
        kap_sides = sides(kap, kap_edges[: NZ * ROWS].reshape(NZ, ROWS, COLS))
        tracer_sides = sides(state, edge_columns(recvs, 0))
        core = state[:, 8:24, :]
        own_kap = kap[:, 8:24, :]
        change = jnp.zeros_like(core)
        for n in range(4):
            difference = tracer_sides[n] - core
            weight = (own_kap + kap_sides[n]) * pair[n]
            contrast[n] = difference
            coef[n] = weight
            change = change + jnp.concatenate([weight, weight], 0) * difference
        return core + change

    def pull_flux(adjoint, recvs, at, contrast, coef, slope):
        core = adjoint[:, 8:24, :]
        around = sides(adjoint, edge_columns(recvs, at))
        total_direct = core
        kappa_bar = jnp.zeros((NZ, ROWS, COLS), F32)
        for n in range(4):
            difference = around[n] - core
            weight = coef[n]
            total_direct = total_direct + jnp.concatenate([weight, weight], 0) * difference
            product = contrast[n] * difference
            kappa_bar = kappa_bar - pair[n] * (product[:NZ] + product[NZ:])
        direct[...] = total_direct
        obar[...] = kappa_bar.reshape(CHUNKS, 8, COLS) * slope[...]

    def pull_cells(bar, h1_high, h1_low, h2):
        n = bar.shape[1] // COLS
        weighted = h2 * bar
        d2_high, d2_low = halves(wide(head[...], n) * (bar - weighted * h2))
        dh1 = dot(w2_bwd[...], jnp.concatenate([d2_high, d2_low, d2_high], axis=0))
        h1 = h1_high.astype(F32) + h1_low.astype(F32)
        d1_high, d1_low = halves(dh1 * (1.0 - h1 * h1))
        return weighted, d2_high, d2_low, d1_high, d1_low

    def pull_closure(h1_ref, h2_ref):
        @pl.loop(0, CHUNKS, unroll=CHUNKS)
        def _(chunk):
            bar = jnp.concatenate([obar[chunk, q : q + 1, :] for q in range(8)], axis=1)
            weighted, d2_high, d2_low, d1_high, d1_low = pull_cells(
                bar, h1_ref[chunk, :HID, :], h1_ref[chunk, HID:, :], h2_ref[chunk]
            )
            dz2[chunk, :HID, :] = d2_high
            dz2[chunk, HID:, :] = d2_low
            dz1[chunk, :HID, :] = d1_high
            dz1[chunk, HID:, :] = d1_low
            heads = weighted[:, :COLS]
            for q in range(1, 8):
                heads = heads + weighted[:, COLS * q : COLS * (q + 1)]
            acch[...] += heads

    def send_edges(h1_ref, h2_ref, sends):
        tops = [(2 * k + 1, 7) for k in range(NZ)]
        lows = [(2 * k, 0) for k in range(NZ)]
        places = tops + lows
        turned = jnp.concatenate(
            [obar[...].reshape(HALF, COLS), jnp.zeros((HALF, COLS), F32)], axis=0
        ).T
        column_bar = paired(turned[COLS - 1 :], turned[0:1])[0][0:1]
        bar = jnp.concatenate([obar[c, q : q + 1, :] for c, q in places] + [column_bar], axis=1)
        cut = [slice(COLS * q, COLS * (q + 1)) for _, q in places]
        high = [h1_ref[c, :HID, l] for (c, _), l in zip(places, cut)] + [h1_edge[0, :HID, :]]
        low = [h1_ref[c, HID:, l] for (c, _), l in zip(places, cut)] + [h1_edge[0, HID:, :]]
        h2 = [h2_ref[c, :, l] for (c, _), l in zip(places, cut)] + [h2_edge[0]]
        high, low, h2 = (jnp.concatenate(x, axis=1) for x in (high, low, h2))
        _, _, _, d1_high, d1_low = pull_cells(bar, high, low, h2)
        d = dot(w1_bwd[...], jnp.concatenate([d1_high, d1_low, d1_high], axis=0))
        d = [d[:8, COLS * i : COLS * (i + 1)] for i in range(len(places) + 1)]
        for side, y in ((NORTH, ROWS - 1), (SOUTH, 0)):
            rows = d[:NZ] if side == NORTH else d[NZ : 2 * NZ]
            wets = [wet_ext[k, 8 + y : 9 + y, :] for k in range(NZ)]
            vertical = [
                (pltpu.roll(rows[k], 4, 0) - pltpu.roll(rows[k + 1], 6, 0))
                * (wets[k + 1] * wets[k])
                for k in range(NZ - 1)
            ]
            for k in range(NZ):
                value = rows[k]
                if k < NZ - 1:
                    value = value - vertical[k]
                if k > 0:
                    value = value + vertical[k - 1]
                for t in range(2):
                    i = NZ * t + k
                    sends[side, i : i + 1, :] = value[t : t + 1] + direct[i, y : y + 1, :]
        cells = d[2 * NZ]
        vertical = pltpu.roll(cells, 4, 0) - pltpu.roll(pltpu.roll(cells, 6, 0), COLS - ROWS, 1)
        vertical = vertical * joint_column(own_edge_wet())
        value = cells - vertical + pltpu.roll(vertical, ROWS, 1)
        other = pltpu.roll(value, HALF, 1)
        first = lane8[0:1] < HALF
        turned = direct[...].reshape(COLS, COLS).T
        from_east = turned[COLS - 1 :] + jnp.where(first, value[0:1], other[1:2])
        from_west = turned[0:1] + jnp.where(first, other[0:1], value[1:2])
        sends[EAST] = jnp.broadcast_to(from_east, (8, COLS))
        sends[WEST] = jnp.broadcast_to(from_west, (8, COLS))

    def pull_features():
        @pl.loop(0, CHUNKS, unroll=CHUNKS)
        def _(chunk):
            d1 = dz1[chunk]
            d = dot(w1_bwd[...], jnp.concatenate([d1, d1[:HID]], axis=0))
            for q in range(8):
                dfeat[chunk, 8 * q : 8 * q + 8, :] = d[:8, COLS * q : COLS * (q + 1)]

    def add_weights(feats, h1_ref):
        @pl.loop(0, CHUNKS, unroll=CHUNKS)
        def _(chunk):
            acc2[...] += dot_nt(h1_ref[chunk], dz2[chunk])
            f = jnp.concatenate([feats[chunk, 8 * q : 8 * q + 8, :] for q in range(8)], axis=1)
            high = f.astype(BF16).astype(F32)
            stacked = jnp.concatenate([high, f - high], axis=0).astype(BF16)
            acc1[...] += dot_nt(stacked, dz1[chunk])

    def pull_state(store):
        for half in range(2):
            rows = pl.ds(8 * half, 8)
            wets = [wet_ext[k, pl.ds(8 + 8 * half, 8), :] for k in range(NZ)]
            for t in range(2):
                bar = [
                    [dfeat[2 * k + half, pl.ds(f, 8, stride=8), :] for k in range(NZ)]
                    for f in (t, 2 + t, 4 + t)
                ]
                vertical = [
                    (bar[2][k] - bar[1][k + 1]) * (wets[k + 1] * wets[k]) for k in range(NZ - 1)
                ]
                for k in range(NZ):
                    value = direct[NZ * t + k, rows, :] + bar[0][k]
                    if k < NZ - 1:
                        value = value - vertical[k]
                    if k > 0:
                        value = value + vertical[k - 1]
                    store(NZ * t + k, half, value)

    depth_here = land[...] * levels[...]
    for k in range(NZ):
        wet = (k < depth_here).astype(F32)
        wet_ext[k, 8:24, :] = wet
        wet_ext[NZ + k, 8:24, :] = wet
    pack(wet_ext, send0, 16)
    loads[0].wait()
    pack(state0, send0, 0)
    loads[1].wait()
    pack(adj0, send0, 8)

    @pl.when(at_bottom)
    def _():
        for recvs in (recv0, recv1, recv2):
            recvs[SOUTH] = jnp.zeros(recvs.shape[1:], F32)

    @pl.when(jnp.logical_not(at_top))
    def _():
        pl.semaphore_wait(barrier, greeted)

    @pl.when(at_top)
    def _():
        pl.semaphore_wait(barrier, greeted + lon_count - 1)

    start_phase(0, send0, recv0, fold0)

    w1_rows[0:6, :] = w_first[...]
    w1_rows[6:7, :] = b_first[...]
    w1_rows[7:8, :] = jnp.zeros((1, HID), F32)
    w1 = w1_rows[...]
    w1_high = w1.astype(BF16).astype(F32)
    w1_low = w1 - w1_high
    tall = jnp.concatenate(
        [w1_high, w1_high, w1_low, w1_low, jnp.zeros((HID - 32, HID), F32)], axis=0
    )
    w1_fwd[...] = tall.T[:, :32].astype(BF16)
    blank = jnp.zeros((8, HID), F32)
    w1_high = jnp.concatenate([w1_high, blank], axis=0).astype(BF16)
    w1_low = jnp.concatenate([w1_low, blank], axis=0).astype(BF16)
    w1_bwd[...] = jnp.concatenate([w1_high, w1_high, w1_low], axis=1)
    w2 = w_second[...]
    high, low = halves(w2)
    w2_bwd[...] = jnp.concatenate([high, high, low], axis=1)
    high, low = halves(w2.T)
    w2_fwd[...] = jnp.concatenate([high, high, low], axis=1)
    bias2[...] = column(b_second[...])
    head[...] = column(w_head[...])
    ones_row = jnp.where(sub8 == 6, 1.0, 0.0)
    for feats in (feats0, feats1):
        for chunk in range(CHUNKS + 1):
            feats[chunk, pl.ds(6, 8, stride=8), :] = jnp.ones((8, COLS), F32)
            feats[chunk, pl.ds(7, 8, stride=8), :] = jnp.zeros((8, COLS), F32)
        feats[CHUNKS + 1, 0:8, :] = ones_row
        feats[CHUNKS + 2, 0:8, :] = ones_row
    logits[CHUNKS + 1] = jnp.zeros((8, COLS), F32)
    acc2[...] = jnp.zeros_like(acc2)
    acc1[...] = jnp.zeros_like(acc1)
    acch[...] = jnp.zeros_like(acch)

    state1[:, 8:24, :] = advance(
        0, state0, feats0, send0, recv0, fold0, h1_0, h2_0, kap0, slope0, contrast0, coef0
    )
    pack(state1, send1, 0)
    start_phase(1, send1, recv1, fold1)
    tracers_out[...] = advance(
        1, state1, feats1, send1, recv1, fold1, h1_1, h2_1, kap1, slope1, contrast1, coef1
    )

    pull_flux(adj0, recv0, 8, contrast1, coef1, slope1)
    send_edges(h1_1, h2_1, send2)
    start_phase(2, send2, recv2, fold2)
    pull_closure(h1_1, h2_1)
    pull_features()

    def keep(i, half, value):
        adj1[i, 8 + 8 * half : 16 + 8 * half, :] = value

    pull_state(keep)
    add_weights(feats1, h1_1)
    wait_phase(2, send2, recv2, fold2)
    unpack(adj1, recv2, 0)
    pull_flux(adj1, recv2, 0, contrast0, coef0, slope0)
    pull_closure(h1_0, h2_0)
    add_weights(feats0, h1_0)

    plane = x_count * sizes["y_high"] * y_low_count
    pillar = core_count * sizes["z"]
    piece, spare = piece_rows(plane)
    second = (
        (acc2[HID:, HID:] + acc2[HID:, :HID]) + acc2[:HID, HID:]
    ) + acc2[:HID, :HID]
    first = (acc1[8:, :HID] + acc1[:8, HID:]) + acc1[:8, :HID]
    head_row = jnp.sum(acch[...].T, axis=0, keepdims=True)
    extra = jnp.where(sub8 == 6, jnp.broadcast_to(head_row, (8, COLS)), first)
    for p in range(plane):
        parts[p, :piece, :] = second[piece * p : piece * (p + 1)]
        if spare * p < 8:
            parts[p, piece:, :] = extra[spare * p : spare * (p + 1)]
        else:
            parts[p, piece:, :] = jnp.zeros((spare, COLS), F32)

    def share(dims, step, source, target):
        me = slot(dims, here)
        for offset in offsets(dims, sizes):
            there = moved(offset)
            pltpu.make_async_remote_copy(
                src_ref=source(slot(dims, there)), dst_ref=target.at[me],
                send_sem=sum_send.at[step], recv_sem=sum_recv.at[step],
                device_id=device_at(there), device_id_type=MESH,
            ).start()
        return me

    def wait_all(ref, count, sem):
        some = ref.at[pl.ds(0, count)]
        pltpu.make_async_copy(some, some, sem).wait()

    me = share(PLANE, 0, lambda there: parts.at[there], parts_plane)
    parts_plane[me] = parts[me]

    pull_features()

    def finish(i, half, value):
        tracer_grad[i, 8 * half : 8 * half + 8, :] = value

    pull_state(finish)

    wait_all(parts_plane, plane - 1, sum_recv.at[0])
    summed = parts_plane[0]
    for p in range(1, plane):
        summed = summed + parts_plane[p]
    me = slot(PILLAR, here)
    parts_pillar[me] = summed
    share(PILLAR, 1, lambda there: parts_pillar.at[me], parts_pillar)
    wait_all(parts_pillar, pillar - 1, sum_recv.at[1])
    summed = parts_pillar[0]
    for p in range(1, pillar):
        summed = summed + parts_pillar[p]
    cells_all = lat_count * ROWS * lon_count * COLS * NZ
    me = slot(PLANE, here)
    gathered[me] = summed * (1.0 / math.sqrt(cells_all))
    share(PLANE, 2, lambda there: gathered.at[me], gathered)
    wait_all(gathered, plane - 1, sum_recv.at[2])
    for p in range(plane):
        gw_second[piece * p : piece * (p + 1), :] = gathered[p, :piece, :]
        if spare * p < 8:
            extras[spare * p : spare * (p + 1), :] = gathered[p, piece:, :]
    gw_first[...] = extras[0:6, :]
    gw_head[...] = extras[6:7, :]

    finish_phase(0, send0, recv0, fold0)
    finish_phase(1, send1, recv1, fold1)
    finish_phase(2, send2, recv2, fold2)
    wait_all(parts_plane, plane - 1, sum_send.at[0])
    wait_all(parts_pillar, pillar - 1, sum_send.at[1])
    wait_all(gathered, plane - 1, sum_send.at[2])


def hand_over(*refs):
    for source, target in zip(refs[:5], refs[5:]):
        target[...] = source[...]


def per_device(lat_count, lon_count, tracers, land_mask, level_counts, fold_partner, cotangent,
               w_first, b_first, w_second, b_second, w_head, b_head):
    field = (FIELDS, ROWS, COLS)
    ext = pltpu.VMEM((FIELDS, 32, COLS), F32)
    kap = pltpu.VMEM((NZ, 32, COLS), F32)
    feats = pltpu.VMEM((CHUNKS + 3, 64, COLS), F32)
    stack = pltpu.VMEM((CHUNKS, 2 * HID, LANES), BF16)
    dense = pltpu.VMEM((CHUNKS, HID, LANES), F32)
    tile = pltpu.VMEM((CHUNKS, 8, COLS), F32)
    sizes = place_sizes(lat_count, lon_count)
    plane = sizes["x"] * sizes["y_low"] * sizes["y_high"]
    pillar = sizes["core"] * sizes["z"]
    both = sum(piece_rows(plane))
    scratch = [
        pltpu.VMEM((8, HID), F32),
        pltpu.VMEM((HID, 32), BF16),
        pltpu.VMEM((16, 3 * HID), BF16),
        pltpu.VMEM((HID, 3 * HID), BF16),
        pltpu.VMEM((HID, 3 * HID), BF16),
        pltpu.VMEM((HID, COLS), F32),
        pltpu.VMEM((HID, COLS), F32),
        ext,
        pltpu.VMEM((4, NZ, ROWS, COLS), F32),
        ext, ext, ext, ext, kap, kap,
        pltpu.VMEM((4,) + field, F32),
        pltpu.VMEM((4,) + field, F32),
        pltpu.VMEM((4, NZ, ROWS, COLS), F32),
        pltpu.VMEM((4, NZ, ROWS, COLS), F32),
        tile, tile,
        pltpu.VMEM(field, F32),
        feats, feats,
        pltpu.VMEM((CHUNKS + 3, 8, COLS), F32),
        stack, stack, dense, dense, stack, stack,
        pltpu.VMEM((1, 2 * HID, COLS), BF16),
        pltpu.VMEM((1, HID, COLS), F32),
        pltpu.VMEM((CHUNKS, 64, COLS), F32),
        tile,
        pltpu.VMEM((2 * HID, 2 * HID), F32),
        pltpu.VMEM((16, 2 * HID), F32),
        pltpu.VMEM((HID, COLS), F32),
    ]
    scratch += [pltpu.VMEM((4, n, COLS), F32) for n in (24, 8, 8)] * 2
    scratch += [pltpu.VMEM((lon_count, n, COLS), F32) for n in (24, 8, 8)]
    scratch += [
        pltpu.VMEM((plane, both, COLS), F32),
        pltpu.VMEM((plane, both, COLS), F32),
        pltpu.VMEM((pillar, both, COLS), F32),
        pltpu.VMEM((plane, both, COLS), F32),
        pltpu.VMEM((8, COLS), F32),
        pltpu.SemaphoreType.DMA((3, 4)),
        pltpu.SemaphoreType.DMA((3, 4)),
        pltpu.SemaphoreType.DMA((3,)),
        pltpu.SemaphoreType.DMA((3,)),
        pltpu.SemaphoreType.DMA((3,)),
        pltpu.SemaphoreType.DMA((3,)),
        pltpu.SemaphoreType.DMA((2,)),
    ]
    vmem = pl.BlockSpec(memory_space=pltpu.VMEM)
    anywhere = pl.BlockSpec(memory_space=pl.ANY)
    run = pl.pallas_call(
        lambda *refs: kernel(lat_count, lon_count, *refs),
        out_shape=[
            jax.ShapeDtypeStruct(field, F32),
            jax.ShapeDtypeStruct(field, F32),
            jax.ShapeDtypeStruct((6, HID), F32),
            jax.ShapeDtypeStruct((HID, HID), F32),
            jax.ShapeDtypeStruct((1, HID), F32),
        ],
        in_specs=[anywhere] + [vmem] * 3 + [anywhere] + [vmem] * 5
        + [pl.BlockSpec(memory_space=pltpu.SMEM)],
        out_specs=[vmem] * 5,
        scratch_shapes=scratch,
        compiler_params=pltpu.CompilerParams(
            collective_id=0, has_side_effects=True, vmem_limit_bytes=56 * 2**20
        ),
        name="adjoint_steps",
    )
    results = run(
        tracers.reshape(field), land_mask, level_counts, fold_partner.reshape(1, COLS),
        cotangent.reshape(field), w_first, b_first.reshape(1, HID), w_second,
        b_second.reshape(1, HID), w_head.reshape(1, HID), b_head,
    )
    out, grad, first, second, head = pl.pallas_call(
        hand_over,
        out_shape=[jax.ShapeDtypeStruct(r.shape, F32) for r in results],
        in_specs=[vmem] * 5,
        out_specs=[vmem] * 5,
        name="hand_over",
    )(*results)
    return (
        out.reshape(tracers.shape), grad.reshape(tracers.shape), first, second, head.reshape(HID)
    )


def solution(mesh):
    lat_count, lon_count = mesh.shape["lat"], mesh.shape["lon"]
    grid = P(None, None, "lat", "lon")
    return jax.shard_map(
        lambda *args: per_device(lat_count, lon_count, *args),
        mesh=mesh,
        in_specs=(
            grid, P("lat", "lon"), P("lat", "lon"), P("lon"), grid,
            P(), P(), P(), P(), P(), P(),
        ),
        out_specs=(grid, grid, P(), P(), P()),
        check_vma=False,
    )
```

```python
import math

import jax
import jax.numpy as jnp
from jax import lax
from jax.experimental import pallas as pl
from jax.experimental.pallas import tpu as pltpu
from jax.sharding import PartitionSpec as P

KMAX = 0.24
F32 = jnp.float32
BF16 = jnp.bfloat16
MESH = pl.DeviceIdType.MESH

NZ = 4
ROWS = 16
COLS = 128
HID = 128
FIELDS = 2 * NZ
CHUNKS = NZ * ROWS // 8
LANES = 8 * COLS
EAST, WEST, NORTH, SOUTH = 0, 1, 2, 3
HALF = NZ * ROWS
OPPOSITE = (WEST, EAST, SOUTH, NORTH)


PLANE = ("x", "y_high", "y_low")
PILLAR = ("core", "z")
RIM = ("z", "y_low")


def place_sizes(lat_count, lon_count):
    if lat_count == 16 and lon_count == 16:
        return {"core": 2, "x": 4, "y_high": 2, "y_low": 2, "z": 8}
    return {"core": 1, "x": lat_count, "y_high": 1, "y_low": 1, "z": lon_count}


def offsets(dims, sizes):
    steps = [{}]
    for d in dims:
        steps = [{**s, d: o} for s in steps for o in range(sizes[d])]

    def hops(s):
        y = {(0, 0): 0, (1, 0): 2, (0, 1): 1, (1, 1): 1}[s.get("y_high", 0), s.get("y_low", 0)]
        x, z = s.get("x", 0), s.get("z", 0)
        return y + min(x, sizes["x"] - x) + min(z, sizes["z"] - z)

    return sorted([s for s in steps if any(s.values())], key=hops, reverse=True)


def piece_rows(parts):
    return HID // parts, -(-8 // parts)


def halves(x):
    high = x.astype(BF16)
    return high, (x - high.astype(F32)).astype(BF16)


def dot(a, b):
    return jnp.dot(a, b, preferred_element_type=F32)


def dot_nt(a, b):
    return lax.dot_general(a, b, (((1,), (1,)), ((), ())), preferred_element_type=F32)


def lane_roll(x, by):
    flat = x.reshape(-1, COLS)
    return pltpu.roll(flat, by % COLS, 1).reshape(x.shape)


def column(row):
    return jnp.broadcast_to(row, (COLS, COLS)).T


def kernel(
    lat_count, lon_count,
    tracers, land, levels, partner, cotangent, w_first, b_first, w_second, b_second, w_head, b_head,
    tracers_out, tracer_grad, gw_first, gw_second, gw_head,
    w1_rows, w1_fwd, w1_bwd, w2_fwd, w2_bwd, bias2, head,
    wet_ext, pair, state0, state1, adj0, adj1, kap0, kap1, contrast0, contrast1, coef0, coef1,
    slope0, slope1, direct, feats0, feats1, logits, h1_0, h1_1, h2_0, h2_1, dz2, dz1,
    h1_edge, h2_edge, dfeat,
    obar, acc2, acc1, acch,
    beside_out, beside_in, across_out, across_in, wet_beside_out, wet_beside_in, first_out, first_in,
    fold_first, folded,
    parts, parts_plane, parts_pillar, gathered, extras,
    send_sem, recv_sem, fold_send, fold_recv, sum_send, sum_recv, in_sem,
    land_here, levels_here, partner_here, w1_here, b1_here, w2_here, b2_here, wh_here,
):
    lat = lax.axis_index("lat")
    lon = lax.axis_index("lon")
    at_top = lat == lat_count - 1
    at_bottom = lat == 0
    east = lax.rem(lon + 1, lon_count)
    west = lax.rem(lon + lon_count - 1, lon_count)

    sizes = place_sizes(lat_count, lon_count)
    core_count, x_count, y_low_count = sizes["core"], sizes["x"], sizes["y_low"]
    here = {
        "core": lax.rem(lat, core_count),
        "x": lax.rem(lax.div(lat, core_count), x_count),
        "y_high": lax.div(lat, core_count * x_count),
        "y_low": lax.rem(lon, y_low_count),
        "z": lax.div(lon, y_low_count),
    }

    def device_at(at):
        return {
            "lat": (at["y_high"] * x_count + at["x"]) * core_count + at["core"],
            "lon": at["z"] * y_low_count + at["y_low"],
        }

    def moved(offset):
        return {d: lax.rem(here[d] + offset.get(d, 0), sizes[d]) for d in here}

    def slot(dims, at):
        index = 0
        for d in dims:
            index = index * sizes[d] + at[d]
        return index

    def load(i, source, target):
        copy = pltpu.make_async_copy(source, target, in_sem.at[i])
        copy.start()
        return copy

    loads = [
        load(0, land, land_here),
        load(1, levels, levels_here),
        load(2, tracers, state0.at[:, pl.ds(8, ROWS), :]),
        load(3, cotangent, adj0.at[:, pl.ds(8, ROWS), :]),
        load(4, partner, partner_here),
        load(5, w_first, w1_here),
        load(6, b_first, b1_here),
        load(7, w_second, w2_here),
        load(8, b_second, b2_here),
        load(9, w_head, wh_here),
    ]
    barrier = pltpu.get_barrier_semaphore()

    def greet(device):
        pl.semaphore_signal(barrier, inc=1, device_id=device, device_id_type=MESH)

    @pl.when(at_top)
    def _():
        for offset in offsets(RIM, sizes):
            greet(device_at(moved(offset)))

    greeted = 4
    for dims in (PILLAR, PLANE):
        for offset in offsets(dims, sizes):
            greet(device_at(moved(offset)))
            greeted += 1
    greet({"lat": lat, "lon": east})
    greet({"lat": lat, "lon": west})
    greet({"lat": lax.rem(lat + 1, lat_count), "lon": lon})
    greet({"lat": lax.rem(lat + lat_count - 1, lat_count), "lon": lon})

    lane3 = lax.broadcasted_iota(jnp.int32, (FIELDS, ROWS, COLS), 2)
    lane8 = lax.broadcasted_iota(jnp.int32, (8, COLS), 1)
    sub8 = lax.broadcasted_iota(jnp.int32, (8, COLS), 0)

    send0 = {EAST: wet_beside_out.at[0], WEST: wet_beside_out.at[1],
             NORTH: first_out.at[0], SOUTH: first_out.at[1]}
    recv0 = {EAST: wet_beside_in.at[0], WEST: wet_beside_in.at[1],
             NORTH: first_in.at[0], SOUTH: first_in.at[1]}
    send1, send2, send3 = (
        {EAST: beside_out.at[i, 0], WEST: beside_out.at[i, 1],
         NORTH: across_out.at[i, 0], SOUTH: across_out.at[i, 1]}
        for i in range(3)
    )
    recv1, recv2, recv3 = (
        {EAST: beside_in.at[i, 0], WEST: beside_in.at[i, 1],
         NORTH: across_in.at[i, 0], SOUTH: across_in.at[i, 1]}
        for i in range(3)
    )
    fold0, fold1, fold2, fold3 = fold_first, folded.at[0], folded.at[1], folded.at[2]

    def to_side(phase, side, sends, recvs):
        target = {
            EAST: {"lat": lat, "lon": east},
            WEST: {"lat": lat, "lon": west},
            NORTH: {"lat": jnp.minimum(lat + 1, lat_count - 1), "lon": lon},
            SOUTH: {"lat": jnp.maximum(lat - 1, 0), "lon": lon},
        }[side]
        back = OPPOSITE[side]
        return pltpu.make_async_remote_copy(
            src_ref=sends[side], dst_ref=recvs[back],
            send_sem=send_sem.at[phase, side], recv_sem=recv_sem.at[phase, back],
            device_id=target, device_id_type=MESH,
        )

    def start_phase(phase, sends, recvs, folds):
        @pl.when(at_top)
        def _():
            for offset in offsets(RIM, sizes):
                pltpu.make_async_remote_copy(
                    src_ref=sends[NORTH], dst_ref=folds.at[lon],
                    send_sem=fold_send.at[phase], recv_sem=fold_recv.at[phase],
                    device_id=device_at(moved(offset)), device_id_type=MESH,
                ).start()

        to_side(phase, EAST, sends, recvs).start()
        to_side(phase, WEST, sends, recvs).start()

        @pl.when(jnp.logical_not(at_top))
        def _():
            to_side(phase, NORTH, sends, recvs).start()

        @pl.when(jnp.logical_not(at_bottom))
        def _():
            to_side(phase, SOUTH, sends, recvs).start()

        @pl.when(at_top)
        def _():
            folds[lon] = sends[NORTH][...]

    def wait_phase(phase, sends, recvs, folds):
        to_side(phase, WEST, sends, recvs).wait_recv()
        to_side(phase, EAST, sends, recvs).wait_recv()

        @pl.when(jnp.logical_not(at_top))
        def _():
            to_side(phase, SOUTH, sends, recvs).wait_recv()

        @pl.when(jnp.logical_not(at_bottom))
        def _():
            to_side(phase, NORTH, sends, recvs).wait_recv()

        @pl.when(at_top)
        def _():
            others = folds.at[pl.ds(0, lon_count - 1)]
            pltpu.make_async_copy(others, others, fold_recv.at[phase]).wait()
            block = jnp.broadcast_to(partner_here[...] >> 7, (8, COLS))
            lane = jnp.broadcast_to(partner_here[...] & (COLS - 1), (8, COLS))
            picked = jnp.zeros((8, COLS), F32)
            for j in range(lon_count):
                taken = jnp.take_along_axis(folds[j, 0:8, :], lane, axis=1)
                picked = jnp.where(block == j, taken, picked)
            recvs[NORTH][0:8, :] = picked
            if phase == 0:
                picked = jnp.zeros((8, COLS), F32)
                for j in range(lon_count):
                    counts = jnp.broadcast_to(folds[j, 8:9, :], (8, COLS))
                    taken = jnp.take_along_axis(counts, lane, axis=1)
                    picked = jnp.where(block == j, taken, picked)
                recvs[NORTH][8:9, :] = picked[0:1]

    def finish_phase(phase, sends, recvs, folds):
        to_side(phase, EAST, sends, recvs).wait_send()
        to_side(phase, WEST, sends, recvs).wait_send()

        @pl.when(jnp.logical_not(at_top))
        def _():
            to_side(phase, NORTH, sends, recvs).wait_send()

        @pl.when(jnp.logical_not(at_bottom))
        def _():
            to_side(phase, SOUTH, sends, recvs).wait_send()

        @pl.when(at_top)
        def _():
            others = folds.at[pl.ds(0, lon_count - 1)]
            pltpu.make_async_copy(others, others, fold_send.at[phase]).wait()

    def pack_beside(ext, sends, at):
        turned = ext[:, 8:24, :].reshape(COLS, COLS).T
        sends[EAST][at : at + 8, :] = turned[COLS - 8 :]
        sends[WEST][at : at + 8, :] = turned[:8]

    def pack(ext, sends):
        pack_beside(ext, sends, 0)
        sends[NORTH][0:8, :] = ext[:, 23, :]
        sends[SOUTH][0:8, :] = ext[:, 8, :]

    def unpack(ext, recvs):
        ext[:, 24, :] = recvs[NORTH][0:8, :]
        ext[:, 7, :] = recvs[SOUTH][0:8, :]

    def edge_columns(recvs, at):
        first = pltpu.roll(recvs[WEST][at : at + 8, :], 1, 0)
        last = pltpu.roll(recvs[EAST][at : at + 8, :], 7, 0)
        middle = jnp.zeros((COLS - 16, COLS), F32)
        return jnp.concatenate([first, middle, last], axis=0).T.reshape(FIELDS, ROWS, COLS)

    def sides(ext, edges):
        core = ext[:, 8:24, :]
        lane = lane3[: core.shape[0]]
        return [
            jnp.where(lane == COLS - 1, edges, lane_roll(core, -1)),
            jnp.where(lane == 0, edges, lane_roll(core, 1)),
            ext[:, 9:25, :],
            ext[:, 7:23, :],
        ]

    def store_feature(feats, chunk, f, value):
        feats[chunk, pl.ds(f, 8, stride=8), :] = value

    def own_features(ext, feats):
        for half in range(2):
            rows = pl.ds(8 + 8 * half, 8)
            wets = [wet_ext[k, rows, :] for k in range(NZ)]
            for t in range(2):
                cells = [ext[NZ * t + k, rows, :] for k in range(NZ)]
                vertical = [
                    (cells[k + 1] - cells[k]) * (wets[k + 1] * wets[k]) for k in range(NZ - 1)
                ]
                zero = jnp.zeros((8, COLS), F32)
                for k in range(NZ):
                    chunk = 2 * k + half
                    store_feature(feats, chunk, t, cells[k])
                    store_feature(feats, chunk, 2 + t, -vertical[k - 1] if k > 0 else zero)
                    store_feature(feats, chunk, 4 + t, vertical[k] if k < NZ - 1 else zero)

    def halo_features(recvs, feats):
        north, south = recvs[NORTH][0:8, :], recvs[SOUTH][0:8, :]
        first = sub8 < NZ
        depths = [jnp.broadcast_to(recv0[side][8:9, :], (8, COLS)) for side in (NORTH, SOUTH)]
        level = lax.rem(sub8, NZ).astype(F32)
        wet = (level < jnp.where(first, *depths)).astype(F32)
        joint = jnp.where(
            lax.rem(sub8, NZ) == NZ - 1, 0.0, wet * pltpu.roll(wet, 7, 0)
        )
        fields = (
            jnp.where(first, north, pltpu.roll(south, 4, 0)),
            jnp.where(first, pltpu.roll(north, 4, 0), south),
        )
        for t, cells in enumerate(fields):
            vertical = (pltpu.roll(cells, 7, 0) - cells) * joint
            store_feature(feats, CHUNKS, t, cells)
            store_feature(feats, CHUNKS, 2 + t, -pltpu.roll(vertical, 1, 0))
            store_feature(feats, CHUNKS, 4 + t, vertical)
        column_features(
            recvs[EAST][0:1, :], recvs[WEST][7:8, :], edge_wet(), feats, CHUNKS + 1
        )
        return wet

    def paired(east_row, west_row):
        east_row = jnp.broadcast_to(east_row, (8, COLS))
        west_row = jnp.broadcast_to(west_row, (8, COLS))
        first = lane8 < HALF
        return (
            jnp.where(first, east_row, pltpu.roll(west_row, HALF, 1)),
            jnp.where(first, pltpu.roll(east_row, HALF, 1), west_row),
        )

    def joint_column(wet_col):
        below = pltpu.roll(wet_col, COLS - ROWS, 1)
        return jnp.where(lax.rem(lane8, HALF) >= HALF - ROWS, 0.0, wet_col * below)

    def column_features(east_row, west_row, wet_col, feats, chunk):
        joint = joint_column(wet_col)
        for t, cells in enumerate(paired(east_row, west_row)):
            vertical = (pltpu.roll(cells, COLS - ROWS, 1) - cells) * joint
            feats[chunk, t : t + 1, :] = cells[0:1]
            feats[chunk, 2 + t : 3 + t, :] = -pltpu.roll(vertical, ROWS, 1)[0:1]
            feats[chunk, 4 + t : 5 + t, :] = vertical[0:1]

    def edge_wet():
        return paired(recv0[EAST][8:9, :], recv0[WEST][15:16, :])[0]

    def own_edge_wet():
        return paired(send0[EAST][15:16, :], send0[WEST][8:9, :])[0]

    def wide(x, n):
        return jnp.concatenate([x] * n, axis=1) if n > 1 else x

    def closure_chunk(feats, chunk, rows, h1_ref, h2_ref, at=None):
        at = chunk if at is None else at
        n = rows
        f = [feats[chunk, 8 * q : 8 * q + 8, :] for q in range(n)]
        f = jnp.concatenate(f, axis=1) if n > 1 else f[0]
        high = f.astype(BF16).astype(F32)
        low = f - high
        stacked = jnp.concatenate([high, low, high, low], axis=0).astype(BF16)
        h1 = jnp.tanh(dot(w1_fwd[...], stacked))
        h1_high, h1_low = halves(h1)
        pre2 = dot(w2_fwd[...], jnp.concatenate([h1_high, h1_low, h1_high], axis=0))
        h2 = jnp.tanh(pre2 + wide(bias2[...], n))
        o = jnp.sum(h2 * wide(head[...], n), axis=0, keepdims=True)
        for q in range(n):
            logits[chunk, q : q + 1, :] = o[:, COLS * q : COLS * (q + 1)]
        if h1_ref is not None:
            h1_ref[at, :HID, :] = h1_high
            h1_ref[at, HID:, :] = h1_low
            h2_ref[at] = h2

    def closure_own(feats, h1_ref, h2_ref):
        @pl.loop(0, CHUNKS, unroll=CHUNKS)
        def _(chunk):
            closure_chunk(feats, chunk, 8, h1_ref, h2_ref)

    def kappa_from(o, wet):
        gate = jax.nn.sigmoid(o + b_head[0])
        return KMAX * gate * wet, KMAX * gate * (1.0 - gate) * wet

    def advance(phase, state, feats, sends, recvs, folds, h1_ref, h2_ref, kap, slope, contrast, coef):
        own_features(state, feats)
        closure_own(feats, h1_ref, h2_ref)
        if phase == 1:
            column_features(
                sends[EAST][7:8, :], sends[WEST][0:1, :], own_edge_wet(), feats, CHUNKS + 2
            )
            closure_chunk(feats, CHUNKS + 2, 1, h1_edge, h2_edge, 0)
        wait_phase(phase, sends, recvs, folds)
        unpack(state, recvs)
        if phase == 0:
            for k in range(NZ):
                wet_ext[k, 24:25, :] = (recvs[NORTH][8:9, :] > k).astype(F32)
                wet_ext[k, 7:8, :] = (recvs[SOUTH][8:9, :] > k).astype(F32)
            wet = wet_ext[:NZ, 8:24, :]
            around = sides(wet_ext.at[pl.ds(0, NZ)], edge_columns(recvs, 8)[:NZ])
            for n in range(4):
                pair[n] = 0.5 * wet * around[n]
        wet_halo = halo_features(recvs, feats)
        closure_chunk(feats, CHUNKS, 8, None, None)
        closure_chunk(feats, CHUNKS + 1, 1, None, None)
        for k in range(NZ):
            for half in range(2):
                rows = pl.ds(8 + 8 * half, 8)
                value, rise = kappa_from(logits[2 * k + half], wet_ext[k, rows, :])
                kap[k, rows, :] = value
                slope[2 * k + half] = rise
        value, _ = kappa_from(logits[CHUNKS], wet_halo)
        for k in range(NZ):
            kap[k, 24:25, :] = value[k : k + 1]
            kap[k, 7:8, :] = value[NZ + k : NZ + k + 1]
        value, _ = kappa_from(logits[CHUNKS + 1], edge_wet())
        same = jnp.broadcast_to(value[0:1], (8, COLS))
        middle = jnp.zeros((COLS - 16, COLS), F32)
        kap_edges = jnp.concatenate([pltpu.roll(same, NZ * ROWS, 1), middle, same], axis=0).T
        kap_sides = sides(kap, kap_edges[: NZ * ROWS].reshape(NZ, ROWS, COLS))
        tracer_sides = sides(state, edge_columns(recvs, 0))
        core = state[:, 8:24, :]
        own_kap = kap[:, 8:24, :]
        change = jnp.zeros_like(core)
        for n in range(4):
            difference = tracer_sides[n] - core
            weight = (own_kap + kap_sides[n]) * pair[n]
            contrast[n] = difference
            coef[n] = weight
            change = change + jnp.concatenate([weight, weight], 0) * difference
        return core + change

    def pull_flux(adjoint, recvs, contrast, coef, slope):
        core = adjoint[:, 8:24, :]
        around = sides(adjoint, edge_columns(recvs, 0))
        total_direct = core
        kappa_bar = jnp.zeros((NZ, ROWS, COLS), F32)
        for n in range(4):
            difference = around[n] - core
            weight = coef[n]
            total_direct = total_direct + jnp.concatenate([weight, weight], 0) * difference
            product = contrast[n] * difference
            kappa_bar = kappa_bar - pair[n] * (product[:NZ] + product[NZ:])
        direct[...] = total_direct
        obar[...] = kappa_bar.reshape(CHUNKS, 8, COLS) * slope[...]

    def pull_cells(bar, h1_high, h1_low, h2):
        n = bar.shape[1] // COLS
        weighted = h2 * bar
        d2_high, d2_low = halves(wide(head[...], n) * (bar - weighted * h2))
        dh1 = dot(w2_bwd[...], jnp.concatenate([d2_high, d2_low, d2_high], axis=0))
        h1 = h1_high.astype(F32) + h1_low.astype(F32)
        d1_high, d1_low = halves(dh1 * (1.0 - h1 * h1))
        return weighted, d2_high, d2_low, d1_high, d1_low

    def pull_closure(h1_ref, h2_ref):
        @pl.loop(0, CHUNKS, unroll=CHUNKS)
        def _(chunk):
            bar = jnp.concatenate([obar[chunk, q : q + 1, :] for q in range(8)], axis=1)
            weighted, d2_high, d2_low, d1_high, d1_low = pull_cells(
                bar, h1_ref[chunk, :HID, :], h1_ref[chunk, HID:, :], h2_ref[chunk]
            )
            dz2[chunk, :HID, :] = d2_high
            dz2[chunk, HID:, :] = d2_low
            dz1[chunk, :HID, :] = d1_high
            dz1[chunk, HID:, :] = d1_low
            heads = weighted[:, :COLS]
            for q in range(1, 8):
                heads = heads + weighted[:, COLS * q : COLS * (q + 1)]
            acch[...] += heads

    def send_edges(h1_ref, h2_ref, sends):
        tops = [(2 * k + 1, 7) for k in range(NZ)]
        lows = [(2 * k, 0) for k in range(NZ)]
        places = tops + lows
        turned = jnp.concatenate(
            [obar[...].reshape(HALF, COLS), jnp.zeros((HALF, COLS), F32)], axis=0
        ).T
        column_bar = paired(turned[COLS - 1 :], turned[0:1])[0][0:1]
        bar = jnp.concatenate([obar[c, q : q + 1, :] for c, q in places] + [column_bar], axis=1)
        cut = [slice(COLS * q, COLS * (q + 1)) for _, q in places]
        high = [h1_ref[c, :HID, l] for (c, _), l in zip(places, cut)] + [h1_edge[0, :HID, :]]
        low = [h1_ref[c, HID:, l] for (c, _), l in zip(places, cut)] + [h1_edge[0, HID:, :]]
        h2 = [h2_ref[c, :, l] for (c, _), l in zip(places, cut)] + [h2_edge[0]]
        high, low, h2 = (jnp.concatenate(x, axis=1) for x in (high, low, h2))
        _, _, _, d1_high, d1_low = pull_cells(bar, high, low, h2)
        d = dot(w1_bwd[...], jnp.concatenate([d1_high, d1_low, d1_high], axis=0))
        d = [d[:8, COLS * i : COLS * (i + 1)] for i in range(len(places) + 1)]
        for side, y in ((NORTH, ROWS - 1), (SOUTH, 0)):
            rows = d[:NZ] if side == NORTH else d[NZ : 2 * NZ]
            wets = [wet_ext[k, 8 + y : 9 + y, :] for k in range(NZ)]
            vertical = [
                (pltpu.roll(rows[k], 4, 0) - pltpu.roll(rows[k + 1], 6, 0))
                * (wets[k + 1] * wets[k])
                for k in range(NZ - 1)
            ]
            for k in range(NZ):
                value = rows[k]
                if k < NZ - 1:
                    value = value - vertical[k]
                if k > 0:
                    value = value + vertical[k - 1]
                for t in range(2):
                    i = NZ * t + k
                    sends[side][i : i + 1, :] = value[t : t + 1] + direct[i, y : y + 1, :]
        cells = d[2 * NZ]
        vertical = pltpu.roll(cells, 4, 0) - pltpu.roll(pltpu.roll(cells, 6, 0), COLS - ROWS, 1)
        vertical = vertical * joint_column(own_edge_wet())
        value = cells - vertical + pltpu.roll(vertical, ROWS, 1)
        other = pltpu.roll(value, HALF, 1)
        first = lane8[0:1] < HALF
        turned = direct[...].reshape(COLS, COLS).T
        from_east = turned[COLS - 1 :] + jnp.where(first, value[0:1], other[1:2])
        from_west = turned[0:1] + jnp.where(first, other[0:1], value[1:2])
        sends[EAST][...] = jnp.broadcast_to(from_east, (8, COLS))
        sends[WEST][...] = jnp.broadcast_to(from_west, (8, COLS))

    def pull_features():
        @pl.loop(0, CHUNKS, unroll=CHUNKS)
        def _(chunk):
            d1 = dz1[chunk]
            d = dot(w1_bwd[...], jnp.concatenate([d1, d1[:HID]], axis=0))
            for q in range(8):
                dfeat[chunk, 8 * q : 8 * q + 8, :] = d[:8, COLS * q : COLS * (q + 1)]

    def add_weights(feats, h1_ref):
        @pl.loop(0, CHUNKS, unroll=CHUNKS)
        def _(chunk):
            acc2[...] += dot_nt(h1_ref[chunk], dz2[chunk])
            f = jnp.concatenate([feats[chunk, 8 * q : 8 * q + 8, :] for q in range(8)], axis=1)
            high = f.astype(BF16).astype(F32)
            stacked = jnp.concatenate([high, f - high], axis=0).astype(BF16)
            acc1[...] += dot_nt(stacked, dz1[chunk])

    def pull_state(store):
        for half in range(2):
            rows = pl.ds(8 * half, 8)
            wets = [wet_ext[k, pl.ds(8 + 8 * half, 8), :] for k in range(NZ)]
            for t in range(2):
                bar = [
                    [dfeat[2 * k + half, pl.ds(f, 8, stride=8), :] for k in range(NZ)]
                    for f in (t, 2 + t, 4 + t)
                ]
                vertical = [
                    (bar[2][k] - bar[1][k + 1]) * (wets[k + 1] * wets[k]) for k in range(NZ - 1)
                ]
                for k in range(NZ):
                    value = direct[NZ * t + k, rows, :] + bar[0][k]
                    if k < NZ - 1:
                        value = value - vertical[k]
                    if k > 0:
                        value = value + vertical[k - 1]
                    store(NZ * t + k, half, value)

    loads[0].wait()
    loads[1].wait()
    depth_here = land_here[...] * levels_here[...]
    for k in range(NZ):
        wet = (k < depth_here).astype(F32)
        wet_ext[k, 8:24, :] = wet
        wet_ext[NZ + k, 8:24, :] = wet
    pack_beside(wet_ext, send0, 8)
    depths = depth_here.astype(F32)
    send0[NORTH][8:9, :] = depths[ROWS - 1 :]
    send0[SOUTH][8:9, :] = depths[0:1]
    loads[2].wait()
    pack(state0, send0)

    @pl.when(at_bottom)
    def _():
        for recvs in (recv0, recv1, recv2, recv3):
            recvs[SOUTH][...] = jnp.zeros(recvs[SOUTH].shape, F32)

    for copy in loads[3:]:
        copy.wait()

    @pl.when(jnp.logical_not(at_top))
    def _():
        pl.semaphore_wait(barrier, greeted)

    @pl.when(at_top)
    def _():
        pl.semaphore_wait(barrier, greeted + lon_count - 1)

    start_phase(0, send0, recv0, fold0)
    pack(adj0, send3)
    start_phase(3, send3, recv3, fold3)

    w1_rows[0:6, :] = w1_here[...]
    w1_rows[6:7, :] = b1_here[...]
    w1_rows[7:8, :] = jnp.zeros((1, HID), F32)
    w1 = w1_rows[...]
    w1_high = w1.astype(BF16).astype(F32)
    w1_low = w1 - w1_high
    tall = jnp.concatenate(
        [w1_high, w1_high, w1_low, w1_low, jnp.zeros((HID - 32, HID), F32)], axis=0
    )
    w1_fwd[...] = tall.T[:, :32].astype(BF16)
    blank = jnp.zeros((8, HID), F32)
    w1_high = jnp.concatenate([w1_high, blank], axis=0).astype(BF16)
    w1_low = jnp.concatenate([w1_low, blank], axis=0).astype(BF16)
    w1_bwd[...] = jnp.concatenate([w1_high, w1_high, w1_low], axis=1)
    w2 = w2_here[...]
    high, low = halves(w2)
    w2_bwd[...] = jnp.concatenate([high, high, low], axis=1)
    high, low = halves(w2.T)
    w2_fwd[...] = jnp.concatenate([high, high, low], axis=1)
    bias2[...] = column(b2_here[...])
    head[...] = column(wh_here[...])
    ones_row = jnp.where(sub8 == 6, 1.0, 0.0)
    for feats in (feats0, feats1):
        for chunk in range(CHUNKS + 1):
            feats[chunk, pl.ds(6, 8, stride=8), :] = jnp.ones((8, COLS), F32)
            feats[chunk, pl.ds(7, 8, stride=8), :] = jnp.zeros((8, COLS), F32)
        feats[CHUNKS + 1, 0:8, :] = ones_row
        feats[CHUNKS + 2, 0:8, :] = ones_row
    logits[CHUNKS + 1] = jnp.zeros((8, COLS), F32)
    acc2[...] = jnp.zeros_like(acc2)
    acc1[...] = jnp.zeros_like(acc1)
    acch[...] = jnp.zeros_like(acch)

    state1[:, 8:24, :] = advance(
        0, state0, feats0, send0, recv0, fold0, h1_0, h2_0, kap0, slope0, contrast0, coef0
    )
    pack(state1, send1)
    start_phase(1, send1, recv1, fold1)
    tracers_out[...] = advance(
        1, state1, feats1, send1, recv1, fold1, h1_1, h2_1, kap1, slope1, contrast1, coef1
    )

    wait_phase(3, send3, recv3, fold3)
    unpack(adj0, recv3)
    pull_flux(adj0, recv3, contrast1, coef1, slope1)
    send_edges(h1_1, h2_1, send2)
    start_phase(2, send2, recv2, fold2)
    pull_closure(h1_1, h2_1)
    pull_features()

    def keep(i, half, value):
        adj1[i, 8 + 8 * half : 16 + 8 * half, :] = value

    pull_state(keep)
    add_weights(feats1, h1_1)
    wait_phase(2, send2, recv2, fold2)
    unpack(adj1, recv2)
    pull_flux(adj1, recv2, contrast0, coef0, slope0)
    pull_closure(h1_0, h2_0)
    add_weights(feats0, h1_0)

    plane = x_count * sizes["y_high"] * y_low_count
    pillar = core_count * sizes["z"]
    piece, spare = piece_rows(plane)
    second = (
        (acc2[HID:, HID:] + acc2[HID:, :HID]) + acc2[:HID, HID:]
    ) + acc2[:HID, :HID]
    first = (acc1[8:, :HID] + acc1[:8, HID:]) + acc1[:8, :HID]
    head_row = jnp.sum(acch[...].T, axis=0, keepdims=True)
    extra = jnp.where(sub8 == 6, jnp.broadcast_to(head_row, (8, COLS)), first)
    for p in range(plane):
        parts[p, :piece, :] = second[piece * p : piece * (p + 1)]
        if spare * p < 8:
            parts[p, piece:, :] = extra[spare * p : spare * (p + 1)]
        else:
            parts[p, piece:, :] = jnp.zeros((spare, COLS), F32)

    def share(dims, step, source, target):
        me = slot(dims, here)
        for offset in offsets(dims, sizes):
            there = moved(offset)
            pltpu.make_async_remote_copy(
                src_ref=source(slot(dims, there)), dst_ref=target.at[me],
                send_sem=sum_send.at[step], recv_sem=sum_recv.at[step],
                device_id=device_at(there), device_id_type=MESH,
            ).start()
        return me

    def wait_all(ref, count, sem):
        some = ref.at[pl.ds(0, count)]
        pltpu.make_async_copy(some, some, sem).wait()

    me = share(PLANE, 0, lambda there: parts.at[there], parts_plane)
    parts_plane[me] = parts[me]

    pull_features()

    def finish(i, half, value):
        tracer_grad[i, 8 * half : 8 * half + 8, :] = value

    pull_state(finish)

    wait_all(parts_plane, plane - 1, sum_recv.at[0])
    summed = parts_plane[0]
    for p in range(1, plane):
        summed = summed + parts_plane[p]
    me = slot(PILLAR, here)
    parts_pillar[me] = summed
    share(PILLAR, 1, lambda there: parts_pillar.at[me], parts_pillar)
    wait_all(parts_pillar, pillar - 1, sum_recv.at[1])
    summed = parts_pillar[0]
    for p in range(1, pillar):
        summed = summed + parts_pillar[p]
    cells_all = lat_count * ROWS * lon_count * COLS * NZ
    me = slot(PLANE, here)
    gathered[me] = summed * (1.0 / math.sqrt(cells_all))
    share(PLANE, 2, lambda there: gathered.at[me], gathered)
    wait_all(gathered, plane - 1, sum_recv.at[2])
    for p in range(plane):
        gw_second[piece * p : piece * (p + 1), :] = gathered[p, :piece, :]
        if spare * p < 8:
            extras[spare * p : spare * (p + 1), :] = gathered[p, piece:, :]
    gw_first[...] = extras[0:6, :]
    gw_head[...] = extras[6:7, :]

    finish_phase(0, send0, recv0, fold0)
    finish_phase(1, send1, recv1, fold1)
    finish_phase(2, send2, recv2, fold2)
    finish_phase(3, send3, recv3, fold3)
    wait_all(parts_plane, plane - 1, sum_send.at[0])
    wait_all(parts_pillar, pillar - 1, sum_send.at[1])
    wait_all(gathered, plane - 1, sum_send.at[2])


def hand_over(*refs):
    for source, target in zip(refs[:5], refs[5:]):
        target[...] = source[...]


def per_device(lat_count, lon_count, tracers, land_mask, level_counts, fold_partner, cotangent,
               w_first, b_first, w_second, b_second, w_head, b_head):
    field = (FIELDS, ROWS, COLS)
    ext = pltpu.VMEM((FIELDS, 32, COLS), F32)
    kap = pltpu.VMEM((NZ, 32, COLS), F32)
    feats = pltpu.VMEM((CHUNKS + 3, 64, COLS), F32)
    stack = pltpu.VMEM((CHUNKS, 2 * HID, LANES), BF16)
    dense = pltpu.VMEM((CHUNKS, HID, LANES), F32)
    tile = pltpu.VMEM((CHUNKS, 8, COLS), F32)
    sizes = place_sizes(lat_count, lon_count)
    plane = sizes["x"] * sizes["y_low"] * sizes["y_high"]
    pillar = sizes["core"] * sizes["z"]
    both = sum(piece_rows(plane))
    scratch = [
        pltpu.VMEM((8, HID), F32),
        pltpu.VMEM((HID, 32), BF16),
        pltpu.VMEM((16, 3 * HID), BF16),
        pltpu.VMEM((HID, 3 * HID), BF16),
        pltpu.VMEM((HID, 3 * HID), BF16),
        pltpu.VMEM((HID, COLS), F32),
        pltpu.VMEM((HID, COLS), F32),
        ext,
        pltpu.VMEM((4, NZ, ROWS, COLS), F32),
        ext, ext, ext, ext, kap, kap,
        pltpu.VMEM((4,) + field, F32),
        pltpu.VMEM((4,) + field, F32),
        pltpu.VMEM((4, NZ, ROWS, COLS), F32),
        pltpu.VMEM((4, NZ, ROWS, COLS), F32),
        tile, tile,
        pltpu.VMEM(field, F32),
        feats, feats,
        pltpu.VMEM((CHUNKS + 3, 8, COLS), F32),
        stack, stack, dense, dense, stack, stack,
        pltpu.VMEM((1, 2 * HID, COLS), BF16),
        pltpu.VMEM((1, HID, COLS), F32),
        pltpu.VMEM((CHUNKS, 64, COLS), F32),
        tile,
        pltpu.VMEM((2 * HID, 2 * HID), F32),
        pltpu.VMEM((16, 2 * HID), F32),
        pltpu.VMEM((HID, COLS), F32),
    ]
    scratch += [pltpu.VMEM((3, 2, 8, COLS), F32)] * 4
    scratch += [pltpu.VMEM((2, 16, COLS), F32)] * 2 + [pltpu.VMEM((2, 9, COLS), F32)] * 2
    scratch += [pltpu.VMEM((lon_count, 9, COLS), F32), pltpu.VMEM((3, lon_count, 8, COLS), F32)]
    scratch += [
        pltpu.VMEM((plane, both, COLS), F32),
        pltpu.VMEM((plane, both, COLS), F32),
        pltpu.VMEM((pillar, both, COLS), F32),
        pltpu.VMEM((plane, both, COLS), F32),
        pltpu.VMEM((8, COLS), F32),
        pltpu.SemaphoreType.DMA((4, 4)),
        pltpu.SemaphoreType.DMA((4, 4)),
        pltpu.SemaphoreType.DMA((4,)),
        pltpu.SemaphoreType.DMA((4,)),
        pltpu.SemaphoreType.DMA((3,)),
        pltpu.SemaphoreType.DMA((3,)),
        pltpu.SemaphoreType.DMA((10,)),
        pltpu.VMEM((ROWS, COLS), jnp.int32),
        pltpu.VMEM((ROWS, COLS), jnp.int32),
        pltpu.VMEM((1, COLS), jnp.int32),
        pltpu.VMEM((6, HID), F32),
        pltpu.VMEM((1, HID), F32),
        pltpu.VMEM((HID, HID), F32),
        pltpu.VMEM((1, HID), F32),
        pltpu.VMEM((1, HID), F32),
    ]
    vmem = pl.BlockSpec(memory_space=pltpu.VMEM)
    anywhere = pl.BlockSpec(memory_space=pl.ANY)
    run = pl.pallas_call(
        lambda *refs: kernel(lat_count, lon_count, *refs),
        out_shape=[
            pltpu.VMEM(field, F32),
            pltpu.VMEM(field, F32),
            pltpu.VMEM((6, HID), F32),
            pltpu.VMEM((HID, HID), F32),
            pltpu.VMEM((1, HID), F32),
        ],
        in_specs=[anywhere] * 10 + [pl.BlockSpec(memory_space=pltpu.SMEM)],
        out_specs=[vmem] * 5,
        scratch_shapes=scratch,
        compiler_params=pltpu.CompilerParams(
            collective_id=0, has_side_effects=True, vmem_limit_bytes=56 * 2**20
        ),
        name="adjoint_steps",
    )
    results = run(
        tracers.reshape(field), land_mask, level_counts, fold_partner.reshape(1, COLS),
        cotangent.reshape(field), w_first, b_first.reshape(1, HID), w_second,
        b_second.reshape(1, HID), w_head.reshape(1, HID), b_head,
    )
    out, grad, first, second, head = pl.pallas_call(
        hand_over,
        out_shape=[jax.ShapeDtypeStruct(r.shape, F32) for r in results],
        in_specs=[vmem] * 5,
        out_specs=[vmem] * 5,
        name="hand_over",
    )(*(pltpu.with_memory_space_constraint(r, pltpu.VMEM) for r in results))
    return (
        out.reshape(tracers.shape), grad.reshape(tracers.shape), first, second, head.reshape(HID)
    )


def solution(mesh):
    lat_count, lon_count = mesh.shape["lat"], mesh.shape["lon"]
    grid = P(None, None, "lat", "lon")
    return jax.shard_map(
        lambda *args: per_device(lat_count, lon_count, *args),
        mesh=mesh,
        in_specs=(
            grid, P("lat", "lon"), P("lat", "lon"), P("lon"), grid,
            P(), P(), P(), P(), P(), P(),
        ),
        out_specs=(grid, grid, P(), P(), P()),
        check_vma=False,
    )
```

```python
import math

import jax
import jax.numpy as jnp
from jax import lax
from jax.experimental import pallas as pl
from jax.experimental.pallas import tpu as pltpu
from jax.sharding import PartitionSpec as P

KMAX = 0.24
F32 = jnp.float32
BF16 = jnp.bfloat16
MESH = pl.DeviceIdType.MESH

NZ = 4
ROWS = 16
COLS = 128
HID = 128
FIELDS = 2 * NZ
CHUNKS = NZ * ROWS // 8
LANES = 8 * COLS
EAST, WEST, NORTH, SOUTH = 0, 1, 2, 3
HALF = NZ * ROWS
OPPOSITE = (WEST, EAST, SOUTH, NORTH)


PLANE = ("x", "y_high", "y_low")
PILLAR = ("core", "z")
RIM = ("z", "y_low")


def place_sizes(lat_count, lon_count):
    if lat_count == 16 and lon_count == 16:
        return {"core": 2, "x": 4, "y_high": 2, "y_low": 2, "z": 8}
    return {"core": 1, "x": lat_count, "y_high": 1, "y_low": 1, "z": lon_count}


def offsets(dims, sizes):
    steps = [{}]
    for d in dims:
        steps = [{**s, d: o} for s in steps for o in range(sizes[d])]

    def hops(s):
        y = {(0, 0): 0, (1, 0): 2, (0, 1): 1, (1, 1): 1}[s.get("y_high", 0), s.get("y_low", 0)]
        x, z = s.get("x", 0), s.get("z", 0)
        return y + min(x, sizes["x"] - x) + min(z, sizes["z"] - z)

    return sorted([s for s in steps if any(s.values())], key=hops, reverse=True)


def piece_rows(parts):
    return HID // parts, -(-8 // parts)


def halves(x):
    high = x.astype(BF16)
    return high, (x - high.astype(F32)).astype(BF16)


def dot(a, b):
    return jnp.dot(a, b, preferred_element_type=F32)


def dot_nt(a, b):
    return lax.dot_general(a, b, (((1,), (1,)), ((), ())), preferred_element_type=F32)


def lane_roll(x, by):
    flat = x.reshape(-1, COLS)
    return pltpu.roll(flat, by % COLS, 1).reshape(x.shape)


def column(row):
    return jnp.broadcast_to(row, (COLS, COLS)).T


def kernel(
    lat_count, lon_count,
    tracers, land, levels, partner, cotangent, w_first, b_first, w_second, b_second, w_head, b_head,
    tracers_out, tracer_grad, gw_first, gw_second, gw_head,
    w1_rows, w1_fwd, w1_bwd, w2_fwd, w2_bwd, bias2, head,
    wet_ext, pair, state0, state1, adj0, adj1, kap0, kap1, contrast0, contrast1, coef0, coef1,
    slope0, slope1, direct, feats0, feats1, logits, h1_0, h1_1, h2_0, h2_1,
    u2_0, u2_1, u1_0, u1_1, by_feat0, by_feat1,
    obar, acc2, acc1, acch,
    beside_out, beside_in, across_out, across_in, wet_beside_out, wet_beside_in, first_out, first_in,
    fold_first, folded,
    parts, parts_plane, parts_pillar, gathered, extras,
    send_sem, recv_sem, fold_send, fold_recv, sum_send, sum_recv, in_sem,
    land_here, levels_here, partner_here, w1_here, b1_here, w2_here, b2_here, wh_here,
):
    lat = lax.axis_index("lat")
    lon = lax.axis_index("lon")
    at_top = lat == lat_count - 1
    at_bottom = lat == 0
    east = lax.rem(lon + 1, lon_count)
    west = lax.rem(lon + lon_count - 1, lon_count)

    sizes = place_sizes(lat_count, lon_count)
    core_count, x_count, y_low_count = sizes["core"], sizes["x"], sizes["y_low"]
    here = {
        "core": lax.rem(lat, core_count),
        "x": lax.rem(lax.div(lat, core_count), x_count),
        "y_high": lax.div(lat, core_count * x_count),
        "y_low": lax.rem(lon, y_low_count),
        "z": lax.div(lon, y_low_count),
    }

    def device_at(at):
        return {
            "lat": (at["y_high"] * x_count + at["x"]) * core_count + at["core"],
            "lon": at["z"] * y_low_count + at["y_low"],
        }

    def moved(offset):
        return {d: lax.rem(here[d] + offset.get(d, 0), sizes[d]) for d in here}

    def slot(dims, at):
        index = 0
        for d in dims:
            index = index * sizes[d] + at[d]
        return index

    def load(i, source, target):
        copy = pltpu.make_async_copy(source, target, in_sem.at[i])
        copy.start()
        return copy

    loads = [
        load(0, land, land_here),
        load(1, levels, levels_here),
        load(2, tracers, state0.at[:, pl.ds(8, ROWS), :]),
        load(3, cotangent, adj0.at[:, pl.ds(8, ROWS), :]),
        load(4, partner, partner_here),
        load(5, w_first, w1_here),
        load(6, b_first, b1_here),
        load(7, w_second, w2_here),
        load(8, b_second, b2_here),
        load(9, w_head, wh_here),
    ]
    barrier = pltpu.get_barrier_semaphore()

    def greet(device):
        pl.semaphore_signal(barrier, inc=1, device_id=device, device_id_type=MESH)

    @pl.when(at_top)
    def _():
        for offset in offsets(RIM, sizes):
            greet(device_at(moved(offset)))

    greeted = 4
    for dims in (PILLAR, PLANE):
        for offset in offsets(dims, sizes):
            greet(device_at(moved(offset)))
            greeted += 1
    greet({"lat": lat, "lon": east})
    greet({"lat": lat, "lon": west})
    greet({"lat": lax.rem(lat + 1, lat_count), "lon": lon})
    greet({"lat": lax.rem(lat + lat_count - 1, lat_count), "lon": lon})

    lane3 = lax.broadcasted_iota(jnp.int32, (FIELDS, ROWS, COLS), 2)
    lane8 = lax.broadcasted_iota(jnp.int32, (8, COLS), 1)
    sub8 = lax.broadcasted_iota(jnp.int32, (8, COLS), 0)

    send0 = {EAST: wet_beside_out.at[0], WEST: wet_beside_out.at[1],
             NORTH: first_out.at[0], SOUTH: first_out.at[1]}
    recv0 = {EAST: wet_beside_in.at[0], WEST: wet_beside_in.at[1],
             NORTH: first_in.at[0], SOUTH: first_in.at[1]}
    send1, send2, send3 = (
        {EAST: beside_out.at[i, 0], WEST: beside_out.at[i, 1],
         NORTH: across_out.at[i, 0], SOUTH: across_out.at[i, 1]}
        for i in range(3)
    )
    recv1, recv2, recv3 = (
        {EAST: beside_in.at[i, 0], WEST: beside_in.at[i, 1],
         NORTH: across_in.at[i, 0], SOUTH: across_in.at[i, 1]}
        for i in range(3)
    )
    fold0, fold1, fold2, fold3 = fold_first, folded.at[0], folded.at[1], folded.at[2]

    def to_side(phase, side, sends, recvs):
        target = {
            EAST: {"lat": lat, "lon": east},
            WEST: {"lat": lat, "lon": west},
            NORTH: {"lat": jnp.minimum(lat + 1, lat_count - 1), "lon": lon},
            SOUTH: {"lat": jnp.maximum(lat - 1, 0), "lon": lon},
        }[side]
        back = OPPOSITE[side]
        return pltpu.make_async_remote_copy(
            src_ref=sends[side], dst_ref=recvs[back],
            send_sem=send_sem.at[phase, side], recv_sem=recv_sem.at[phase, back],
            device_id=target, device_id_type=MESH,
        )

    def start_phase(phase, sends, recvs, folds):
        @pl.when(at_top)
        def _():
            for offset in offsets(RIM, sizes):
                pltpu.make_async_remote_copy(
                    src_ref=sends[NORTH], dst_ref=folds.at[lon],
                    send_sem=fold_send.at[phase], recv_sem=fold_recv.at[phase],
                    device_id=device_at(moved(offset)), device_id_type=MESH,
                ).start()

        to_side(phase, EAST, sends, recvs).start()
        to_side(phase, WEST, sends, recvs).start()

        @pl.when(jnp.logical_not(at_top))
        def _():
            to_side(phase, NORTH, sends, recvs).start()

        @pl.when(jnp.logical_not(at_bottom))
        def _():
            to_side(phase, SOUTH, sends, recvs).start()

        @pl.when(at_top)
        def _():
            folds[lon] = sends[NORTH][...]

    def wait_phase(phase, sends, recvs, folds):
        to_side(phase, WEST, sends, recvs).wait_recv()
        to_side(phase, EAST, sends, recvs).wait_recv()

        @pl.when(jnp.logical_not(at_top))
        def _():
            to_side(phase, SOUTH, sends, recvs).wait_recv()

        @pl.when(jnp.logical_not(at_bottom))
        def _():
            to_side(phase, NORTH, sends, recvs).wait_recv()

        @pl.when(at_top)
        def _():
            others = folds.at[pl.ds(0, lon_count - 1)]
            pltpu.make_async_copy(others, others, fold_recv.at[phase]).wait()
            block = jnp.broadcast_to(partner_here[...] >> 7, (8, COLS))
            lane = jnp.broadcast_to(partner_here[...] & (COLS - 1), (8, COLS))
            picked = jnp.zeros((8, COLS), F32)
            for j in range(lon_count):
                taken = jnp.take_along_axis(folds[j, 0:8, :], lane, axis=1)
                picked = jnp.where(block == j, taken, picked)
            recvs[NORTH][0:8, :] = picked
            if phase == 0:
                picked = jnp.zeros((8, COLS), F32)
                for j in range(lon_count):
                    counts = jnp.broadcast_to(folds[j, 8:9, :], (8, COLS))
                    taken = jnp.take_along_axis(counts, lane, axis=1)
                    picked = jnp.where(block == j, taken, picked)
                recvs[NORTH][8:9, :] = picked[0:1]

    def finish_phase(phase, sends, recvs, folds):
        to_side(phase, EAST, sends, recvs).wait_send()
        to_side(phase, WEST, sends, recvs).wait_send()

        @pl.when(jnp.logical_not(at_top))
        def _():
            to_side(phase, NORTH, sends, recvs).wait_send()

        @pl.when(jnp.logical_not(at_bottom))
        def _():
            to_side(phase, SOUTH, sends, recvs).wait_send()

        @pl.when(at_top)
        def _():
            others = folds.at[pl.ds(0, lon_count - 1)]
            pltpu.make_async_copy(others, others, fold_send.at[phase]).wait()

    def pack_beside(ext, sends, at):
        turned = ext[:, 8:24, :].reshape(COLS, COLS).T
        sends[EAST][at : at + 8, :] = turned[COLS - 8 :]
        sends[WEST][at : at + 8, :] = turned[:8]

    def pack(ext, sends):
        pack_beside(ext, sends, 0)
        sends[NORTH][0:8, :] = ext[:, 23, :]
        sends[SOUTH][0:8, :] = ext[:, 8, :]

    def unpack(ext, recvs):
        ext[:, 24, :] = recvs[NORTH][0:8, :]
        ext[:, 7, :] = recvs[SOUTH][0:8, :]

    def edge_columns(recvs, at):
        first = pltpu.roll(recvs[WEST][at : at + 8, :], 1, 0)
        last = pltpu.roll(recvs[EAST][at : at + 8, :], 7, 0)
        middle = jnp.zeros((COLS - 16, COLS), F32)
        return jnp.concatenate([first, middle, last], axis=0).T.reshape(FIELDS, ROWS, COLS)

    def sides(ext, edges):
        core = ext[:, 8:24, :]
        lane = lane3[: core.shape[0]]
        return [
            jnp.where(lane == COLS - 1, edges, lane_roll(core, -1)),
            jnp.where(lane == 0, edges, lane_roll(core, 1)),
            ext[:, 9:25, :],
            ext[:, 7:23, :],
        ]

    def store_feature(feats, chunk, f, value):
        feats[chunk, pl.ds(f, 8, stride=8), :] = value

    def own_features(ext, feats):
        for half in range(2):
            rows = pl.ds(8 + 8 * half, 8)
            wets = [wet_ext[k, rows, :] for k in range(NZ)]
            for t in range(2):
                cells = [ext[NZ * t + k, rows, :] for k in range(NZ)]
                vertical = [
                    (cells[k + 1] - cells[k]) * (wets[k + 1] * wets[k]) for k in range(NZ - 1)
                ]
                zero = jnp.zeros((8, COLS), F32)
                for k in range(NZ):
                    chunk = 2 * k + half
                    store_feature(feats, chunk, t, cells[k])
                    store_feature(feats, chunk, 2 + t, -vertical[k - 1] if k > 0 else zero)
                    store_feature(feats, chunk, 4 + t, vertical[k] if k < NZ - 1 else zero)

    def halo_features(recvs, feats):
        north, south = recvs[NORTH][0:8, :], recvs[SOUTH][0:8, :]
        first = sub8 < NZ
        depths = [jnp.broadcast_to(recv0[side][8:9, :], (8, COLS)) for side in (NORTH, SOUTH)]
        level = lax.rem(sub8, NZ).astype(F32)
        wet = (level < jnp.where(first, *depths)).astype(F32)
        joint = jnp.where(
            lax.rem(sub8, NZ) == NZ - 1, 0.0, wet * pltpu.roll(wet, 7, 0)
        )
        fields = (
            jnp.where(first, north, pltpu.roll(south, 4, 0)),
            jnp.where(first, pltpu.roll(north, 4, 0), south),
        )
        for t, cells in enumerate(fields):
            vertical = (pltpu.roll(cells, 7, 0) - cells) * joint
            store_feature(feats, CHUNKS, t, cells)
            store_feature(feats, CHUNKS, 2 + t, -pltpu.roll(vertical, 1, 0))
            store_feature(feats, CHUNKS, 4 + t, vertical)
        column_features(
            recvs[EAST][0:1, :], recvs[WEST][7:8, :], edge_wet(), feats, CHUNKS + 1
        )
        return wet

    def paired(east_row, west_row):
        east_row = jnp.broadcast_to(east_row, (8, COLS))
        west_row = jnp.broadcast_to(west_row, (8, COLS))
        first = lane8 < HALF
        return (
            jnp.where(first, east_row, pltpu.roll(west_row, HALF, 1)),
            jnp.where(first, pltpu.roll(east_row, HALF, 1), west_row),
        )

    def joint_column(wet_col):
        below = pltpu.roll(wet_col, COLS - ROWS, 1)
        return jnp.where(lax.rem(lane8, HALF) >= HALF - ROWS, 0.0, wet_col * below)

    def column_features(east_row, west_row, wet_col, feats, chunk):
        joint = joint_column(wet_col)
        for t, cells in enumerate(paired(east_row, west_row)):
            vertical = (pltpu.roll(cells, COLS - ROWS, 1) - cells) * joint
            feats[chunk, t : t + 1, :] = cells[0:1]
            feats[chunk, 2 + t : 3 + t, :] = -pltpu.roll(vertical, ROWS, 1)[0:1]
            feats[chunk, 4 + t : 5 + t, :] = vertical[0:1]

    def edge_wet():
        return paired(recv0[EAST][8:9, :], recv0[WEST][15:16, :])[0]

    def wide(x, n):
        return jnp.concatenate([x] * n, axis=1) if n > 1 else x

    def closure_chunk(feats, chunk, n, keep=None):
        f = [feats[chunk, 8 * q : 8 * q + 8, :] for q in range(n)]
        f = jnp.concatenate(f, axis=1) if n > 1 else f[0]
        high = f.astype(BF16).astype(F32)
        low = f - high
        stacked = jnp.concatenate([high, low, high, low], axis=0).astype(BF16)
        h1 = jnp.tanh(dot(w1_fwd[...], stacked))
        h1_high, h1_low = halves(h1)
        pre2 = dot(w2_fwd[...], jnp.concatenate([h1_high, h1_low, h1_high], axis=0))
        h2 = jnp.tanh(pre2 + wide(bias2[...], n))
        o = jnp.sum(h2 * wide(head[...], n), axis=0, keepdims=True)
        for q in range(n):
            logits[chunk, q : q + 1, :] = o[:, COLS * q : COLS * (q + 1)]
        if keep is None:
            return
        h1_ref, h2_ref, u2_ref, u1_ref, by_feat = keep
        h1_ref[chunk, :HID, :] = h1_high
        h1_ref[chunk, HID:, :] = h1_low
        h2_ref[chunk] = h2
        u2 = wide(head[...], n) * (1.0 - h2 * h2)
        u2_ref[chunk] = u2
        u2_high, u2_low = halves(u2)
        by_h1 = dot(w2_bwd[...], jnp.concatenate([u2_high, u2_low, u2_high], axis=0))
        u1_high, u1_low = halves(by_h1 * (1.0 - h1 * h1))
        u1_ref[chunk, :HID, :] = u1_high
        u1_ref[chunk, HID:, :] = u1_low
        d = dot(w1_bwd[...], jnp.concatenate([u1_high, u1_low, u1_high], axis=0))
        for q in range(n):
            by_feat[chunk, 8 * q : 8 * q + 8, :] = d[:8, COLS * q : COLS * (q + 1)]

    def closure_own(feats, keep):
        @pl.loop(0, CHUNKS, unroll=CHUNKS)
        def _(chunk):
            closure_chunk(feats, chunk, 8, keep)

    def kappa_from(o, wet):
        gate = jax.nn.sigmoid(o + b_head[0])
        return KMAX * gate * wet, KMAX * gate * (1.0 - gate) * wet

    def advance(phase, state, feats, sends, recvs, folds, keep, kap, slope, contrast, coef):
        own_features(state, feats)
        closure_own(feats, keep)
        wait_phase(phase, sends, recvs, folds)
        unpack(state, recvs)
        if phase == 0:
            for k in range(NZ):
                wet_ext[k, 24:25, :] = (recvs[NORTH][8:9, :] > k).astype(F32)
                wet_ext[k, 7:8, :] = (recvs[SOUTH][8:9, :] > k).astype(F32)
            wet = wet_ext[:NZ, 8:24, :]
            around = sides(wet_ext.at[pl.ds(0, NZ)], edge_columns(recvs, 8)[:NZ])
            for n in range(4):
                pair[n] = 0.5 * wet * around[n]
        wet_halo = halo_features(recvs, feats)
        closure_chunk(feats, CHUNKS, 8)
        closure_chunk(feats, CHUNKS + 1, 1)
        for k in range(NZ):
            for half in range(2):
                rows = pl.ds(8 + 8 * half, 8)
                value, rise = kappa_from(logits[2 * k + half], wet_ext[k, rows, :])
                kap[k, rows, :] = value
                slope[2 * k + half] = rise
        value, _ = kappa_from(logits[CHUNKS], wet_halo)
        for k in range(NZ):
            kap[k, 24:25, :] = value[k : k + 1]
            kap[k, 7:8, :] = value[NZ + k : NZ + k + 1]
        value, _ = kappa_from(logits[CHUNKS + 1], edge_wet())
        same = jnp.broadcast_to(value[0:1], (8, COLS))
        middle = jnp.zeros((COLS - 16, COLS), F32)
        kap_edges = jnp.concatenate([pltpu.roll(same, NZ * ROWS, 1), middle, same], axis=0).T
        kap_sides = sides(kap, kap_edges[: NZ * ROWS].reshape(NZ, ROWS, COLS))
        tracer_sides = sides(state, edge_columns(recvs, 0))
        core = state[:, 8:24, :]
        own_kap = kap[:, 8:24, :]
        change = jnp.zeros_like(core)
        for n in range(4):
            difference = tracer_sides[n] - core
            weight = (own_kap + kap_sides[n]) * pair[n]
            contrast[n] = difference
            coef[n] = weight
            change = change + jnp.concatenate([weight, weight], 0) * difference
        return core + change

    def pull_flux(adjoint, recvs, contrast, coef, slope):
        core = adjoint[:, 8:24, :]
        around = sides(adjoint, edge_columns(recvs, 0))
        total_direct = core
        kappa_bar = jnp.zeros((NZ, ROWS, COLS), F32)
        for n in range(4):
            difference = around[n] - core
            weight = coef[n]
            total_direct = total_direct + jnp.concatenate([weight, weight], 0) * difference
            product = contrast[n] * difference
            kappa_bar = kappa_bar - pair[n] * (product[:NZ] + product[NZ:])
        direct[...] = total_direct
        obar[...] = kappa_bar.reshape(CHUNKS, 8, COLS) * slope[...]

    def add_weights(feats, keep):
        h1_ref, h2_ref, u2_ref, u1_ref, _ = keep

        @pl.loop(0, CHUNKS, unroll=CHUNKS)
        def _(chunk):
            bar = jnp.concatenate([obar[chunk, q : q + 1, :] for q in range(8)], axis=1)
            high, low = halves(u2_ref[chunk] * bar)
            acc2[...] += dot_nt(h1_ref[chunk], jnp.concatenate([high, low], axis=0))
            f = jnp.concatenate([feats[chunk, 8 * q : 8 * q + 8, :] for q in range(8)], axis=1)
            f = f * bar
            high = f.astype(BF16).astype(F32)
            stacked = jnp.concatenate([high, f - high], axis=0).astype(BF16)
            acc1[...] += dot_nt(stacked, u1_ref[chunk])
            weighted = h2_ref[chunk] * bar
            heads = weighted[:, :COLS]
            for q in range(1, 8):
                heads = heads + weighted[:, COLS * q : COLS * (q + 1)]
            acch[...] += heads

    def pull_state(by_feat, store):
        for half in range(2):
            rows = pl.ds(8 * half, 8)
            wets = [wet_ext[k, pl.ds(8 + 8 * half, 8), :] for k in range(NZ)]
            bars = [obar[2 * k + half] for k in range(NZ)]
            for t in range(2):
                bar = [
                    [by_feat[2 * k + half, pl.ds(f, 8, stride=8), :] * bars[k] for k in range(NZ)]
                    for f in (t, 2 + t, 4 + t)
                ]
                vertical = [
                    (bar[2][k] - bar[1][k + 1]) * (wets[k + 1] * wets[k]) for k in range(NZ - 1)
                ]
                for k in range(NZ):
                    value = direct[NZ * t + k, rows, :] + bar[0][k]
                    if k < NZ - 1:
                        value = value - vertical[k]
                    if k > 0:
                        value = value + vertical[k - 1]
                    store(NZ * t + k, half, value)

    loads[0].wait()
    loads[1].wait()
    depth_here = land_here[...] * levels_here[...]
    for k in range(NZ):
        wet = (k < depth_here).astype(F32)
        wet_ext[k, 8:24, :] = wet
        wet_ext[NZ + k, 8:24, :] = wet
    pack_beside(wet_ext, send0, 8)
    depths = depth_here.astype(F32)
    send0[NORTH][8:9, :] = depths[ROWS - 1 :]
    send0[SOUTH][8:9, :] = depths[0:1]
    loads[2].wait()
    pack(state0, send0)

    @pl.when(at_bottom)
    def _():
        for recvs in (recv0, recv1, recv2, recv3):
            recvs[SOUTH][...] = jnp.zeros(recvs[SOUTH].shape, F32)

    for copy in loads[3:]:
        copy.wait()

    @pl.when(jnp.logical_not(at_top))
    def _():
        pl.semaphore_wait(barrier, greeted)

    @pl.when(at_top)
    def _():
        pl.semaphore_wait(barrier, greeted + lon_count - 1)

    start_phase(0, send0, recv0, fold0)
    pack(adj0, send3)
    start_phase(3, send3, recv3, fold3)

    w1_rows[0:6, :] = w1_here[...]
    w1_rows[6:7, :] = b1_here[...]
    w1_rows[7:8, :] = jnp.zeros((1, HID), F32)
    w1 = w1_rows[...]
    w1_high = w1.astype(BF16).astype(F32)
    w1_low = w1 - w1_high
    tall = jnp.concatenate(
        [w1_high, w1_high, w1_low, w1_low, jnp.zeros((HID - 32, HID), F32)], axis=0
    )
    w1_fwd[...] = tall.T[:, :32].astype(BF16)
    blank = jnp.zeros((8, HID), F32)
    w1_high = jnp.concatenate([w1_high, blank], axis=0).astype(BF16)
    w1_low = jnp.concatenate([w1_low, blank], axis=0).astype(BF16)
    w1_bwd[...] = jnp.concatenate([w1_high, w1_high, w1_low], axis=1)
    w2 = w2_here[...]
    high, low = halves(w2)
    w2_bwd[...] = jnp.concatenate([high, high, low], axis=1)
    high, low = halves(w2.T)
    w2_fwd[...] = jnp.concatenate([high, high, low], axis=1)
    bias2[...] = column(b2_here[...])
    head[...] = column(wh_here[...])
    ones_row = jnp.where(sub8 == 6, 1.0, 0.0)
    for feats in (feats0, feats1):
        for chunk in range(CHUNKS + 1):
            feats[chunk, pl.ds(6, 8, stride=8), :] = jnp.ones((8, COLS), F32)
            feats[chunk, pl.ds(7, 8, stride=8), :] = jnp.zeros((8, COLS), F32)
        feats[CHUNKS + 1, 0:8, :] = ones_row
    logits[CHUNKS + 1] = jnp.zeros((8, COLS), F32)
    acc2[...] = jnp.zeros_like(acc2)
    acc1[...] = jnp.zeros_like(acc1)
    acch[...] = jnp.zeros_like(acch)

    keep0 = (h1_0, h2_0, u2_0, u1_0, by_feat0)
    keep1 = (h1_1, h2_1, u2_1, u1_1, by_feat1)

    state1[:, 8:24, :] = advance(
        0, state0, feats0, send0, recv0, fold0, keep0, kap0, slope0, contrast0, coef0
    )
    pack(state1, send1)
    start_phase(1, send1, recv1, fold1)
    tracers_out[...] = advance(
        1, state1, feats1, send1, recv1, fold1, keep1, kap1, slope1, contrast1, coef1
    )

    wait_phase(3, send3, recv3, fold3)
    unpack(adj0, recv3)
    pull_flux(adj0, recv3, contrast1, coef1, slope1)

    def store_adjoint(i, half, value):
        adj1[i, 8 + 8 * half : 16 + 8 * half, :] = value

    pull_state(by_feat1, store_adjoint)
    pack(adj1, send2)
    start_phase(2, send2, recv2, fold2)
    add_weights(feats1, keep1)
    wait_phase(2, send2, recv2, fold2)
    unpack(adj1, recv2)
    pull_flux(adj1, recv2, contrast0, coef0, slope0)
    add_weights(feats0, keep0)

    plane = x_count * sizes["y_high"] * y_low_count
    pillar = core_count * sizes["z"]
    piece, spare = piece_rows(plane)
    second = (
        (acc2[HID:, HID:] + acc2[HID:, :HID]) + acc2[:HID, HID:]
    ) + acc2[:HID, :HID]
    first = (acc1[8:, :HID] + acc1[:8, HID:]) + acc1[:8, :HID]
    head_row = jnp.sum(acch[...].T, axis=0, keepdims=True)
    extra = jnp.where(sub8 == 6, jnp.broadcast_to(head_row, (8, COLS)), first)
    for p in range(plane):
        parts[p, :piece, :] = second[piece * p : piece * (p + 1)]
        if spare * p < 8:
            parts[p, piece:, :] = extra[spare * p : spare * (p + 1)]
        else:
            parts[p, piece:, :] = jnp.zeros((spare, COLS), F32)

    def share(dims, step, source, target):
        me = slot(dims, here)
        for offset in offsets(dims, sizes):
            there = moved(offset)
            pltpu.make_async_remote_copy(
                src_ref=source(slot(dims, there)), dst_ref=target.at[me],
                send_sem=sum_send.at[step], recv_sem=sum_recv.at[step],
                device_id=device_at(there), device_id_type=MESH,
            ).start()
        return me

    def wait_all(ref, count, sem):
        some = ref.at[pl.ds(0, count)]
        pltpu.make_async_copy(some, some, sem).wait()

    me = share(PLANE, 0, lambda there: parts.at[there], parts_plane)
    parts_plane[me] = parts[me]

    def finish(i, half, value):
        tracer_grad[i, 8 * half : 8 * half + 8, :] = value

    pull_state(by_feat0, finish)

    wait_all(parts_plane, plane - 1, sum_recv.at[0])
    summed = parts_plane[0]
    for p in range(1, plane):
        summed = summed + parts_plane[p]
    me = slot(PILLAR, here)
    parts_pillar[me] = summed
    share(PILLAR, 1, lambda there: parts_pillar.at[me], parts_pillar)
    wait_all(parts_pillar, pillar - 1, sum_recv.at[1])
    summed = parts_pillar[0]
    for p in range(1, pillar):
        summed = summed + parts_pillar[p]
    cells_all = lat_count * ROWS * lon_count * COLS * NZ
    me = slot(PLANE, here)
    gathered[me] = summed * (1.0 / math.sqrt(cells_all))
    share(PLANE, 2, lambda there: gathered.at[me], gathered)
    wait_all(gathered, plane - 1, sum_recv.at[2])
    for p in range(plane):
        gw_second[piece * p : piece * (p + 1), :] = gathered[p, :piece, :]
        if spare * p < 8:
            extras[spare * p : spare * (p + 1), :] = gathered[p, piece:, :]
    gw_first[...] = extras[0:6, :]
    gw_head[...] = extras[6:7, :]

    finish_phase(0, send0, recv0, fold0)
    finish_phase(1, send1, recv1, fold1)
    finish_phase(2, send2, recv2, fold2)
    finish_phase(3, send3, recv3, fold3)
    wait_all(parts_plane, plane - 1, sum_send.at[0])
    wait_all(parts_pillar, pillar - 1, sum_send.at[1])
    wait_all(gathered, plane - 1, sum_send.at[2])


def hand_over(*refs):
    for source, target in zip(refs[:5], refs[5:]):
        target[...] = source[...]


def per_device(lat_count, lon_count, tracers, land_mask, level_counts, fold_partner, cotangent,
               w_first, b_first, w_second, b_second, w_head, b_head):
    field = (FIELDS, ROWS, COLS)
    ext = pltpu.VMEM((FIELDS, 32, COLS), F32)
    kap = pltpu.VMEM((NZ, 32, COLS), F32)
    feats = pltpu.VMEM((CHUNKS + 2, 64, COLS), F32)
    stack = pltpu.VMEM((CHUNKS, 2 * HID, LANES), BF16)
    dense = pltpu.VMEM((CHUNKS, HID, LANES), F32)
    tile = pltpu.VMEM((CHUNKS, 8, COLS), F32)
    sizes = place_sizes(lat_count, lon_count)
    plane = sizes["x"] * sizes["y_low"] * sizes["y_high"]
    pillar = sizes["core"] * sizes["z"]
    both = sum(piece_rows(plane))
    scratch = [
        pltpu.VMEM((8, HID), F32),
        pltpu.VMEM((HID, 32), BF16),
        pltpu.VMEM((16, 3 * HID), BF16),
        pltpu.VMEM((HID, 3 * HID), BF16),
        pltpu.VMEM((HID, 3 * HID), BF16),
        pltpu.VMEM((HID, COLS), F32),
        pltpu.VMEM((HID, COLS), F32),
        ext,
        pltpu.VMEM((4, NZ, ROWS, COLS), F32),
        ext, ext, ext, ext, kap, kap,
        pltpu.VMEM((4,) + field, F32),
        pltpu.VMEM((4,) + field, F32),
        pltpu.VMEM((4, NZ, ROWS, COLS), F32),
        pltpu.VMEM((4, NZ, ROWS, COLS), F32),
        tile, tile,
        pltpu.VMEM(field, F32),
        feats, feats,
        pltpu.VMEM((CHUNKS + 2, 8, COLS), F32),
        stack, stack, dense, dense, dense, dense, stack, stack,
        pltpu.VMEM((CHUNKS, 64, COLS), F32),
        pltpu.VMEM((CHUNKS, 64, COLS), F32),
        tile,
        pltpu.VMEM((2 * HID, 2 * HID), F32),
        pltpu.VMEM((16, 2 * HID), F32),
        pltpu.VMEM((HID, COLS), F32),
    ]
    scratch += [pltpu.VMEM((3, 2, 8, COLS), F32)] * 4
    scratch += [pltpu.VMEM((2, 16, COLS), F32)] * 2 + [pltpu.VMEM((2, 9, COLS), F32)] * 2
    scratch += [pltpu.VMEM((lon_count, 9, COLS), F32), pltpu.VMEM((3, lon_count, 8, COLS), F32)]
    scratch += [
        pltpu.VMEM((plane, both, COLS), F32),
        pltpu.VMEM((plane, both, COLS), F32),
        pltpu.VMEM((pillar, both, COLS), F32),
        pltpu.VMEM((plane, both, COLS), F32),
        pltpu.VMEM((8, COLS), F32),
        pltpu.SemaphoreType.DMA((4, 4)),
        pltpu.SemaphoreType.DMA((4, 4)),
        pltpu.SemaphoreType.DMA((4,)),
        pltpu.SemaphoreType.DMA((4,)),
        pltpu.SemaphoreType.DMA((3,)),
        pltpu.SemaphoreType.DMA((3,)),
        pltpu.SemaphoreType.DMA((10,)),
        pltpu.VMEM((ROWS, COLS), jnp.int32),
        pltpu.VMEM((ROWS, COLS), jnp.int32),
        pltpu.VMEM((1, COLS), jnp.int32),
        pltpu.VMEM((6, HID), F32),
        pltpu.VMEM((1, HID), F32),
        pltpu.VMEM((HID, HID), F32),
        pltpu.VMEM((1, HID), F32),
        pltpu.VMEM((1, HID), F32),
    ]
    vmem = pl.BlockSpec(memory_space=pltpu.VMEM)
    anywhere = pl.BlockSpec(memory_space=pl.ANY)
    run = pl.pallas_call(
        lambda *refs: kernel(lat_count, lon_count, *refs),
        out_shape=[
            pltpu.VMEM(field, F32),
            pltpu.VMEM(field, F32),
            pltpu.VMEM((6, HID), F32),
            pltpu.VMEM((HID, HID), F32),
            pltpu.VMEM((1, HID), F32),
        ],
        in_specs=[anywhere] * 10 + [pl.BlockSpec(memory_space=pltpu.SMEM)],
        out_specs=[vmem] * 5,
        scratch_shapes=scratch,
        compiler_params=pltpu.CompilerParams(
            collective_id=0, has_side_effects=True, vmem_limit_bytes=56 * 2**20
        ),
        name="adjoint_steps",
    )
    results = run(
        tracers.reshape(field), land_mask, level_counts, fold_partner.reshape(1, COLS),
        cotangent.reshape(field), w_first, b_first.reshape(1, HID), w_second,
        b_second.reshape(1, HID), w_head.reshape(1, HID), b_head,
    )
    out, grad, first, second, head = pl.pallas_call(
        hand_over,
        out_shape=[jax.ShapeDtypeStruct(r.shape, F32) for r in results],
        in_specs=[vmem] * 5,
        out_specs=[vmem] * 5,
        name="hand_over",
    )(*(pltpu.with_memory_space_constraint(r, pltpu.VMEM) for r in results))
    return (
        out.reshape(tracers.shape), grad.reshape(tracers.shape), first, second, head.reshape(HID)
    )


def solution(mesh):
    lat_count, lon_count = mesh.shape["lat"], mesh.shape["lon"]
    grid = P(None, None, "lat", "lon")
    return jax.shard_map(
        lambda *args: per_device(lat_count, lon_count, *args),
        mesh=mesh,
        in_specs=(
            grid, P("lat", "lon"), P("lat", "lon"), P("lon"), grid,
            P(), P(), P(), P(), P(), P(),
        ),
        out_specs=(grid, grid, P(), P(), P()),
        check_vma=False,
    )
```

```python
import math

import jax
import jax.numpy as jnp
from jax import lax
from jax.experimental import pallas as pl
from jax.experimental.pallas import tpu as pltpu
from jax.sharding import PartitionSpec as P

KMAX = 0.24
F32 = jnp.float32
BF16 = jnp.bfloat16
MESH = pl.DeviceIdType.MESH

NZ = 4
ROWS = 16
COLS = 128
HID = 128
FIELDS = 2 * NZ
CHUNKS = NZ * ROWS // 8
LANES = 8 * COLS
EAST, WEST, NORTH, SOUTH = 0, 1, 2, 3
HALF = NZ * ROWS
OPPOSITE = (WEST, EAST, SOUTH, NORTH)


PLANE = ("x", "y_high", "y_low")
PILLAR = ("core", "z")
RIM = ("z", "y_low")


def place_sizes(lat_count, lon_count):
    if lat_count == 16 and lon_count == 16:
        return {"core": 2, "x": 4, "y_high": 2, "y_low": 2, "z": 8}
    return {"core": 1, "x": lat_count, "y_high": 1, "y_low": 1, "z": lon_count}


def offsets(dims, sizes):
    steps = [{}]
    for d in dims:
        steps = [{**s, d: o} for s in steps for o in range(sizes[d])]

    def hops(s):
        y = {(0, 0): 0, (1, 0): 2, (0, 1): 1, (1, 1): 1}[s.get("y_high", 0), s.get("y_low", 0)]
        x, z = s.get("x", 0), s.get("z", 0)
        return y + min(x, sizes["x"] - x) + min(z, sizes["z"] - z)

    return sorted([s for s in steps if any(s.values())], key=hops, reverse=True)


def piece_rows(parts):
    return HID // parts, -(-8 // parts)


def halves(x):
    high = x.astype(BF16)
    return high, (x - high.astype(F32)).astype(BF16)


def dot(a, b):
    return jnp.dot(a, b, preferred_element_type=F32)


def product(weights, high, low):
    both = dot(weights[...], jnp.concatenate([high, low], axis=0))
    half = both.shape[0] // 2
    return both[:half] + both[half:]


def dot_nt(a, b):
    return lax.dot_general(a, b, (((1,), (1,)), ((), ())), preferred_element_type=F32)


def lane_roll(x, by):
    flat = x.reshape(-1, COLS)
    return pltpu.roll(flat, by % COLS, 1).reshape(x.shape)


def column(row):
    return jnp.broadcast_to(row, (COLS, COLS)).T


def kernel(
    lat_count, lon_count,
    tracers, land, levels, partner, cotangent, w_first, b_first, w_second, b_second, w_head, b_head,
    tracers_out, tracer_grad, gw_first, gw_second, gw_head,
    w1_rows, w1_fwd, w1_bwd, w2_fwd, w2_bwd, bias2, head,
    wet_ext, pair, state0, state1, adj0, adj1, kap0, kap1, contrast0, contrast1, coef0, coef1,
    slope0, slope1, direct, feats0, feats1, logits, h1_0, h1_1, h2_0, h2_1,
    u2_0, u2_1, u1_0, u1_1, by_feat0, by_feat1,
    obar, acc2, acc1, acch,
    beside_out, beside_in, across_out, across_in, wet_beside_out, wet_beside_in, first_out, first_in,
    fold_first, folded,
    parts, parts_plane, parts_pillar, gathered, extras,
    send_sem, recv_sem, fold_send, fold_recv, sum_send, sum_recv, in_sem,
    land_here, levels_here, partner_here, w1_here, b1_here, w2_here, b2_here, wh_here,
):
    lat = lax.axis_index("lat")
    lon = lax.axis_index("lon")
    at_top = lat == lat_count - 1
    at_bottom = lat == 0
    east = lax.rem(lon + 1, lon_count)
    west = lax.rem(lon + lon_count - 1, lon_count)

    sizes = place_sizes(lat_count, lon_count)
    core_count, x_count, y_low_count = sizes["core"], sizes["x"], sizes["y_low"]
    here = {
        "core": lax.rem(lat, core_count),
        "x": lax.rem(lax.div(lat, core_count), x_count),
        "y_high": lax.div(lat, core_count * x_count),
        "y_low": lax.rem(lon, y_low_count),
        "z": lax.div(lon, y_low_count),
    }

    def device_at(at):
        return {
            "lat": (at["y_high"] * x_count + at["x"]) * core_count + at["core"],
            "lon": at["z"] * y_low_count + at["y_low"],
        }

    def moved(offset):
        return {d: lax.rem(here[d] + offset.get(d, 0), sizes[d]) for d in here}

    def slot(dims, at):
        index = 0
        for d in dims:
            index = index * sizes[d] + at[d]
        return index

    def load(i, source, target):
        copy = pltpu.make_async_copy(source, target, in_sem.at[i])
        copy.start()
        return copy

    loads = [
        load(0, land, land_here),
        load(1, levels, levels_here),
        load(2, tracers, state0.at[:, pl.ds(8, ROWS), :]),
        load(3, cotangent, adj0.at[:, pl.ds(8, ROWS), :]),
        load(4, partner, partner_here),
        load(5, w_first, w1_here),
        load(6, b_first, b1_here),
        load(7, w_second, w2_here),
        load(8, b_second, b2_here),
        load(9, w_head, wh_here),
    ]
    barrier = pltpu.get_barrier_semaphore()

    def greet(device):
        pl.semaphore_signal(barrier, inc=1, device_id=device, device_id_type=MESH)

    @pl.when(at_top)
    def _():
        for offset in offsets(RIM, sizes):
            greet(device_at(moved(offset)))

    greeted = 4
    for dims in (PILLAR, PLANE):
        for offset in offsets(dims, sizes):
            greet(device_at(moved(offset)))
            greeted += 1
    greet({"lat": lat, "lon": east})
    greet({"lat": lat, "lon": west})
    greet({"lat": lax.rem(lat + 1, lat_count), "lon": lon})
    greet({"lat": lax.rem(lat + lat_count - 1, lat_count), "lon": lon})

    lane3 = lax.broadcasted_iota(jnp.int32, (FIELDS, ROWS, COLS), 2)
    lane8 = lax.broadcasted_iota(jnp.int32, (8, COLS), 1)
    sub8 = lax.broadcasted_iota(jnp.int32, (8, COLS), 0)

    send0 = {EAST: wet_beside_out.at[0], WEST: wet_beside_out.at[1],
             NORTH: first_out.at[0], SOUTH: first_out.at[1]}
    recv0 = {EAST: wet_beside_in.at[0], WEST: wet_beside_in.at[1],
             NORTH: first_in.at[0], SOUTH: first_in.at[1]}
    send1, send2, send3 = (
        {EAST: beside_out.at[i, 0], WEST: beside_out.at[i, 1],
         NORTH: across_out.at[i, 0], SOUTH: across_out.at[i, 1]}
        for i in range(3)
    )
    recv1, recv2, recv3 = (
        {EAST: beside_in.at[i, 0], WEST: beside_in.at[i, 1],
         NORTH: across_in.at[i, 0], SOUTH: across_in.at[i, 1]}
        for i in range(3)
    )
    fold0, fold1, fold2, fold3 = fold_first, folded.at[0], folded.at[1], folded.at[2]

    def to_side(phase, side, sends, recvs):
        target = {
            EAST: {"lat": lat, "lon": east},
            WEST: {"lat": lat, "lon": west},
            NORTH: {"lat": jnp.minimum(lat + 1, lat_count - 1), "lon": lon},
            SOUTH: {"lat": jnp.maximum(lat - 1, 0), "lon": lon},
        }[side]
        back = OPPOSITE[side]
        return pltpu.make_async_remote_copy(
            src_ref=sends[side], dst_ref=recvs[back],
            send_sem=send_sem.at[phase, side], recv_sem=recv_sem.at[phase, back],
            device_id=target, device_id_type=MESH,
        )

    def start_phase(phase, sends, recvs, folds):
        @pl.when(at_top)
        def _():
            for offset in offsets(RIM, sizes):
                pltpu.make_async_remote_copy(
                    src_ref=sends[NORTH], dst_ref=folds.at[lon],
                    send_sem=fold_send.at[phase], recv_sem=fold_recv.at[phase],
                    device_id=device_at(moved(offset)), device_id_type=MESH,
                ).start()

        to_side(phase, EAST, sends, recvs).start()
        to_side(phase, WEST, sends, recvs).start()

        @pl.when(jnp.logical_not(at_top))
        def _():
            to_side(phase, NORTH, sends, recvs).start()

        @pl.when(jnp.logical_not(at_bottom))
        def _():
            to_side(phase, SOUTH, sends, recvs).start()

        @pl.when(at_top)
        def _():
            folds[lon] = sends[NORTH][...]

    def wait_phase(phase, sends, recvs, folds):
        to_side(phase, WEST, sends, recvs).wait_recv()
        to_side(phase, EAST, sends, recvs).wait_recv()

        @pl.when(jnp.logical_not(at_top))
        def _():
            to_side(phase, SOUTH, sends, recvs).wait_recv()

        @pl.when(jnp.logical_not(at_bottom))
        def _():
            to_side(phase, NORTH, sends, recvs).wait_recv()

        @pl.when(at_top)
        def _():
            others = folds.at[pl.ds(0, lon_count - 1)]
            pltpu.make_async_copy(others, others, fold_recv.at[phase]).wait()
            block = jnp.broadcast_to(partner_here[...] >> 7, (8, COLS))
            lane = jnp.broadcast_to(partner_here[...] & (COLS - 1), (8, COLS))
            picked = jnp.zeros((8, COLS), F32)
            for j in range(lon_count):
                taken = jnp.take_along_axis(folds[j, 0:8, :], lane, axis=1)
                picked = jnp.where(block == j, taken, picked)
            recvs[NORTH][0:8, :] = picked
            if phase == 0:
                picked = jnp.zeros((8, COLS), F32)
                for j in range(lon_count):
                    counts = jnp.broadcast_to(folds[j, 8:9, :], (8, COLS))
                    taken = jnp.take_along_axis(counts, lane, axis=1)
                    picked = jnp.where(block == j, taken, picked)
                recvs[NORTH][8:9, :] = picked[0:1]

    def finish_phase(phase, sends, recvs, folds):
        to_side(phase, EAST, sends, recvs).wait_send()
        to_side(phase, WEST, sends, recvs).wait_send()

        @pl.when(jnp.logical_not(at_top))
        def _():
            to_side(phase, NORTH, sends, recvs).wait_send()

        @pl.when(jnp.logical_not(at_bottom))
        def _():
            to_side(phase, SOUTH, sends, recvs).wait_send()

        @pl.when(at_top)
        def _():
            others = folds.at[pl.ds(0, lon_count - 1)]
            pltpu.make_async_copy(others, others, fold_send.at[phase]).wait()

    def pack_beside(ext, sends, at):
        turned = ext[:, 8:24, :].reshape(COLS, COLS).T
        sends[EAST][at : at + 8, :] = turned[COLS - 8 :]
        sends[WEST][at : at + 8, :] = turned[:8]

    def pack(ext, sends):
        pack_beside(ext, sends, 0)
        sends[NORTH][0:8, :] = ext[:, 23, :]
        sends[SOUTH][0:8, :] = ext[:, 8, :]

    def unpack(ext, recvs):
        ext[:, 24, :] = recvs[NORTH][0:8, :]
        ext[:, 7, :] = recvs[SOUTH][0:8, :]

    def edge_columns(recvs, at):
        first = pltpu.roll(recvs[WEST][at : at + 8, :], 1, 0)
        last = pltpu.roll(recvs[EAST][at : at + 8, :], 7, 0)
        middle = jnp.zeros((COLS - 16, COLS), F32)
        return jnp.concatenate([first, middle, last], axis=0).T.reshape(FIELDS, ROWS, COLS)

    def sides(ext, edges):
        core = ext[:, 8:24, :]
        lane = lane3[: core.shape[0]]
        return [
            jnp.where(lane == COLS - 1, edges, lane_roll(core, -1)),
            jnp.where(lane == 0, edges, lane_roll(core, 1)),
            ext[:, 9:25, :],
            ext[:, 7:23, :],
        ]

    def store_feature(feats, chunk, f, value):
        feats[chunk, pl.ds(f, 8, stride=8), :] = value

    def own_features(ext, feats):
        for half in range(2):
            rows = pl.ds(8 + 8 * half, 8)
            wets = [wet_ext[k, rows, :] for k in range(NZ)]
            for t in range(2):
                cells = [ext[NZ * t + k, rows, :] for k in range(NZ)]
                vertical = [
                    (cells[k + 1] - cells[k]) * (wets[k + 1] * wets[k]) for k in range(NZ - 1)
                ]
                zero = jnp.zeros((8, COLS), F32)
                for k in range(NZ):
                    chunk = 2 * k + half
                    store_feature(feats, chunk, t, cells[k])
                    store_feature(feats, chunk, 2 + t, -vertical[k - 1] if k > 0 else zero)
                    store_feature(feats, chunk, 4 + t, vertical[k] if k < NZ - 1 else zero)

    def halo_features(recvs, feats):
        north, south = recvs[NORTH][0:8, :], recvs[SOUTH][0:8, :]
        first = sub8 < NZ
        depths = [jnp.broadcast_to(recv0[side][8:9, :], (8, COLS)) for side in (NORTH, SOUTH)]
        level = lax.rem(sub8, NZ).astype(F32)
        wet = (level < jnp.where(first, *depths)).astype(F32)
        joint = jnp.where(
            lax.rem(sub8, NZ) == NZ - 1, 0.0, wet * pltpu.roll(wet, 7, 0)
        )
        fields = (
            jnp.where(first, north, pltpu.roll(south, 4, 0)),
            jnp.where(first, pltpu.roll(north, 4, 0), south),
        )
        for t, cells in enumerate(fields):
            vertical = (pltpu.roll(cells, 7, 0) - cells) * joint
            store_feature(feats, CHUNKS, t, cells)
            store_feature(feats, CHUNKS, 2 + t, -pltpu.roll(vertical, 1, 0))
            store_feature(feats, CHUNKS, 4 + t, vertical)
        column_features(
            recvs[EAST][0:1, :], recvs[WEST][7:8, :], edge_wet(), feats, CHUNKS + 1
        )
        return wet

    def paired(east_row, west_row):
        east_row = jnp.broadcast_to(east_row, (8, COLS))
        west_row = jnp.broadcast_to(west_row, (8, COLS))
        first = lane8 < HALF
        return (
            jnp.where(first, east_row, pltpu.roll(west_row, HALF, 1)),
            jnp.where(first, pltpu.roll(east_row, HALF, 1), west_row),
        )

    def joint_column(wet_col):
        below = pltpu.roll(wet_col, COLS - ROWS, 1)
        return jnp.where(lax.rem(lane8, HALF) >= HALF - ROWS, 0.0, wet_col * below)

    def column_features(east_row, west_row, wet_col, feats, chunk):
        joint = joint_column(wet_col)
        for t, cells in enumerate(paired(east_row, west_row)):
            vertical = (pltpu.roll(cells, COLS - ROWS, 1) - cells) * joint
            feats[chunk, t : t + 1, :] = cells[0:1]
            feats[chunk, 2 + t : 3 + t, :] = -pltpu.roll(vertical, ROWS, 1)[0:1]
            feats[chunk, 4 + t : 5 + t, :] = vertical[0:1]

    def edge_wet():
        return paired(recv0[EAST][8:9, :], recv0[WEST][15:16, :])[0]

    def wide(x, n):
        return jnp.concatenate([x] * n, axis=1) if n > 1 else x

    def closure_chunk(feats, chunk, n, keep=None):
        f = [feats[chunk, 8 * q : 8 * q + 8, :] for q in range(n)]
        f = jnp.concatenate(f, axis=1) if n > 1 else f[0]
        high = f.astype(BF16).astype(F32)
        low = f - high
        stacked = jnp.concatenate([high, low, high, low], axis=0).astype(BF16)
        h1 = jnp.tanh(dot(w1_fwd[...], stacked))
        h1_high, h1_low = halves(h1)
        pre2 = product(w2_fwd, h1_high, h1_low)
        h2 = jnp.tanh(pre2 + wide(bias2[...], n))
        o = jnp.sum(h2 * wide(head[...], n), axis=0, keepdims=True)
        for q in range(n):
            logits[chunk, q : q + 1, :] = o[:, COLS * q : COLS * (q + 1)]
        if keep is None:
            return
        h1_ref, h2_ref, u2_ref, u1_ref, by_feat = keep
        h1_ref[chunk, :HID, :] = h1_high
        h1_ref[chunk, HID:, :] = h1_low
        h2_ref[chunk] = h2
        u2 = wide(head[...], n) * (1.0 - h2 * h2)
        u2_ref[chunk] = u2
        u2_high, u2_low = halves(u2)
        by_h1 = product(w2_bwd, u2_high, u2_low)
        u1_high, u1_low = halves(by_h1 * (1.0 - h1 * h1))
        u1_ref[chunk, :HID, :] = u1_high
        u1_ref[chunk, HID:, :] = u1_low
        d = product(w1_bwd, u1_high, u1_low)
        for q in range(n):
            by_feat[chunk, 8 * q : 8 * q + 8, :] = d[:, COLS * q : COLS * (q + 1)]

    def closure_own(feats, keep):
        @pl.loop(0, CHUNKS, unroll=CHUNKS)
        def _(chunk):
            closure_chunk(feats, chunk, 8, keep)

    def kappa_from(o, wet):
        gate = jax.nn.sigmoid(o + b_head[0])
        return KMAX * gate * wet, KMAX * gate * (1.0 - gate) * wet

    def advance(phase, state, feats, sends, recvs, folds, keep, kap, slope, contrast, coef):
        own_features(state, feats)
        closure_own(feats, keep)
        wait_phase(phase, sends, recvs, folds)
        unpack(state, recvs)
        if phase == 0:
            for k in range(NZ):
                wet_ext[k, 24:25, :] = (recvs[NORTH][8:9, :] > k).astype(F32)
                wet_ext[k, 7:8, :] = (recvs[SOUTH][8:9, :] > k).astype(F32)
            wet = wet_ext[:NZ, 8:24, :]
            around = sides(wet_ext.at[pl.ds(0, NZ)], edge_columns(recvs, 8)[:NZ])
            for n in range(4):
                pair[n] = 0.5 * wet * around[n]
        wet_halo = halo_features(recvs, feats)
        closure_chunk(feats, CHUNKS, 8)
        closure_chunk(feats, CHUNKS + 1, 1)
        for k in range(NZ):
            for half in range(2):
                rows = pl.ds(8 + 8 * half, 8)
                value, rise = kappa_from(logits[2 * k + half], wet_ext[k, rows, :])
                kap[k, rows, :] = value
                slope[2 * k + half] = rise
        value, _ = kappa_from(logits[CHUNKS], wet_halo)
        for k in range(NZ):
            kap[k, 24:25, :] = value[k : k + 1]
            kap[k, 7:8, :] = value[NZ + k : NZ + k + 1]
        value, _ = kappa_from(logits[CHUNKS + 1], edge_wet())
        same = jnp.broadcast_to(value[0:1], (8, COLS))
        middle = jnp.zeros((COLS - 16, COLS), F32)
        kap_edges = jnp.concatenate([pltpu.roll(same, NZ * ROWS, 1), middle, same], axis=0).T
        kap_sides = sides(kap, kap_edges[: NZ * ROWS].reshape(NZ, ROWS, COLS))
        tracer_sides = sides(state, edge_columns(recvs, 0))
        core = state[:, 8:24, :]
        own_kap = kap[:, 8:24, :]
        change = jnp.zeros_like(core)
        for n in range(4):
            difference = tracer_sides[n] - core
            weight = (own_kap + kap_sides[n]) * pair[n]
            contrast[n] = difference
            coef[n] = weight
            change = change + jnp.concatenate([weight, weight], 0) * difference
        return core + change

    def pull_flux(adjoint, recvs, contrast, coef, slope):
        core = adjoint[:, 8:24, :]
        around = sides(adjoint, edge_columns(recvs, 0))
        total_direct = core
        kappa_bar = jnp.zeros((NZ, ROWS, COLS), F32)
        for n in range(4):
            difference = around[n] - core
            weight = coef[n]
            total_direct = total_direct + jnp.concatenate([weight, weight], 0) * difference
            product = contrast[n] * difference
            kappa_bar = kappa_bar - pair[n] * (product[:NZ] + product[NZ:])
        direct[...] = total_direct
        obar[...] = kappa_bar.reshape(CHUNKS, 8, COLS) * slope[...]

    def add_weights(feats, keep):
        h1_ref, h2_ref, u2_ref, u1_ref, _ = keep

        @pl.loop(0, CHUNKS, unroll=CHUNKS)
        def _(chunk):
            bar = jnp.concatenate([obar[chunk, q : q + 1, :] for q in range(8)], axis=1)
            high, low = halves(u2_ref[chunk] * bar)
            acc2[...] += dot_nt(h1_ref[chunk], jnp.concatenate([high, low], axis=0))
            f = jnp.concatenate([feats[chunk, 8 * q : 8 * q + 8, :] for q in range(8)], axis=1)
            f = f * bar
            high = f.astype(BF16).astype(F32)
            stacked = jnp.concatenate([high, f - high], axis=0).astype(BF16)
            acc1[...] += dot_nt(stacked, u1_ref[chunk])
            weighted = h2_ref[chunk] * bar
            heads = weighted[:, :COLS]
            for q in range(1, 8):
                heads = heads + weighted[:, COLS * q : COLS * (q + 1)]
            acch[...] += heads

    def pull_state(by_feat, store):
        for half in range(2):
            rows = pl.ds(8 * half, 8)
            wets = [wet_ext[k, pl.ds(8 + 8 * half, 8), :] for k in range(NZ)]
            bars = [obar[2 * k + half] for k in range(NZ)]
            for t in range(2):
                bar = [
                    [by_feat[2 * k + half, pl.ds(f, 8, stride=8), :] * bars[k] for k in range(NZ)]
                    for f in (t, 2 + t, 4 + t)
                ]
                vertical = [
                    (bar[2][k] - bar[1][k + 1]) * (wets[k + 1] * wets[k]) for k in range(NZ - 1)
                ]
                for k in range(NZ):
                    value = direct[NZ * t + k, rows, :] + bar[0][k]
                    if k < NZ - 1:
                        value = value - vertical[k]
                    if k > 0:
                        value = value + vertical[k - 1]
                    store(NZ * t + k, half, value)

    loads[0].wait()
    loads[1].wait()
    depth_here = land_here[...] * levels_here[...]
    for k in range(NZ):
        wet = (k < depth_here).astype(F32)
        wet_ext[k, 8:24, :] = wet
        wet_ext[NZ + k, 8:24, :] = wet
    pack_beside(wet_ext, send0, 8)
    depths = depth_here.astype(F32)
    send0[NORTH][8:9, :] = depths[ROWS - 1 :]
    send0[SOUTH][8:9, :] = depths[0:1]
    loads[2].wait()
    pack(state0, send0)

    @pl.when(at_bottom)
    def _():
        for recvs in (recv0, recv1, recv2, recv3):
            recvs[SOUTH][...] = jnp.zeros(recvs[SOUTH].shape, F32)

    for copy in loads[3:]:
        copy.wait()

    @pl.when(jnp.logical_not(at_top))
    def _():
        pl.semaphore_wait(barrier, greeted)

    @pl.when(at_top)
    def _():
        pl.semaphore_wait(barrier, greeted + lon_count - 1)

    start_phase(0, send0, recv0, fold0)
    pack(adj0, send3)
    start_phase(3, send3, recv3, fold3)

    w1_rows[0:6, :] = w1_here[...]
    w1_rows[6:7, :] = b1_here[...]
    w1_rows[7:8, :] = jnp.zeros((1, HID), F32)
    w1 = w1_rows[...]
    w1_high = w1.astype(BF16).astype(F32)
    w1_low = w1 - w1_high
    tall = jnp.concatenate(
        [w1_high, w1_high, w1_low, w1_low, jnp.zeros((HID - 32, HID), F32)], axis=0
    )
    w1_fwd[...] = tall.T[:, :32].astype(BF16)
    blank = jnp.zeros((8, HID), F32)
    w1_bwd[...] = jnp.concatenate(
        [jnp.concatenate([w1_high, w1_low], axis=0), jnp.concatenate([w1_high, blank], axis=0)],
        axis=1,
    ).astype(BF16)
    w2 = w2_here[...]
    for target, matrix in ((w2_bwd, w2), (w2_fwd, w2.T)):
        high, low = halves(matrix)
        target[:HID, :HID] = high
        target[:HID, HID:] = high
        target[HID:, :HID] = low
        target[HID:, HID:] = jnp.zeros((HID, HID), BF16)
    bias2[...] = column(b2_here[...])
    head[...] = column(wh_here[...])
    ones_row = jnp.where(sub8 == 6, 1.0, 0.0)
    for feats in (feats0, feats1):
        for chunk in range(CHUNKS + 1):
            feats[chunk, pl.ds(6, 8, stride=8), :] = jnp.ones((8, COLS), F32)
            feats[chunk, pl.ds(7, 8, stride=8), :] = jnp.zeros((8, COLS), F32)
        feats[CHUNKS + 1, 0:8, :] = ones_row
    logits[CHUNKS + 1] = jnp.zeros((8, COLS), F32)
    acc2[...] = jnp.zeros_like(acc2)
    acc1[...] = jnp.zeros_like(acc1)
    acch[...] = jnp.zeros_like(acch)

    keep0 = (h1_0, h2_0, u2_0, u1_0, by_feat0)
    keep1 = (h1_1, h2_1, u2_1, u1_1, by_feat1)

    state1[:, 8:24, :] = advance(
        0, state0, feats0, send0, recv0, fold0, keep0, kap0, slope0, contrast0, coef0
    )
    pack(state1, send1)
    start_phase(1, send1, recv1, fold1)
    tracers_out[...] = advance(
        1, state1, feats1, send1, recv1, fold1, keep1, kap1, slope1, contrast1, coef1
    )

    wait_phase(3, send3, recv3, fold3)
    unpack(adj0, recv3)
    pull_flux(adj0, recv3, contrast1, coef1, slope1)

    def store_adjoint(i, half, value):
        adj1[i, 8 + 8 * half : 16 + 8 * half, :] = value

    pull_state(by_feat1, store_adjoint)
    pack(adj1, send2)
    start_phase(2, send2, recv2, fold2)
    add_weights(feats1, keep1)
    wait_phase(2, send2, recv2, fold2)
    unpack(adj1, recv2)
    pull_flux(adj1, recv2, contrast0, coef0, slope0)
    add_weights(feats0, keep0)

    plane = x_count * sizes["y_high"] * y_low_count
    pillar = core_count * sizes["z"]
    piece, spare = piece_rows(plane)
    second = (
        (acc2[HID:, HID:] + acc2[HID:, :HID]) + acc2[:HID, HID:]
    ) + acc2[:HID, :HID]
    first = (acc1[8:, :HID] + acc1[:8, HID:]) + acc1[:8, :HID]
    head_row = jnp.sum(acch[...].T, axis=0, keepdims=True)
    extra = jnp.where(sub8 == 6, jnp.broadcast_to(head_row, (8, COLS)), first)
    for p in range(plane):
        parts[p, :piece, :] = second[piece * p : piece * (p + 1)]
        if spare * p < 8:
            parts[p, piece:, :] = extra[spare * p : spare * (p + 1)]
        else:
            parts[p, piece:, :] = jnp.zeros((spare, COLS), F32)

    def share(dims, step, source, target):
        me = slot(dims, here)
        for offset in offsets(dims, sizes):
            there = moved(offset)
            pltpu.make_async_remote_copy(
                src_ref=source(slot(dims, there)), dst_ref=target.at[me],
                send_sem=sum_send.at[step], recv_sem=sum_recv.at[step],
                device_id=device_at(there), device_id_type=MESH,
            ).start()
        return me

    def wait_all(ref, count, sem):
        some = ref.at[pl.ds(0, count)]
        pltpu.make_async_copy(some, some, sem).wait()

    me = share(PLANE, 0, lambda there: parts.at[there], parts_plane)
    parts_plane[me] = parts[me]

    def finish(i, half, value):
        tracer_grad[i, 8 * half : 8 * half + 8, :] = value

    pull_state(by_feat0, finish)

    wait_all(parts_plane, plane - 1, sum_recv.at[0])
    summed = parts_plane[0]
    for p in range(1, plane):
        summed = summed + parts_plane[p]
    me = slot(PILLAR, here)
    parts_pillar[me] = summed
    share(PILLAR, 1, lambda there: parts_pillar.at[me], parts_pillar)
    wait_all(parts_pillar, pillar - 1, sum_recv.at[1])
    summed = parts_pillar[0]
    for p in range(1, pillar):
        summed = summed + parts_pillar[p]
    cells_all = lat_count * ROWS * lon_count * COLS * NZ
    me = slot(PLANE, here)
    gathered[me] = summed * (1.0 / math.sqrt(cells_all))
    share(PLANE, 2, lambda there: gathered.at[me], gathered)
    wait_all(gathered, plane - 1, sum_recv.at[2])
    for p in range(plane):
        gw_second[piece * p : piece * (p + 1), :] = gathered[p, :piece, :]
        if spare * p < 8:
            extras[spare * p : spare * (p + 1), :] = gathered[p, piece:, :]
    gw_first[...] = extras[0:6, :]
    gw_head[...] = extras[6:7, :]

    finish_phase(0, send0, recv0, fold0)
    finish_phase(1, send1, recv1, fold1)
    finish_phase(2, send2, recv2, fold2)
    finish_phase(3, send3, recv3, fold3)
    wait_all(parts_plane, plane - 1, sum_send.at[0])
    wait_all(parts_pillar, pillar - 1, sum_send.at[1])
    wait_all(gathered, plane - 1, sum_send.at[2])


def hand_over(*refs):
    for source, target in zip(refs[:5], refs[5:]):
        target[...] = source[...]


def per_device(lat_count, lon_count, tracers, land_mask, level_counts, fold_partner, cotangent,
               w_first, b_first, w_second, b_second, w_head, b_head):
    field = (FIELDS, ROWS, COLS)
    ext = pltpu.VMEM((FIELDS, 32, COLS), F32)
    kap = pltpu.VMEM((NZ, 32, COLS), F32)
    feats = pltpu.VMEM((CHUNKS + 2, 64, COLS), F32)
    stack = pltpu.VMEM((CHUNKS, 2 * HID, LANES), BF16)
    dense = pltpu.VMEM((CHUNKS, HID, LANES), F32)
    tile = pltpu.VMEM((CHUNKS, 8, COLS), F32)
    sizes = place_sizes(lat_count, lon_count)
    plane = sizes["x"] * sizes["y_low"] * sizes["y_high"]
    pillar = sizes["core"] * sizes["z"]
    both = sum(piece_rows(plane))
    scratch = [
        pltpu.VMEM((8, HID), F32),
        pltpu.VMEM((HID, 32), BF16),
        pltpu.VMEM((16, 2 * HID), BF16),
        pltpu.VMEM((2 * HID, 2 * HID), BF16),
        pltpu.VMEM((2 * HID, 2 * HID), BF16),
        pltpu.VMEM((HID, COLS), F32),
        pltpu.VMEM((HID, COLS), F32),
        ext,
        pltpu.VMEM((4, NZ, ROWS, COLS), F32),
        ext, ext, ext, ext, kap, kap,
        pltpu.VMEM((4,) + field, F32),
        pltpu.VMEM((4,) + field, F32),
        pltpu.VMEM((4, NZ, ROWS, COLS), F32),
        pltpu.VMEM((4, NZ, ROWS, COLS), F32),
        tile, tile,
        pltpu.VMEM(field, F32),
        feats, feats,
        pltpu.VMEM((CHUNKS + 2, 8, COLS), F32),
        stack, stack, dense, dense, dense, dense, stack, stack,
        pltpu.VMEM((CHUNKS, 64, COLS), F32),
        pltpu.VMEM((CHUNKS, 64, COLS), F32),
        tile,
        pltpu.VMEM((2 * HID, 2 * HID), F32),
        pltpu.VMEM((16, 2 * HID), F32),
        pltpu.VMEM((HID, COLS), F32),
    ]
    scratch += [pltpu.VMEM((3, 2, 8, COLS), F32)] * 4
    scratch += [pltpu.VMEM((2, 16, COLS), F32)] * 2 + [pltpu.VMEM((2, 9, COLS), F32)] * 2
    scratch += [pltpu.VMEM((lon_count, 9, COLS), F32), pltpu.VMEM((3, lon_count, 8, COLS), F32)]
    scratch += [
        pltpu.VMEM((plane, both, COLS), F32),
        pltpu.VMEM((plane, both, COLS), F32),
        pltpu.VMEM((pillar, both, COLS), F32),
        pltpu.VMEM((plane, both, COLS), F32),
        pltpu.VMEM((8, COLS), F32),
        pltpu.SemaphoreType.DMA((4, 4)),
        pltpu.SemaphoreType.DMA((4, 4)),
        pltpu.SemaphoreType.DMA((4,)),
        pltpu.SemaphoreType.DMA((4,)),
        pltpu.SemaphoreType.DMA((3,)),
        pltpu.SemaphoreType.DMA((3,)),
        pltpu.SemaphoreType.DMA((10,)),
        pltpu.VMEM((ROWS, COLS), jnp.int32),
        pltpu.VMEM((ROWS, COLS), jnp.int32),
        pltpu.VMEM((1, COLS), jnp.int32),
        pltpu.VMEM((6, HID), F32),
        pltpu.VMEM((1, HID), F32),
        pltpu.VMEM((HID, HID), F32),
        pltpu.VMEM((1, HID), F32),
        pltpu.VMEM((1, HID), F32),
    ]
    vmem = pl.BlockSpec(memory_space=pltpu.VMEM)
    anywhere = pl.BlockSpec(memory_space=pl.ANY)
    run = pl.pallas_call(
        lambda *refs: kernel(lat_count, lon_count, *refs),
        out_shape=[
            pltpu.VMEM(field, F32),
            pltpu.VMEM(field, F32),
            pltpu.VMEM((6, HID), F32),
            pltpu.VMEM((HID, HID), F32),
            pltpu.VMEM((1, HID), F32),
        ],
        in_specs=[anywhere] * 10 + [pl.BlockSpec(memory_space=pltpu.SMEM)],
        out_specs=[vmem] * 5,
        scratch_shapes=scratch,
        compiler_params=pltpu.CompilerParams(
            collective_id=0, has_side_effects=True, vmem_limit_bytes=56 * 2**20
        ),
        name="adjoint_steps",
    )
    results = run(
        tracers.reshape(field), land_mask, level_counts, fold_partner.reshape(1, COLS),
        cotangent.reshape(field), w_first, b_first.reshape(1, HID), w_second,
        b_second.reshape(1, HID), w_head.reshape(1, HID), b_head,
    )
    out, grad, first, second, head = pl.pallas_call(
        hand_over,
        out_shape=[jax.ShapeDtypeStruct(r.shape, F32) for r in results],
        in_specs=[vmem] * 5,
        out_specs=[vmem] * 5,
        name="hand_over",
    )(*(pltpu.with_memory_space_constraint(r, pltpu.VMEM) for r in results))
    return (
        out.reshape(tracers.shape), grad.reshape(tracers.shape), first, second, head.reshape(HID)
    )


def solution(mesh):
    lat_count, lon_count = mesh.shape["lat"], mesh.shape["lon"]
    grid = P(None, None, "lat", "lon")
    return jax.shard_map(
        lambda *args: per_device(lat_count, lon_count, *args),
        mesh=mesh,
        in_specs=(
            grid, P("lat", "lon"), P("lat", "lon"), P("lon"), grid,
            P(), P(), P(), P(), P(), P(),
        ),
        out_specs=(grid, grid, P(), P(), P()),
        check_vma=False,
    )
```

```python
import math

import jax
import jax.numpy as jnp
from jax import lax
from jax.experimental import pallas as pl
from jax.experimental.pallas import tpu as pltpu
from jax.sharding import PartitionSpec as P

KMAX = 0.24
F32 = jnp.float32
BF16 = jnp.bfloat16
MESH = pl.DeviceIdType.MESH

NZ = 4
ROWS = 16
COLS = 128
HID = 128
FIELDS = 2 * NZ
CHUNKS = NZ * ROWS // 8
LANES = 8 * COLS
EAST, WEST, NORTH, SOUTH = 0, 1, 2, 3
HALF = NZ * ROWS
OPPOSITE = (WEST, EAST, SOUTH, NORTH)


PLANE = ("x", "y_high", "y_low")
PILLAR = ("core", "z")
RIM = ("z", "y_low")


def place_sizes(lat_count, lon_count):
    if lat_count == 16 and lon_count == 16:
        return {"core": 2, "x": 4, "y_high": 2, "y_low": 2, "z": 8}
    return {"core": 1, "x": lat_count, "y_high": 1, "y_low": 1, "z": lon_count}


def offsets(dims, sizes):
    steps = [{}]
    for d in dims:
        steps = [{**s, d: o} for s in steps for o in range(sizes[d])]

    def hops(s):
        y = {(0, 0): 0, (1, 0): 2, (0, 1): 1, (1, 1): 1}[s.get("y_high", 0), s.get("y_low", 0)]
        x, z = s.get("x", 0), s.get("z", 0)
        return y + min(x, sizes["x"] - x) + min(z, sizes["z"] - z)

    return sorted([s for s in steps if any(s.values())], key=hops, reverse=True)


def piece_rows(parts):
    return HID // parts, -(-8 // parts)


def halves(x):
    high = x.astype(BF16)
    return high, (x - high.astype(F32)).astype(BF16)


def dot(a, b):
    return jnp.dot(a, b, preferred_element_type=F32)


def product(weights, high, low):
    both = dot(weights[...], jnp.concatenate([high, low], axis=0))
    half = both.shape[0] // 2
    return both[:half] + both[half:]


def dot_nt(a, b):
    return lax.dot_general(a, b, (((1,), (1,)), ((), ())), preferred_element_type=F32)


def lane_roll(x, by):
    flat = x.reshape(-1, COLS)
    return pltpu.roll(flat, by % COLS, 1).reshape(x.shape)


def column(row):
    return jnp.broadcast_to(row, (COLS, COLS)).T


def kernel(
    lat_count, lon_count,
    tracers, land, levels, partner, cotangent, w_first, b_first, w_second, b_second, w_head, b_head,
    tracers_out, tracer_grad, gw_first, gw_second, gw_head,
    w1_rows, w1_fwd, w1_bwd, w2_fwd, w2_bwd, bias2, head,
    wet_ext, pair, state0, state1, adj0, adj1, kap0, kap1, contrast0, contrast1, coef0, coef1,
    slope0, slope1, direct, feats0, feats1, logits, h1_0, h1_1, h2_0, h2_1,
    u2_0, u2_1, u1_0, u1_1, by_feat0, by_feat1,
    obar, acc2, acc1, acch,
    beside_out, beside_in, across_out, across_in, wet_beside_out, wet_beside_in, first_out, first_in,
    fold_first, folded,
    parts, parts_plane, parts_pillar, gathered, extras,
    send_sem, recv_sem, fold_send, fold_recv, sum_send, sum_recv, in_sem,
    land_here, levels_here, partner_here, w1_here, b1_here, w2_here, b2_here, wh_here,
):
    lat = lax.axis_index("lat")
    lon = lax.axis_index("lon")
    at_top = lat == lat_count - 1
    at_bottom = lat == 0
    east = lax.rem(lon + 1, lon_count)
    west = lax.rem(lon + lon_count - 1, lon_count)

    sizes = place_sizes(lat_count, lon_count)
    core_count, x_count, y_low_count = sizes["core"], sizes["x"], sizes["y_low"]
    here = {
        "core": lax.rem(lat, core_count),
        "x": lax.rem(lax.div(lat, core_count), x_count),
        "y_high": lax.div(lat, core_count * x_count),
        "y_low": lax.rem(lon, y_low_count),
        "z": lax.div(lon, y_low_count),
    }

    def device_at(at):
        return {
            "lat": (at["y_high"] * x_count + at["x"]) * core_count + at["core"],
            "lon": at["z"] * y_low_count + at["y_low"],
        }

    def moved(offset):
        return {d: lax.rem(here[d] + offset.get(d, 0), sizes[d]) for d in here}

    def slot(dims, at):
        index = 0
        for d in dims:
            index = index * sizes[d] + at[d]
        return index

    def load(i, source, target):
        copy = pltpu.make_async_copy(source, target, in_sem.at[i])
        copy.start()
        return copy

    loads = [
        load(0, land, land_here),
        load(1, levels, levels_here),
        load(2, tracers, state0.at[:, pl.ds(8, ROWS), :]),
        load(3, cotangent, adj0.at[:, pl.ds(8, ROWS), :]),
        load(4, partner, partner_here),
        load(5, w_first, w1_here),
        load(6, b_first, b1_here),
        load(7, w_second, w2_here),
        load(8, b_second, b2_here),
        load(9, w_head, wh_here),
    ]
    barrier = pltpu.get_barrier_semaphore()

    def greet(device):
        pl.semaphore_signal(barrier, inc=1, device_id=device, device_id_type=MESH)

    @pl.when(at_top)
    def _():
        for offset in offsets(RIM, sizes):
            greet(device_at(moved(offset)))

    greeted = 4
    for dims in (PILLAR, PLANE):
        for offset in offsets(dims, sizes):
            greet(device_at(moved(offset)))
            greeted += 1
    greet({"lat": lat, "lon": east})
    greet({"lat": lat, "lon": west})
    greet({"lat": lax.rem(lat + 1, lat_count), "lon": lon})
    greet({"lat": lax.rem(lat + lat_count - 1, lat_count), "lon": lon})

    lane3 = lax.broadcasted_iota(jnp.int32, (FIELDS, ROWS, COLS), 2)
    lane8 = lax.broadcasted_iota(jnp.int32, (8, COLS), 1)
    sub8 = lax.broadcasted_iota(jnp.int32, (8, COLS), 0)

    send0 = {EAST: wet_beside_out.at[0], WEST: wet_beside_out.at[1],
             NORTH: first_out.at[0], SOUTH: first_out.at[1]}
    recv0 = {EAST: wet_beside_in.at[0], WEST: wet_beside_in.at[1],
             NORTH: first_in.at[0], SOUTH: first_in.at[1]}
    send1, send2, send3 = (
        {EAST: beside_out.at[i, 0], WEST: beside_out.at[i, 1],
         NORTH: across_out.at[i, 0], SOUTH: across_out.at[i, 1]}
        for i in range(3)
    )
    recv1, recv2, recv3 = (
        {EAST: beside_in.at[i, 0], WEST: beside_in.at[i, 1],
         NORTH: across_in.at[i, 0], SOUTH: across_in.at[i, 1]}
        for i in range(3)
    )
    fold0, fold1, fold2, fold3 = fold_first, folded.at[0], folded.at[1], folded.at[2]

    def to_side(phase, side, sends, recvs):
        target = {
            EAST: {"lat": lat, "lon": east},
            WEST: {"lat": lat, "lon": west},
            NORTH: {"lat": jnp.minimum(lat + 1, lat_count - 1), "lon": lon},
            SOUTH: {"lat": jnp.maximum(lat - 1, 0), "lon": lon},
        }[side]
        back = OPPOSITE[side]
        return pltpu.make_async_remote_copy(
            src_ref=sends[side], dst_ref=recvs[back],
            send_sem=send_sem.at[phase, side], recv_sem=recv_sem.at[phase, back],
            device_id=target, device_id_type=MESH,
        )

    def start_phase(phase, sends, recvs, folds):
        @pl.when(at_top)
        def _():
            for offset in offsets(RIM, sizes):
                pltpu.make_async_remote_copy(
                    src_ref=sends[NORTH], dst_ref=folds.at[lon],
                    send_sem=fold_send.at[phase], recv_sem=fold_recv.at[phase],
                    device_id=device_at(moved(offset)), device_id_type=MESH,
                ).start()

        to_side(phase, EAST, sends, recvs).start()
        to_side(phase, WEST, sends, recvs).start()

        @pl.when(jnp.logical_not(at_top))
        def _():
            to_side(phase, NORTH, sends, recvs).start()

        @pl.when(jnp.logical_not(at_bottom))
        def _():
            to_side(phase, SOUTH, sends, recvs).start()

        @pl.when(at_top)
        def _():
            folds[lon] = sends[NORTH][...]

    def wait_phase(phase, sends, recvs, folds):
        to_side(phase, WEST, sends, recvs).wait_recv()
        to_side(phase, EAST, sends, recvs).wait_recv()

        @pl.when(jnp.logical_not(at_top))
        def _():
            to_side(phase, SOUTH, sends, recvs).wait_recv()

        @pl.when(jnp.logical_not(at_bottom))
        def _():
            to_side(phase, NORTH, sends, recvs).wait_recv()

        @pl.when(at_top)
        def _():
            others = folds.at[pl.ds(0, lon_count - 1)]
            pltpu.make_async_copy(others, others, fold_recv.at[phase]).wait()
            block = jnp.broadcast_to(partner_here[...] >> 7, (8, COLS))
            lane = jnp.broadcast_to(partner_here[...] & (COLS - 1), (8, COLS))
            picked = jnp.zeros((8, COLS), F32)
            for j in range(lon_count):
                taken = jnp.take_along_axis(folds[j, 0:8, :], lane, axis=1)
                picked = jnp.where(block == j, taken, picked)
            recvs[NORTH][0:8, :] = picked
            if phase == 0:
                picked = jnp.zeros((8, COLS), F32)
                for j in range(lon_count):
                    counts = jnp.broadcast_to(folds[j, 8:9, :], (8, COLS))
                    taken = jnp.take_along_axis(counts, lane, axis=1)
                    picked = jnp.where(block == j, taken, picked)
                recvs[NORTH][8:9, :] = picked[0:1]

    def finish_phase(phase, sends, recvs, folds):
        to_side(phase, EAST, sends, recvs).wait_send()
        to_side(phase, WEST, sends, recvs).wait_send()

        @pl.when(jnp.logical_not(at_top))
        def _():
            to_side(phase, NORTH, sends, recvs).wait_send()

        @pl.when(jnp.logical_not(at_bottom))
        def _():
            to_side(phase, SOUTH, sends, recvs).wait_send()

        @pl.when(at_top)
        def _():
            others = folds.at[pl.ds(0, lon_count - 1)]
            pltpu.make_async_copy(others, others, fold_send.at[phase]).wait()

    def pack_beside(ext, sends, at):
        turned = ext[:, 8:24, :].reshape(COLS, COLS).T
        sends[EAST][at : at + 8, :] = turned[COLS - 8 :]
        sends[WEST][at : at + 8, :] = turned[:8]

    def pack(ext, sends):
        pack_beside(ext, sends, 0)
        sends[NORTH][0:8, :] = ext[:, 23, :]
        sends[SOUTH][0:8, :] = ext[:, 8, :]

    def unpack(ext, recvs):
        ext[:, 24, :] = recvs[NORTH][0:8, :]
        ext[:, 7, :] = recvs[SOUTH][0:8, :]

    def edge_columns(recvs, at):
        first = pltpu.roll(recvs[WEST][at : at + 8, :], 1, 0)
        last = pltpu.roll(recvs[EAST][at : at + 8, :], 7, 0)
        middle = jnp.zeros((COLS - 16, COLS), F32)
        return jnp.concatenate([first, middle, last], axis=0).T.reshape(FIELDS, ROWS, COLS)

    def sides(ext, edges):
        core = ext[:, 8:24, :]
        lane = lane3[: core.shape[0]]
        return [
            jnp.where(lane == COLS - 1, edges, lane_roll(core, -1)),
            jnp.where(lane == 0, edges, lane_roll(core, 1)),
            ext[:, 9:25, :],
            ext[:, 7:23, :],
        ]

    def store_feature(feats, chunk, f, value):
        feats[chunk, pl.ds(f, 8, stride=8), :] = value

    def own_features(ext, feats):
        for half in range(2):
            rows = pl.ds(8 + 8 * half, 8)
            wets = [wet_ext[k, rows, :] for k in range(NZ)]
            for t in range(2):
                cells = [ext[NZ * t + k, rows, :] for k in range(NZ)]
                vertical = [
                    (cells[k + 1] - cells[k]) * (wets[k + 1] * wets[k]) for k in range(NZ - 1)
                ]
                zero = jnp.zeros((8, COLS), F32)
                for k in range(NZ):
                    chunk = 2 * k + half
                    store_feature(feats, chunk, t, cells[k])
                    store_feature(feats, chunk, 2 + t, -vertical[k - 1] if k > 0 else zero)
                    store_feature(feats, chunk, 4 + t, vertical[k] if k < NZ - 1 else zero)

    def halo_features(recvs, feats):
        north, south = recvs[NORTH][0:8, :], recvs[SOUTH][0:8, :]
        first = sub8 < NZ
        depths = [jnp.broadcast_to(recv0[side][8:9, :], (8, COLS)) for side in (NORTH, SOUTH)]
        level = lax.rem(sub8, NZ).astype(F32)
        wet = (level < jnp.where(first, *depths)).astype(F32)
        joint = jnp.where(
            lax.rem(sub8, NZ) == NZ - 1, 0.0, wet * pltpu.roll(wet, 7, 0)
        )
        fields = (
            jnp.where(first, north, pltpu.roll(south, 4, 0)),
            jnp.where(first, pltpu.roll(north, 4, 0), south),
        )
        for t, cells in enumerate(fields):
            vertical = (pltpu.roll(cells, 7, 0) - cells) * joint
            store_feature(feats, CHUNKS, t, cells)
            store_feature(feats, CHUNKS, 2 + t, -pltpu.roll(vertical, 1, 0))
            store_feature(feats, CHUNKS, 4 + t, vertical)
        column_features(
            recvs[EAST][0:1, :], recvs[WEST][7:8, :], edge_wet(), feats, CHUNKS + 1
        )
        return wet

    def paired(east_row, west_row):
        east_row = jnp.broadcast_to(east_row, (8, COLS))
        west_row = jnp.broadcast_to(west_row, (8, COLS))
        first = lane8 < HALF
        return (
            jnp.where(first, east_row, pltpu.roll(west_row, HALF, 1)),
            jnp.where(first, pltpu.roll(east_row, HALF, 1), west_row),
        )

    def joint_column(wet_col):
        below = pltpu.roll(wet_col, COLS - ROWS, 1)
        return jnp.where(lax.rem(lane8, HALF) >= HALF - ROWS, 0.0, wet_col * below)

    def column_features(east_row, west_row, wet_col, feats, chunk):
        joint = joint_column(wet_col)
        for t, cells in enumerate(paired(east_row, west_row)):
            vertical = (pltpu.roll(cells, COLS - ROWS, 1) - cells) * joint
            feats[chunk, t : t + 1, :] = cells[0:1]
            feats[chunk, 2 + t : 3 + t, :] = -pltpu.roll(vertical, ROWS, 1)[0:1]
            feats[chunk, 4 + t : 5 + t, :] = vertical[0:1]

    def edge_wet():
        return paired(recv0[EAST][8:9, :], recv0[WEST][15:16, :])[0]

    def wide(x, n):
        return jnp.concatenate([x] * n, axis=1) if n > 1 else x

    def closure_chunk(feats, chunk, n, keep=None):
        f = [feats[chunk, 8 * q : 8 * q + 8, :] for q in range(n)]
        f = jnp.concatenate(f, axis=1) if n > 1 else f[0]
        high = f.astype(BF16).astype(F32)
        low = f - high
        stacked = jnp.concatenate([high, low, high, low], axis=0).astype(BF16)
        h1 = jnp.tanh(dot(w1_fwd[...], stacked))
        h1_high, h1_low = halves(h1)
        pre2 = product(w2_fwd, h1_high, h1_low)
        h2 = jnp.tanh(pre2 + wide(bias2[...], n))
        o = jnp.sum(h2 * wide(head[...], n), axis=0, keepdims=True)
        for q in range(n):
            logits[chunk, q : q + 1, :] = o[:, COLS * q : COLS * (q + 1)]
        if keep is None:
            return
        h1_ref, h2_ref, u2_ref, u1_ref, by_feat = keep
        h1_ref[chunk, :HID, :] = h1_high
        h1_ref[chunk, HID:, :] = h1_low
        h2_ref[chunk] = h2
        u2 = wide(head[...], n) * (1.0 - h2 * h2)
        u2_ref[chunk] = u2
        u2_high, u2_low = halves(u2)
        by_h1 = product(w2_bwd, u2_high, u2_low)
        u1_high, u1_low = halves(by_h1 * (1.0 - h1 * h1))
        u1_ref[chunk, :HID, :] = u1_high
        u1_ref[chunk, HID:, :] = u1_low
        d = product(w1_bwd, u1_high, u1_low)
        for q in range(n):
            by_feat[chunk, 8 * q : 8 * q + 8, :] = d[:, COLS * q : COLS * (q + 1)]

    def closure_own(feats, keep):
        @pl.loop(0, CHUNKS, unroll=CHUNKS)
        def _(chunk):
            closure_chunk(feats, chunk, 8, keep)

    def kappa_from(o, wet):
        gate = jax.nn.sigmoid(o + b_head[0])
        return KMAX * gate * wet, KMAX * gate * (1.0 - gate) * wet

    def advance(phase, state, feats, sends, recvs, folds, keep, kap, slope, contrast, coef):
        own_features(state, feats)
        closure_own(feats, keep)
        wait_phase(phase, sends, recvs, folds)
        unpack(state, recvs)
        if phase == 0:
            for k in range(NZ):
                wet_ext[k, 24:25, :] = (recvs[NORTH][8:9, :] > k).astype(F32)
                wet_ext[k, 7:8, :] = (recvs[SOUTH][8:9, :] > k).astype(F32)
            wet = wet_ext[:NZ, 8:24, :]
            around = sides(wet_ext.at[pl.ds(0, NZ)], edge_columns(recvs, 8)[:NZ])
            for n in range(4):
                pair[n] = 0.5 * wet * around[n]
        wet_halo = halo_features(recvs, feats)
        closure_chunk(feats, CHUNKS, 8)
        closure_chunk(feats, CHUNKS + 1, 1)
        for k in range(NZ):
            for half in range(2):
                rows = pl.ds(8 + 8 * half, 8)
                value, rise = kappa_from(logits[2 * k + half], wet_ext[k, rows, :])
                kap[k, rows, :] = value
                slope[2 * k + half] = rise
        value, _ = kappa_from(logits[CHUNKS], wet_halo)
        for k in range(NZ):
            kap[k, 24:25, :] = value[k : k + 1]
            kap[k, 7:8, :] = value[NZ + k : NZ + k + 1]
        value, _ = kappa_from(logits[CHUNKS + 1], edge_wet())
        same = jnp.broadcast_to(value[0:1], (8, COLS))
        middle = jnp.zeros((COLS - 16, COLS), F32)
        kap_edges = jnp.concatenate([pltpu.roll(same, NZ * ROWS, 1), middle, same], axis=0).T
        kap_sides = sides(kap, kap_edges[: NZ * ROWS].reshape(NZ, ROWS, COLS))
        tracer_sides = sides(state, edge_columns(recvs, 0))
        core = state[:, 8:24, :]
        own_kap = kap[:, 8:24, :]
        change = jnp.zeros_like(core)
        for n in range(4):
            difference = tracer_sides[n] - core
            weight = (own_kap + kap_sides[n]) * pair[n]
            contrast[n] = difference
            coef[n] = weight
            change = change + jnp.concatenate([weight, weight], 0) * difference
        return core + change

    def pull_flux(adjoint, recvs, contrast, coef, slope):
        core = adjoint[:, 8:24, :]
        around = sides(adjoint, edge_columns(recvs, 0))
        total_direct = core
        kappa_bar = jnp.zeros((NZ, ROWS, COLS), F32)
        for n in range(4):
            difference = around[n] - core
            weight = coef[n]
            total_direct = total_direct + jnp.concatenate([weight, weight], 0) * difference
            product = contrast[n] * difference
            kappa_bar = kappa_bar - pair[n] * (product[:NZ] + product[NZ:])
        direct[...] = total_direct
        obar[...] = kappa_bar.reshape(CHUNKS, 8, COLS) * slope[...]

    def add_weights(feats, keep):
        h1_ref, h2_ref, u2_ref, u1_ref, _ = keep

        @pl.loop(0, CHUNKS, unroll=CHUNKS)
        def _(chunk):
            bar = jnp.concatenate([obar[chunk, q : q + 1, :] for q in range(8)], axis=1)
            high, low = halves(u2_ref[chunk] * bar)
            acc2[...] += dot_nt(h1_ref[chunk], jnp.concatenate([high, low], axis=0))
            f = jnp.concatenate([feats[chunk, 8 * q : 8 * q + 8, :] for q in range(8)], axis=1)
            f = f * bar
            high = f.astype(BF16).astype(F32)
            stacked = jnp.concatenate([high, f - high], axis=0).astype(BF16)
            acc1[...] += dot_nt(stacked, u1_ref[chunk])
            weighted = h2_ref[chunk] * bar
            heads = weighted[:, :COLS]
            for q in range(1, 8):
                heads = heads + weighted[:, COLS * q : COLS * (q + 1)]
            acch[...] += heads

    def pull_state(by_feat, store):
        for half in range(2):
            rows = pl.ds(8 * half, 8)
            wets = [wet_ext[k, pl.ds(8 + 8 * half, 8), :] for k in range(NZ)]
            bars = [obar[2 * k + half] for k in range(NZ)]
            for t in range(2):
                bar = [
                    [by_feat[2 * k + half, pl.ds(f, 8, stride=8), :] * bars[k] for k in range(NZ)]
                    for f in (t, 2 + t, 4 + t)
                ]
                vertical = [
                    (bar[2][k] - bar[1][k + 1]) * (wets[k + 1] * wets[k]) for k in range(NZ - 1)
                ]
                for k in range(NZ):
                    value = direct[NZ * t + k, rows, :] + bar[0][k]
                    if k < NZ - 1:
                        value = value - vertical[k]
                    if k > 0:
                        value = value + vertical[k - 1]
                    store(NZ * t + k, half, value)

    loads[0].wait()
    loads[1].wait()
    depth_here = land_here[...] * levels_here[...]
    for k in range(NZ):
        wet = (k < depth_here).astype(F32)
        wet_ext[k, 8:24, :] = wet
        wet_ext[NZ + k, 8:24, :] = wet
    pack_beside(wet_ext, send0, 8)
    depths = depth_here.astype(F32)
    send0[NORTH][8:9, :] = depths[ROWS - 1 :]
    send0[SOUTH][8:9, :] = depths[0:1]
    loads[2].wait()
    pack(state0, send0)

    @pl.when(at_bottom)
    def _():
        for recvs in (recv0, recv1, recv2, recv3):
            recvs[SOUTH][...] = jnp.zeros(recvs[SOUTH].shape, F32)

    for copy in loads[3:]:
        copy.wait()

    @pl.when(jnp.logical_not(at_top))
    def _():
        pl.semaphore_wait(barrier, greeted)

    @pl.when(at_top)
    def _():
        pl.semaphore_wait(barrier, greeted + lon_count - 1)

    start_phase(0, send0, recv0, fold0)
    pack(adj0, send3)
    start_phase(3, send3, recv3, fold3)

    w1_rows[0:6, :] = w1_here[...]
    w1_rows[6:7, :] = b1_here[...]
    w1_rows[7:8, :] = jnp.zeros((1, HID), F32)
    w1 = w1_rows[...]
    w1_high = w1.astype(BF16).astype(F32)
    w1_low = w1 - w1_high
    tall = jnp.concatenate(
        [w1_high, w1_high, w1_low, w1_low, jnp.zeros((HID - 32, HID), F32)], axis=0
    )
    w1_fwd[...] = tall.T[:, :32].astype(BF16)
    blank = jnp.zeros((8, HID), F32)
    w1_bwd[...] = jnp.concatenate(
        [jnp.concatenate([w1_high, w1_low], axis=0), jnp.concatenate([w1_high, blank], axis=0)],
        axis=1,
    ).astype(BF16)
    w2 = w2_here[...]
    for target, matrix in ((w2_bwd, w2), (w2_fwd, w2.T)):
        high, low = halves(matrix)
        target[:HID, :HID] = high
        target[:HID, HID:] = high
        target[HID:, :HID] = low
        target[HID:, HID:] = jnp.zeros((HID, HID), BF16)
    bias2[...] = column(b2_here[...])
    head[...] = column(wh_here[...])
    ones_row = jnp.where(sub8 == 6, 1.0, 0.0)
    for feats in (feats0, feats1):
        for chunk in range(CHUNKS + 1):
            feats[chunk, pl.ds(6, 8, stride=8), :] = jnp.ones((8, COLS), F32)
            feats[chunk, pl.ds(7, 8, stride=8), :] = jnp.zeros((8, COLS), F32)
        feats[CHUNKS + 1, 0:8, :] = ones_row
    logits[CHUNKS + 1] = jnp.zeros((8, COLS), F32)
    acc2[...] = jnp.zeros_like(acc2)
    acc1[...] = jnp.zeros_like(acc1)
    acch[...] = jnp.zeros_like(acch)

    keep0 = (h1_0, h2_0, u2_0, u1_0, by_feat0)
    keep1 = (h1_1, h2_1, u2_1, u1_1, by_feat1)

    state1[:, 8:24, :] = advance(
        0, state0, feats0, send0, recv0, fold0, keep0, kap0, slope0, contrast0, coef0
    )
    pack(state1, send1)
    start_phase(1, send1, recv1, fold1)
    tracers_out[...] = advance(
        1, state1, feats1, send1, recv1, fold1, keep1, kap1, slope1, contrast1, coef1
    )

    wait_phase(3, send3, recv3, fold3)
    unpack(adj0, recv3)
    pull_flux(adj0, recv3, contrast1, coef1, slope1)

    def store_adjoint(i, half, value):
        adj1[i, 8 + 8 * half : 16 + 8 * half, :] = value

    pull_state(by_feat1, store_adjoint)
    pack(adj1, send2)
    start_phase(2, send2, recv2, fold2)
    add_weights(feats1, keep1)
    wait_phase(2, send2, recv2, fold2)
    unpack(adj1, recv2)
    pull_flux(adj1, recv2, contrast0, coef0, slope0)
    add_weights(feats0, keep0)

    plane = x_count * sizes["y_high"] * y_low_count
    pillar = core_count * sizes["z"]
    piece, spare = piece_rows(plane)
    second = (
        (acc2[HID:, HID:] + acc2[HID:, :HID]) + acc2[:HID, HID:]
    ) + acc2[:HID, :HID]
    first = (acc1[8:, :HID] + acc1[:8, HID:]) + acc1[:8, :HID]
    head_row = jnp.sum(acch[...].T, axis=0, keepdims=True)
    extra = jnp.where(sub8 == 6, jnp.broadcast_to(head_row, (8, COLS)), first)
    for p in range(plane):
        parts[p, :piece, :] = second[piece * p : piece * (p + 1)]
        if spare * p < 8:
            parts[p, piece:, :] = extra[spare * p : spare * (p + 1)]
        else:
            parts[p, piece:, :] = jnp.zeros((spare, COLS), F32)

    def share(dims, step, source, target):
        me = slot(dims, here)
        for offset in offsets(dims, sizes):
            there = moved(offset)
            pltpu.make_async_remote_copy(
                src_ref=source(slot(dims, there)), dst_ref=target.at[me],
                send_sem=sum_send.at[step], recv_sem=sum_recv.at[step],
                device_id=device_at(there), device_id_type=MESH,
            ).start()
        return me

    def wait_all(ref, count, sem):
        some = ref.at[pl.ds(0, count)]
        pltpu.make_async_copy(some, some, sem).wait()

    me = share(PLANE, 0, lambda there: parts.at[there], parts_plane)
    parts_plane[me] = parts[me]

    def finish(i, half, value):
        tracer_grad[i, 8 * half : 8 * half + 8, :] = value

    pull_state(by_feat0, finish)

    finish_phase(0, send0, recv0, fold0)
    finish_phase(1, send1, recv1, fold1)
    finish_phase(2, send2, recv2, fold2)
    finish_phase(3, send3, recv3, fold3)
    wait_all(parts_plane, plane - 1, sum_send.at[0])

    wait_all(parts_plane, plane - 1, sum_recv.at[0])
    summed = parts_plane[0]
    for p in range(1, plane):
        summed = summed + parts_plane[p]
    me = slot(PILLAR, here)
    parts_pillar[me] = summed
    share(PILLAR, 1, lambda there: parts_pillar.at[me], parts_pillar)
    wait_all(parts_pillar, pillar - 1, sum_send.at[1])
    wait_all(parts_pillar, pillar - 1, sum_recv.at[1])
    summed = parts_pillar[0]
    for p in range(1, pillar):
        summed = summed + parts_pillar[p]
    cells_all = lat_count * ROWS * lon_count * COLS * NZ
    me = slot(PLANE, here)
    gathered[me] = summed * (1.0 / math.sqrt(cells_all))
    share(PLANE, 2, lambda there: gathered.at[me], gathered)
    wait_all(gathered, plane - 1, sum_recv.at[2])
    for p in range(plane):
        gw_second[piece * p : piece * (p + 1), :] = gathered[p, :piece, :]
        if spare * p < 8:
            extras[spare * p : spare * (p + 1), :] = gathered[p, piece:, :]
    gw_first[...] = extras[0:6, :]
    gw_head[...] = extras[6:7, :]
    wait_all(gathered, plane - 1, sum_send.at[2])


def hand_over(*refs):
    for source, target in zip(refs[:5], refs[5:]):
        target[...] = source[...]


def per_device(lat_count, lon_count, tracers, land_mask, level_counts, fold_partner, cotangent,
               w_first, b_first, w_second, b_second, w_head, b_head):
    field = (FIELDS, ROWS, COLS)
    ext = pltpu.VMEM((FIELDS, 32, COLS), F32)
    kap = pltpu.VMEM((NZ, 32, COLS), F32)
    feats = pltpu.VMEM((CHUNKS + 2, 64, COLS), F32)
    stack = pltpu.VMEM((CHUNKS, 2 * HID, LANES), BF16)
    dense = pltpu.VMEM((CHUNKS, HID, LANES), F32)
    tile = pltpu.VMEM((CHUNKS, 8, COLS), F32)
    sizes = place_sizes(lat_count, lon_count)
    plane = sizes["x"] * sizes["y_low"] * sizes["y_high"]
    pillar = sizes["core"] * sizes["z"]
    both = sum(piece_rows(plane))
    scratch = [
        pltpu.VMEM((8, HID), F32),
        pltpu.VMEM((HID, 32), BF16),
        pltpu.VMEM((16, 2 * HID), BF16),
        pltpu.VMEM((2 * HID, 2 * HID), BF16),
        pltpu.VMEM((2 * HID, 2 * HID), BF16),
        pltpu.VMEM((HID, COLS), F32),
        pltpu.VMEM((HID, COLS), F32),
        ext,
        pltpu.VMEM((4, NZ, ROWS, COLS), F32),
        ext, ext, ext, ext, kap, kap,
        pltpu.VMEM((4,) + field, F32),
        pltpu.VMEM((4,) + field, F32),
        pltpu.VMEM((4, NZ, ROWS, COLS), F32),
        pltpu.VMEM((4, NZ, ROWS, COLS), F32),
        tile, tile,
        pltpu.VMEM(field, F32),
        feats, feats,
        pltpu.VMEM((CHUNKS + 2, 8, COLS), F32),
        stack, stack, dense, dense, dense, dense, stack, stack,
        pltpu.VMEM((CHUNKS, 64, COLS), F32),
        pltpu.VMEM((CHUNKS, 64, COLS), F32),
        tile,
        pltpu.VMEM((2 * HID, 2 * HID), F32),
        pltpu.VMEM((16, 2 * HID), F32),
        pltpu.VMEM((HID, COLS), F32),
    ]
    scratch += [pltpu.VMEM((3, 2, 8, COLS), F32)] * 4
    scratch += [pltpu.VMEM((2, 16, COLS), F32)] * 2 + [pltpu.VMEM((2, 9, COLS), F32)] * 2
    scratch += [pltpu.VMEM((lon_count, 9, COLS), F32), pltpu.VMEM((3, lon_count, 8, COLS), F32)]
    scratch += [
        pltpu.VMEM((plane, both, COLS), F32),
        pltpu.VMEM((plane, both, COLS), F32),
        pltpu.VMEM((pillar, both, COLS), F32),
        pltpu.VMEM((plane, both, COLS), F32),
        pltpu.VMEM((8, COLS), F32),
        pltpu.SemaphoreType.DMA((4, 4)),
        pltpu.SemaphoreType.DMA((4, 4)),
        pltpu.SemaphoreType.DMA((4,)),
        pltpu.SemaphoreType.DMA((4,)),
        pltpu.SemaphoreType.DMA((3,)),
        pltpu.SemaphoreType.DMA((3,)),
        pltpu.SemaphoreType.DMA((10,)),
        pltpu.VMEM((ROWS, COLS), jnp.int32),
        pltpu.VMEM((ROWS, COLS), jnp.int32),
        pltpu.VMEM((1, COLS), jnp.int32),
        pltpu.VMEM((6, HID), F32),
        pltpu.VMEM((1, HID), F32),
        pltpu.VMEM((HID, HID), F32),
        pltpu.VMEM((1, HID), F32),
        pltpu.VMEM((1, HID), F32),
    ]
    vmem = pl.BlockSpec(memory_space=pltpu.VMEM)
    anywhere = pl.BlockSpec(memory_space=pl.ANY)
    run = pl.pallas_call(
        lambda *refs: kernel(lat_count, lon_count, *refs),
        out_shape=[
            pltpu.VMEM(field, F32),
            pltpu.VMEM(field, F32),
            pltpu.VMEM((6, HID), F32),
            pltpu.VMEM((HID, HID), F32),
            pltpu.VMEM((1, HID), F32),
        ],
        in_specs=[anywhere] * 10 + [pl.BlockSpec(memory_space=pltpu.SMEM)],
        out_specs=[vmem] * 5,
        scratch_shapes=scratch,
        compiler_params=pltpu.CompilerParams(
            collective_id=0, has_side_effects=True, vmem_limit_bytes=56 * 2**20
        ),
        name="adjoint_steps",
    )
    results = run(
        tracers.reshape(field), land_mask, level_counts, fold_partner.reshape(1, COLS),
        cotangent.reshape(field), w_first, b_first.reshape(1, HID), w_second,
        b_second.reshape(1, HID), w_head.reshape(1, HID), b_head,
    )
    out, grad, first, second, head = pl.pallas_call(
        hand_over,
        out_shape=[jax.ShapeDtypeStruct(r.shape, F32) for r in results],
        in_specs=[vmem] * 5,
        out_specs=[vmem] * 5,
        name="hand_over",
    )(*(pltpu.with_memory_space_constraint(r, pltpu.VMEM) for r in results))
    return (
        out.reshape(tracers.shape), grad.reshape(tracers.shape), first, second, head.reshape(HID)
    )


def solution(mesh):
    lat_count, lon_count = mesh.shape["lat"], mesh.shape["lon"]
    grid = P(None, None, "lat", "lon")
    return jax.shard_map(
        lambda *args: per_device(lat_count, lon_count, *args),
        mesh=mesh,
        in_specs=(
            grid, P("lat", "lon"), P("lat", "lon"), P("lon"), grid,
            P(), P(), P(), P(), P(), P(),
        ),
        out_specs=(grid, grid, P(), P(), P()),
        check_vma=False,
    )
```

```python
import math

import jax
import jax.numpy as jnp
from jax import lax
from jax.experimental import pallas as pl
from jax.experimental.pallas import tpu as pltpu
from jax.sharding import PartitionSpec as P

KMAX = 0.24
F32 = jnp.float32
BF16 = jnp.bfloat16
MESH = pl.DeviceIdType.MESH

NZ = 4
ROWS = 16
COLS = 128
HID = 128
FIELDS = 2 * NZ
CHUNKS = NZ * ROWS // 8
LANES = 8 * COLS
EAST, WEST, NORTH, SOUTH = 0, 1, 2, 3
HALF = NZ * ROWS
OPPOSITE = (WEST, EAST, SOUTH, NORTH)


PLANE = ("x", "y_high", "y_low")
PILLAR = ("core", "z")
RIM = ("z", "y_low")


def place_sizes(lat_count, lon_count):
    if lat_count == 16 and lon_count == 16:
        return {"core": 2, "x": 4, "y_high": 2, "y_low": 2, "z": 8}
    return {"core": 1, "x": lat_count, "y_high": 1, "y_low": 1, "z": lon_count}


def offsets(dims, sizes):
    steps = [{}]
    for d in dims:
        steps = [{**s, d: o} for s in steps for o in range(sizes[d])]

    def hops(s):
        y = {(0, 0): 0, (1, 0): 2, (0, 1): 1, (1, 1): 1}[s.get("y_high", 0), s.get("y_low", 0)]
        x, z = s.get("x", 0), s.get("z", 0)
        return y + min(x, sizes["x"] - x) + min(z, sizes["z"] - z)

    return sorted([s for s in steps if any(s.values())], key=hops, reverse=True)


def piece_rows(parts):
    return HID // parts, -(-8 // parts)


def halves(x):
    high = x.astype(BF16)
    return high, (x - high.astype(F32)).astype(BF16)


def dot(a, b):
    return jnp.dot(a, b, preferred_element_type=F32)


def product(weights, high, low):
    both = dot(weights[...], jnp.concatenate([high, low], axis=0))
    half = both.shape[0] // 2
    return both[:half] + both[half:]


def dot_nt(a, b):
    return lax.dot_general(a, b, (((1,), (1,)), ((), ())), preferred_element_type=F32)


def lane_roll(x, by):
    flat = x.reshape(-1, COLS)
    return pltpu.roll(flat, by % COLS, 1).reshape(x.shape)


def column(row):
    return jnp.broadcast_to(row, (COLS, COLS)).T


def kernel(
    lat_count, lon_count,
    tracers, land, levels, partner, cotangent, w_first, b_first, w_second, b_second, w_head, b_head,
    tracers_out, tracer_grad, gw_first, gw_second, gw_head,
    w1_rows, w1_fwd, w1_bwd, w2_fwd, w2_bwd, bias2, head,
    wet_ext, pair, state0, state1, adj0, adj1, kap0, kap1, contrast0, contrast1, coef0, coef1,
    slope0, slope1, direct, feats0, feats1, logits, h1_0, h1_1, h2_0, h2_1,
    u2_0, u2_1, u1_0, u1_1, by_feat0, by_feat1,
    obar, acc2, acc1, acch,
    beside_out, beside_in, across_out, across_in, wet_beside_out, wet_beside_in, first_out, first_in,
    fold_first, folded,
    parts, parts_plane, parts_pillar, gathered, extras,
    send_sem, recv_sem, fold_send, fold_recv, sum_send, sum_recv, in_sem,
    land_here, levels_here, partner_here, w1_here, b1_here, w2_here, b2_here, wh_here,
):
    lat = lax.axis_index("lat")
    lon = lax.axis_index("lon")
    at_top = lat == lat_count - 1
    at_bottom = lat == 0
    east = lax.rem(lon + 1, lon_count)
    west = lax.rem(lon + lon_count - 1, lon_count)

    sizes = place_sizes(lat_count, lon_count)
    core_count, x_count, y_low_count = sizes["core"], sizes["x"], sizes["y_low"]
    here = {
        "core": lax.rem(lat, core_count),
        "x": lax.rem(lax.div(lat, core_count), x_count),
        "y_high": lax.div(lat, core_count * x_count),
        "y_low": lax.rem(lon, y_low_count),
        "z": lax.div(lon, y_low_count),
    }

    def device_at(at):
        return {
            "lat": (at["y_high"] * x_count + at["x"]) * core_count + at["core"],
            "lon": at["z"] * y_low_count + at["y_low"],
        }

    def moved(offset):
        return {d: lax.rem(here[d] + offset.get(d, 0), sizes[d]) for d in here}

    def slot(dims, at):
        index = 0
        for d in dims:
            index = index * sizes[d] + at[d]
        return index

    def load(i, source, target):
        copy = pltpu.make_async_copy(source, target, in_sem.at[i])
        copy.start()
        return copy

    loads = [
        load(0, land, land_here),
        load(1, levels, levels_here),
        load(2, tracers, state0.at[:, pl.ds(8, ROWS), :]),
        load(3, cotangent, adj0.at[:, pl.ds(8, ROWS), :]),
        load(4, partner, partner_here),
        load(5, w_first, w1_here),
        load(6, b_first, b1_here),
        load(7, w_second, w2_here),
        load(8, b_second, b2_here),
        load(9, w_head, wh_here),
    ]
    barrier = pltpu.get_barrier_semaphore()

    def greet(device):
        pl.semaphore_signal(barrier, inc=1, device_id=device, device_id_type=MESH)

    @pl.when(at_top)
    def _():
        for offset in offsets(RIM, sizes):
            greet(device_at(moved(offset)))

    greeted = 4
    for dims in (PILLAR, PLANE):
        for offset in offsets(dims, sizes):
            greet(device_at(moved(offset)))
            greeted += 1
    greet({"lat": lat, "lon": east})
    greet({"lat": lat, "lon": west})
    greet({"lat": lax.rem(lat + 1, lat_count), "lon": lon})
    greet({"lat": lax.rem(lat + lat_count - 1, lat_count), "lon": lon})

    lane3 = lax.broadcasted_iota(jnp.int32, (FIELDS, ROWS, COLS), 2)
    lane8 = lax.broadcasted_iota(jnp.int32, (8, COLS), 1)
    sub8 = lax.broadcasted_iota(jnp.int32, (8, COLS), 0)

    send0 = {EAST: wet_beside_out.at[0], WEST: wet_beside_out.at[1],
             NORTH: first_out.at[0], SOUTH: first_out.at[1]}
    recv0 = {EAST: wet_beside_in.at[0], WEST: wet_beside_in.at[1],
             NORTH: first_in.at[0], SOUTH: first_in.at[1]}
    send1, send2, send3 = (
        {EAST: beside_out.at[i, 0], WEST: beside_out.at[i, 1],
         NORTH: across_out.at[i, 0], SOUTH: across_out.at[i, 1]}
        for i in range(3)
    )
    recv1, recv2, recv3 = (
        {EAST: beside_in.at[i, 0], WEST: beside_in.at[i, 1],
         NORTH: across_in.at[i, 0], SOUTH: across_in.at[i, 1]}
        for i in range(3)
    )
    fold0, fold1, fold2, fold3 = fold_first, folded.at[0], folded.at[1], folded.at[2]

    def to_side(phase, side, sends, recvs):
        target = {
            EAST: {"lat": lat, "lon": east},
            WEST: {"lat": lat, "lon": west},
            NORTH: {"lat": jnp.minimum(lat + 1, lat_count - 1), "lon": lon},
            SOUTH: {"lat": jnp.maximum(lat - 1, 0), "lon": lon},
        }[side]
        back = OPPOSITE[side]
        return pltpu.make_async_remote_copy(
            src_ref=sends[side], dst_ref=recvs[back],
            send_sem=send_sem.at[phase, side], recv_sem=recv_sem.at[phase, back],
            device_id=target, device_id_type=MESH,
        )

    def start_phase(phase, sends, recvs, folds):
        @pl.when(at_top)
        def _():
            for offset in offsets(RIM, sizes):
                pltpu.make_async_remote_copy(
                    src_ref=sends[NORTH], dst_ref=folds.at[lon],
                    send_sem=fold_send.at[phase], recv_sem=fold_recv.at[phase],
                    device_id=device_at(moved(offset)), device_id_type=MESH,
                ).start()

        to_side(phase, EAST, sends, recvs).start()
        to_side(phase, WEST, sends, recvs).start()

        @pl.when(jnp.logical_not(at_top))
        def _():
            to_side(phase, NORTH, sends, recvs).start()

        @pl.when(jnp.logical_not(at_bottom))
        def _():
            to_side(phase, SOUTH, sends, recvs).start()

        @pl.when(at_top)
        def _():
            folds[lon] = sends[NORTH][...]

    def wait_phase(phase, sends, recvs, folds):
        to_side(phase, WEST, sends, recvs).wait_recv()
        to_side(phase, EAST, sends, recvs).wait_recv()

        @pl.when(jnp.logical_not(at_top))
        def _():
            to_side(phase, SOUTH, sends, recvs).wait_recv()

        @pl.when(jnp.logical_not(at_bottom))
        def _():
            to_side(phase, NORTH, sends, recvs).wait_recv()

        @pl.when(at_top)
        def _():
            others = folds.at[pl.ds(0, lon_count - 1)]
            pltpu.make_async_copy(others, others, fold_recv.at[phase]).wait()
            block = jnp.broadcast_to(partner_here[...] >> 7, (8, COLS))
            lane = jnp.broadcast_to(partner_here[...] & (COLS - 1), (8, COLS))
            picked = jnp.zeros((8, COLS), F32)
            for j in range(lon_count):
                taken = jnp.take_along_axis(folds[j, 0:8, :], lane, axis=1)
                picked = jnp.where(block == j, taken, picked)
            recvs[NORTH][0:8, :] = picked
            if phase == 0:
                picked = jnp.zeros((8, COLS), F32)
                for j in range(lon_count):
                    counts = jnp.broadcast_to(folds[j, 8:9, :], (8, COLS))
                    taken = jnp.take_along_axis(counts, lane, axis=1)
                    picked = jnp.where(block == j, taken, picked)
                recvs[NORTH][8:9, :] = picked[0:1]

    def finish_phase(phase, sends, recvs, folds):
        to_side(phase, EAST, sends, recvs).wait_send()
        to_side(phase, WEST, sends, recvs).wait_send()

        @pl.when(jnp.logical_not(at_top))
        def _():
            to_side(phase, NORTH, sends, recvs).wait_send()

        @pl.when(jnp.logical_not(at_bottom))
        def _():
            to_side(phase, SOUTH, sends, recvs).wait_send()

        @pl.when(at_top)
        def _():
            others = folds.at[pl.ds(0, lon_count - 1)]
            pltpu.make_async_copy(others, others, fold_send.at[phase]).wait()

    def pack_beside(ext, sends, at):
        turned = ext[:, 8:24, :].reshape(COLS, COLS).T
        sends[EAST][at : at + 8, :] = turned[COLS - 8 :]
        sends[WEST][at : at + 8, :] = turned[:8]

    def pack(ext, sends):
        pack_beside(ext, sends, 0)
        sends[NORTH][0:8, :] = ext[:, 23, :]
        sends[SOUTH][0:8, :] = ext[:, 8, :]

    def unpack(ext, recvs):
        ext[:, 24, :] = recvs[NORTH][0:8, :]
        ext[:, 7, :] = recvs[SOUTH][0:8, :]

    def edge_columns(recvs, at):
        first = pltpu.roll(recvs[WEST][at : at + 8, :], 1, 0)
        last = pltpu.roll(recvs[EAST][at : at + 8, :], 7, 0)
        middle = jnp.zeros((COLS - 16, COLS), F32)
        return jnp.concatenate([first, middle, last], axis=0).T.reshape(FIELDS, ROWS, COLS)

    def sides(ext, edges):
        core = ext[:, 8:24, :]
        lane = lane3[: core.shape[0]]
        return [
            jnp.where(lane == COLS - 1, edges, lane_roll(core, -1)),
            jnp.where(lane == 0, edges, lane_roll(core, 1)),
            ext[:, 9:25, :],
            ext[:, 7:23, :],
        ]

    def store_feature(feats, chunk, f, value):
        feats[chunk, pl.ds(f, 8, stride=8), :] = value

    def own_features(ext, feats):
        for half in range(2):
            rows = pl.ds(8 + 8 * half, 8)
            wets = [wet_ext[k, rows, :] for k in range(NZ)]
            for t in range(2):
                cells = [ext[NZ * t + k, rows, :] for k in range(NZ)]
                vertical = [
                    (cells[k + 1] - cells[k]) * (wets[k + 1] * wets[k]) for k in range(NZ - 1)
                ]
                zero = jnp.zeros((8, COLS), F32)
                for k in range(NZ):
                    chunk = 2 * k + half
                    store_feature(feats, chunk, t, cells[k])
                    store_feature(feats, chunk, 2 + t, -vertical[k - 1] if k > 0 else zero)
                    store_feature(feats, chunk, 4 + t, vertical[k] if k < NZ - 1 else zero)

    def halo_features(recvs, feats):
        north, south = recvs[NORTH][0:8, :], recvs[SOUTH][0:8, :]
        first = sub8 < NZ
        depths = [jnp.broadcast_to(recv0[side][8:9, :], (8, COLS)) for side in (NORTH, SOUTH)]
        level = lax.rem(sub8, NZ).astype(F32)
        wet = (level < jnp.where(first, *depths)).astype(F32)
        joint = jnp.where(
            lax.rem(sub8, NZ) == NZ - 1, 0.0, wet * pltpu.roll(wet, 7, 0)
        )
        fields = (
            jnp.where(first, north, pltpu.roll(south, 4, 0)),
            jnp.where(first, pltpu.roll(north, 4, 0), south),
        )
        for t, cells in enumerate(fields):
            vertical = (pltpu.roll(cells, 7, 0) - cells) * joint
            store_feature(feats, CHUNKS, t, cells)
            store_feature(feats, CHUNKS, 2 + t, -pltpu.roll(vertical, 1, 0))
            store_feature(feats, CHUNKS, 4 + t, vertical)
        column_features(
            recvs[EAST][0:1, :], recvs[WEST][7:8, :], edge_wet(), feats, CHUNKS + 1
        )
        return wet

    def paired(east_row, west_row):
        east_row = jnp.broadcast_to(east_row, (8, COLS))
        west_row = jnp.broadcast_to(west_row, (8, COLS))
        first = lane8 < HALF
        return (
            jnp.where(first, east_row, pltpu.roll(west_row, HALF, 1)),
            jnp.where(first, pltpu.roll(east_row, HALF, 1), west_row),
        )

    def joint_column(wet_col):
        below = pltpu.roll(wet_col, COLS - ROWS, 1)
        return jnp.where(lax.rem(lane8, HALF) >= HALF - ROWS, 0.0, wet_col * below)

    def column_features(east_row, west_row, wet_col, feats, chunk):
        joint = joint_column(wet_col)
        for t, cells in enumerate(paired(east_row, west_row)):
            vertical = (pltpu.roll(cells, COLS - ROWS, 1) - cells) * joint
            feats[chunk, t : t + 1, :] = cells[0:1]
            feats[chunk, 2 + t : 3 + t, :] = -pltpu.roll(vertical, ROWS, 1)[0:1]
            feats[chunk, 4 + t : 5 + t, :] = vertical[0:1]

    def edge_wet():
        return paired(recv0[EAST][8:9, :], recv0[WEST][15:16, :])[0]

    def wide(x, n):
        return jnp.concatenate([x] * n, axis=1) if n > 1 else x

    def closure_chunk(feats, chunk, n, keep=None):
        f = [feats[chunk + q // 8, 8 * (q % 8) : 8 * (q % 8) + 8, :] for q in range(n)]
        f = jnp.concatenate(f, axis=1) if n > 1 else f[0]
        high = f.astype(BF16).astype(F32)
        low = f - high
        stacked = jnp.concatenate([high, low, high, low], axis=0).astype(BF16)
        h1 = jnp.tanh(dot(w1_fwd[...], stacked))
        h1_high, h1_low = halves(h1)
        pre2 = product(w2_fwd, h1_high, h1_low)
        h2 = jnp.tanh(pre2 + wide(bias2[...], n))
        o = jnp.sum(h2 * wide(head[...], n), axis=0, keepdims=True)
        for q in range(n):
            logits[chunk + q // 8, q % 8 : q % 8 + 1, :] = o[:, COLS * q : COLS * (q + 1)]
        if keep is None:
            return
        h1_ref, h2_ref, u2_ref, u1_ref, by_feat = keep
        parts_of = [slice(LANES * i, LANES * (i + 1)) for i in range(n // 8)]
        for i, lanes in enumerate(parts_of):
            h1_ref[chunk + i, :HID, :] = h1_high[:, lanes]
            h1_ref[chunk + i, HID:, :] = h1_low[:, lanes]
            h2_ref[chunk + i] = h2[:, lanes]
        u2 = wide(head[...], n) * (1.0 - h2 * h2)
        for i, lanes in enumerate(parts_of):
            u2_ref[chunk + i] = u2[:, lanes]
        u2_high, u2_low = halves(u2)
        by_h1 = product(w2_bwd, u2_high, u2_low)
        u1_high, u1_low = halves(by_h1 * (1.0 - h1 * h1))
        for i, lanes in enumerate(parts_of):
            u1_ref[chunk + i, :HID, :] = u1_high[:, lanes]
            u1_ref[chunk + i, HID:, :] = u1_low[:, lanes]
        d = product(w1_bwd, u1_high, u1_low)
        for q in range(n):
            rows = slice(8 * (q % 8), 8 * (q % 8) + 8)
            by_feat[chunk + q // 8, rows, :] = d[:, COLS * q : COLS * (q + 1)]

    def closure_own(feats, keep):
        for chunk in range(0, CHUNKS, 2):
            closure_chunk(feats, chunk, 16, keep)

    def kappa_from(o, wet):
        gate = jax.nn.sigmoid(o + b_head[0])
        return KMAX * gate * wet, KMAX * gate * (1.0 - gate) * wet

    def advance(phase, state, feats, sends, recvs, folds, keep, kap, slope, contrast, coef):
        own_features(state, feats)
        closure_own(feats, keep)
        wait_phase(phase, sends, recvs, folds)
        unpack(state, recvs)
        if phase == 0:
            for k in range(NZ):
                wet_ext[k, 24:25, :] = (recvs[NORTH][8:9, :] > k).astype(F32)
                wet_ext[k, 7:8, :] = (recvs[SOUTH][8:9, :] > k).astype(F32)
            wet = wet_ext[:NZ, 8:24, :]
            around = sides(wet_ext.at[pl.ds(0, NZ)], edge_columns(recvs, 8)[:NZ])
            for n in range(4):
                pair[n] = 0.5 * wet * around[n]
        wet_halo = halo_features(recvs, feats)
        closure_chunk(feats, CHUNKS, 8)
        closure_chunk(feats, CHUNKS + 1, 1)
        for k in range(NZ):
            for half in range(2):
                rows = pl.ds(8 + 8 * half, 8)
                value, rise = kappa_from(logits[2 * k + half], wet_ext[k, rows, :])
                kap[k, rows, :] = value
                slope[2 * k + half] = rise
        value, _ = kappa_from(logits[CHUNKS], wet_halo)
        for k in range(NZ):
            kap[k, 24:25, :] = value[k : k + 1]
            kap[k, 7:8, :] = value[NZ + k : NZ + k + 1]
        value, _ = kappa_from(logits[CHUNKS + 1], edge_wet())
        same = jnp.broadcast_to(value[0:1], (8, COLS))
        middle = jnp.zeros((COLS - 16, COLS), F32)
        kap_edges = jnp.concatenate([pltpu.roll(same, NZ * ROWS, 1), middle, same], axis=0).T
        kap_sides = sides(kap, kap_edges[: NZ * ROWS].reshape(NZ, ROWS, COLS))
        tracer_sides = sides(state, edge_columns(recvs, 0))
        core = state[:, 8:24, :]
        own_kap = kap[:, 8:24, :]
        change = jnp.zeros_like(core)
        for n in range(4):
            difference = tracer_sides[n] - core
            weight = (own_kap + kap_sides[n]) * pair[n]
            contrast[n] = difference
            coef[n] = weight
            change = change + jnp.concatenate([weight, weight], 0) * difference
        return core + change

    def pull_flux(adjoint, recvs, contrast, coef, slope):
        core = adjoint[:, 8:24, :]
        around = sides(adjoint, edge_columns(recvs, 0))
        total_direct = core
        kappa_bar = jnp.zeros((NZ, ROWS, COLS), F32)
        for n in range(4):
            difference = around[n] - core
            weight = coef[n]
            total_direct = total_direct + jnp.concatenate([weight, weight], 0) * difference
            product = contrast[n] * difference
            kappa_bar = kappa_bar - pair[n] * (product[:NZ] + product[NZ:])
        direct[...] = total_direct
        obar[...] = kappa_bar.reshape(CHUNKS, 8, COLS) * slope[...]

    def add_weights(feats, keep):
        h1_ref, h2_ref, u2_ref, u1_ref, _ = keep

        for first in range(0, CHUNKS, 2):
            pair_of = (first, first + 1)
            bars = [
                jnp.concatenate([obar[c, q : q + 1, :] for q in range(8)], axis=1) for c in pair_of
            ]
            split = [halves(u2_ref[c] * bar) for c, bar in zip(pair_of, bars)]
            beside = [jnp.concatenate(x, axis=0) for x in split]
            h1 = jnp.concatenate([h1_ref[c] for c in pair_of], axis=1)
            acc2[...] += dot_nt(h1, jnp.concatenate(beside, axis=1))
            f = [feats[c, 8 * q : 8 * q + 8, :] for c in pair_of for q in range(8)]
            f = jnp.concatenate(f, axis=1) * jnp.concatenate(bars, axis=1)
            high = f.astype(BF16).astype(F32)
            stacked = jnp.concatenate([high, f - high], axis=0).astype(BF16)
            acc1[...] += dot_nt(stacked, jnp.concatenate([u1_ref[c] for c in pair_of], axis=1))
            weighted = [h2_ref[c] * bar for c, bar in zip(pair_of, bars)]
            heads = weighted[0][:, :COLS] + weighted[1][:, :COLS]
            for q in range(1, 8):
                lanes = slice(COLS * q, COLS * (q + 1))
                heads = heads + (weighted[0][:, lanes] + weighted[1][:, lanes])
            acch[...] += heads

    def pull_state(by_feat, store):
        for half in range(2):
            rows = pl.ds(8 * half, 8)
            wets = [wet_ext[k, pl.ds(8 + 8 * half, 8), :] for k in range(NZ)]
            bars = [obar[2 * k + half] for k in range(NZ)]
            for t in range(2):
                bar = [
                    [by_feat[2 * k + half, pl.ds(f, 8, stride=8), :] * bars[k] for k in range(NZ)]
                    for f in (t, 2 + t, 4 + t)
                ]
                vertical = [
                    (bar[2][k] - bar[1][k + 1]) * (wets[k + 1] * wets[k]) for k in range(NZ - 1)
                ]
                for k in range(NZ):
                    value = direct[NZ * t + k, rows, :] + bar[0][k]
                    if k < NZ - 1:
                        value = value - vertical[k]
                    if k > 0:
                        value = value + vertical[k - 1]
                    store(NZ * t + k, half, value)

    loads[0].wait()
    loads[1].wait()
    depth_here = land_here[...] * levels_here[...]
    for k in range(NZ):
        wet = (k < depth_here).astype(F32)
        wet_ext[k, 8:24, :] = wet
        wet_ext[NZ + k, 8:24, :] = wet
    pack_beside(wet_ext, send0, 8)
    depths = depth_here.astype(F32)
    send0[NORTH][8:9, :] = depths[ROWS - 1 :]
    send0[SOUTH][8:9, :] = depths[0:1]
    loads[2].wait()
    pack(state0, send0)

    @pl.when(at_bottom)
    def _():
        for recvs in (recv0, recv1, recv2, recv3):
            recvs[SOUTH][...] = jnp.zeros(recvs[SOUTH].shape, F32)

    for copy in loads[3:]:
        copy.wait()

    @pl.when(jnp.logical_not(at_top))
    def _():
        pl.semaphore_wait(barrier, greeted)

    @pl.when(at_top)
    def _():
        pl.semaphore_wait(barrier, greeted + lon_count - 1)

    start_phase(0, send0, recv0, fold0)
    pack(adj0, send3)
    start_phase(3, send3, recv3, fold3)

    w1_rows[0:6, :] = w1_here[...]
    w1_rows[6:7, :] = b1_here[...]
    w1_rows[7:8, :] = jnp.zeros((1, HID), F32)
    w1 = w1_rows[...]
    w1_high = w1.astype(BF16).astype(F32)
    w1_low = w1 - w1_high
    tall = jnp.concatenate(
        [w1_high, w1_high, w1_low, w1_low, jnp.zeros((HID - 32, HID), F32)], axis=0
    )
    w1_fwd[...] = tall.T[:, :32].astype(BF16)
    blank = jnp.zeros((8, HID), F32)
    w1_bwd[...] = jnp.concatenate(
        [jnp.concatenate([w1_high, w1_low], axis=0), jnp.concatenate([w1_high, blank], axis=0)],
        axis=1,
    ).astype(BF16)
    w2 = w2_here[...]
    for target, matrix in ((w2_bwd, w2), (w2_fwd, w2.T)):
        high, low = halves(matrix)
        target[:HID, :HID] = high
        target[:HID, HID:] = high
        target[HID:, :HID] = low
        target[HID:, HID:] = jnp.zeros((HID, HID), BF16)
    bias2[...] = column(b2_here[...])
    head[...] = column(wh_here[...])
    ones_row = jnp.where(sub8 == 6, 1.0, 0.0)
    for feats in (feats0, feats1):
        for chunk in range(CHUNKS + 1):
            feats[chunk, pl.ds(6, 8, stride=8), :] = jnp.ones((8, COLS), F32)
            feats[chunk, pl.ds(7, 8, stride=8), :] = jnp.zeros((8, COLS), F32)
        feats[CHUNKS + 1, 0:8, :] = ones_row
    logits[CHUNKS + 1] = jnp.zeros((8, COLS), F32)
    acc2[...] = jnp.zeros_like(acc2)
    acc1[...] = jnp.zeros_like(acc1)
    acch[...] = jnp.zeros_like(acch)

    keep0 = (h1_0, h2_0, u2_0, u1_0, by_feat0)
    keep1 = (h1_1, h2_1, u2_1, u1_1, by_feat1)

    state1[:, 8:24, :] = advance(
        0, state0, feats0, send0, recv0, fold0, keep0, kap0, slope0, contrast0, coef0
    )
    pack(state1, send1)
    start_phase(1, send1, recv1, fold1)
    tracers_out[...] = advance(
        1, state1, feats1, send1, recv1, fold1, keep1, kap1, slope1, contrast1, coef1
    )

    wait_phase(3, send3, recv3, fold3)
    unpack(adj0, recv3)
    pull_flux(adj0, recv3, contrast1, coef1, slope1)

    def store_adjoint(i, half, value):
        adj1[i, 8 + 8 * half : 16 + 8 * half, :] = value

    pull_state(by_feat1, store_adjoint)
    pack(adj1, send2)
    start_phase(2, send2, recv2, fold2)
    add_weights(feats1, keep1)
    wait_phase(2, send2, recv2, fold2)
    unpack(adj1, recv2)
    pull_flux(adj1, recv2, contrast0, coef0, slope0)
    add_weights(feats0, keep0)

    plane = x_count * sizes["y_high"] * y_low_count
    pillar = core_count * sizes["z"]
    piece, spare = piece_rows(plane)
    second = (
        (acc2[HID:, HID:] + acc2[HID:, :HID]) + acc2[:HID, HID:]
    ) + acc2[:HID, :HID]
    first = (acc1[8:, :HID] + acc1[:8, HID:]) + acc1[:8, :HID]
    head_row = jnp.sum(acch[...].T, axis=0, keepdims=True)
    extra = jnp.where(sub8 == 6, jnp.broadcast_to(head_row, (8, COLS)), first)
    for p in range(plane):
        parts[p, :piece, :] = second[piece * p : piece * (p + 1)]
        if spare * p < 8:
            parts[p, piece:, :] = extra[spare * p : spare * (p + 1)]
        else:
            parts[p, piece:, :] = jnp.zeros((spare, COLS), F32)

    def share(dims, step, source, target):
        me = slot(dims, here)
        for offset in offsets(dims, sizes):
            there = moved(offset)
            pltpu.make_async_remote_copy(
                src_ref=source(slot(dims, there)), dst_ref=target.at[me],
                send_sem=sum_send.at[step], recv_sem=sum_recv.at[step],
                device_id=device_at(there), device_id_type=MESH,
            ).start()
        return me

    def wait_all(ref, count, sem):
        some = ref.at[pl.ds(0, count)]
        pltpu.make_async_copy(some, some, sem).wait()

    me = share(PLANE, 0, lambda there: parts.at[there], parts_plane)
    parts_plane[me] = parts[me]

    def finish(i, half, value):
        tracer_grad[i, 8 * half : 8 * half + 8, :] = value

    pull_state(by_feat0, finish)

    finish_phase(0, send0, recv0, fold0)
    finish_phase(1, send1, recv1, fold1)
    finish_phase(2, send2, recv2, fold2)
    finish_phase(3, send3, recv3, fold3)
    wait_all(parts_plane, plane - 1, sum_send.at[0])

    wait_all(parts_plane, plane - 1, sum_recv.at[0])
    summed = parts_plane[0]
    for p in range(1, plane):
        summed = summed + parts_plane[p]
    me = slot(PILLAR, here)
    parts_pillar[me] = summed
    share(PILLAR, 1, lambda there: parts_pillar.at[me], parts_pillar)
    wait_all(parts_pillar, pillar - 1, sum_send.at[1])
    wait_all(parts_pillar, pillar - 1, sum_recv.at[1])
    summed = parts_pillar[0]
    for p in range(1, pillar):
        summed = summed + parts_pillar[p]
    cells_all = lat_count * ROWS * lon_count * COLS * NZ
    me = slot(PLANE, here)
    gathered[me] = summed * (1.0 / math.sqrt(cells_all))
    share(PLANE, 2, lambda there: gathered.at[me], gathered)
    wait_all(gathered, plane - 1, sum_recv.at[2])
    for p in range(plane):
        gw_second[piece * p : piece * (p + 1), :] = gathered[p, :piece, :]
        if spare * p < 8:
            extras[spare * p : spare * (p + 1), :] = gathered[p, piece:, :]
    gw_first[...] = extras[0:6, :]
    gw_head[...] = extras[6:7, :]
    wait_all(gathered, plane - 1, sum_send.at[2])


def hand_over(*refs):
    for source, target in zip(refs[:5], refs[5:]):
        target[...] = source[...]


def per_device(lat_count, lon_count, tracers, land_mask, level_counts, fold_partner, cotangent,
               w_first, b_first, w_second, b_second, w_head, b_head):
    field = (FIELDS, ROWS, COLS)
    ext = pltpu.VMEM((FIELDS, 32, COLS), F32)
    kap = pltpu.VMEM((NZ, 32, COLS), F32)
    feats = pltpu.VMEM((CHUNKS + 2, 64, COLS), F32)
    stack = pltpu.VMEM((CHUNKS, 2 * HID, LANES), BF16)
    dense = pltpu.VMEM((CHUNKS, HID, LANES), F32)
    tile = pltpu.VMEM((CHUNKS, 8, COLS), F32)
    sizes = place_sizes(lat_count, lon_count)
    plane = sizes["x"] * sizes["y_low"] * sizes["y_high"]
    pillar = sizes["core"] * sizes["z"]
    both = sum(piece_rows(plane))
    scratch = [
        pltpu.VMEM((8, HID), F32),
        pltpu.VMEM((HID, 32), BF16),
        pltpu.VMEM((16, 2 * HID), BF16),
        pltpu.VMEM((2 * HID, 2 * HID), BF16),
        pltpu.VMEM((2 * HID, 2 * HID), BF16),
        pltpu.VMEM((HID, COLS), F32),
        pltpu.VMEM((HID, COLS), F32),
        ext,
        pltpu.VMEM((4, NZ, ROWS, COLS), F32),
        ext, ext, ext, ext, kap, kap,
        pltpu.VMEM((4,) + field, F32),
        pltpu.VMEM((4,) + field, F32),
        pltpu.VMEM((4, NZ, ROWS, COLS), F32),
        pltpu.VMEM((4, NZ, ROWS, COLS), F32),
        tile, tile,
        pltpu.VMEM(field, F32),
        feats, feats,
        pltpu.VMEM((CHUNKS + 2, 8, COLS), F32),
        stack, stack, dense, dense, dense, dense, stack, stack,
        pltpu.VMEM((CHUNKS, 64, COLS), F32),
        pltpu.VMEM((CHUNKS, 64, COLS), F32),
        tile,
        pltpu.VMEM((2 * HID, 2 * HID), F32),
        pltpu.VMEM((16, 2 * HID), F32),
        pltpu.VMEM((HID, COLS), F32),
    ]
    scratch += [pltpu.VMEM((3, 2, 8, COLS), F32)] * 4
    scratch += [pltpu.VMEM((2, 16, COLS), F32)] * 2 + [pltpu.VMEM((2, 9, COLS), F32)] * 2
    scratch += [pltpu.VMEM((lon_count, 9, COLS), F32), pltpu.VMEM((3, lon_count, 8, COLS), F32)]
    scratch += [
        pltpu.VMEM((plane, both, COLS), F32),
        pltpu.VMEM((plane, both, COLS), F32),
        pltpu.VMEM((pillar, both, COLS), F32),
        pltpu.VMEM((plane, both, COLS), F32),
        pltpu.VMEM((8, COLS), F32),
        pltpu.SemaphoreType.DMA((4, 4)),
        pltpu.SemaphoreType.DMA((4, 4)),
        pltpu.SemaphoreType.DMA((4,)),
        pltpu.SemaphoreType.DMA((4,)),
        pltpu.SemaphoreType.DMA((3,)),
        pltpu.SemaphoreType.DMA((3,)),
        pltpu.SemaphoreType.DMA((10,)),
        pltpu.VMEM((ROWS, COLS), jnp.int32),
        pltpu.VMEM((ROWS, COLS), jnp.int32),
        pltpu.VMEM((1, COLS), jnp.int32),
        pltpu.VMEM((6, HID), F32),
        pltpu.VMEM((1, HID), F32),
        pltpu.VMEM((HID, HID), F32),
        pltpu.VMEM((1, HID), F32),
        pltpu.VMEM((1, HID), F32),
    ]
    vmem = pl.BlockSpec(memory_space=pltpu.VMEM)
    anywhere = pl.BlockSpec(memory_space=pl.ANY)
    run = pl.pallas_call(
        lambda *refs: kernel(lat_count, lon_count, *refs),
        out_shape=[
            pltpu.VMEM(field, F32),
            pltpu.VMEM(field, F32),
            pltpu.VMEM((6, HID), F32),
            pltpu.VMEM((HID, HID), F32),
            pltpu.VMEM((1, HID), F32),
        ],
        in_specs=[anywhere] * 10 + [pl.BlockSpec(memory_space=pltpu.SMEM)],
        out_specs=[vmem] * 5,
        scratch_shapes=scratch,
        compiler_params=pltpu.CompilerParams(
            collective_id=0, has_side_effects=True, vmem_limit_bytes=56 * 2**20
        ),
        name="adjoint_steps",
    )
    results = run(
        tracers.reshape(field), land_mask, level_counts, fold_partner.reshape(1, COLS),
        cotangent.reshape(field), w_first, b_first.reshape(1, HID), w_second,
        b_second.reshape(1, HID), w_head.reshape(1, HID), b_head,
    )
    out, grad, first, second, head = pl.pallas_call(
        hand_over,
        out_shape=[jax.ShapeDtypeStruct(r.shape, F32) for r in results],
        in_specs=[vmem] * 5,
        out_specs=[vmem] * 5,
        name="hand_over",
    )(*(pltpu.with_memory_space_constraint(r, pltpu.VMEM) for r in results))
    return (
        out.reshape(tracers.shape), grad.reshape(tracers.shape), first, second, head.reshape(HID)
    )


def solution(mesh):
    lat_count, lon_count = mesh.shape["lat"], mesh.shape["lon"]
    grid = P(None, None, "lat", "lon")
    return jax.shard_map(
        lambda *args: per_device(lat_count, lon_count, *args),
        mesh=mesh,
        in_specs=(
            grid, P("lat", "lon"), P("lat", "lon"), P("lon"), grid,
            P(), P(), P(), P(), P(), P(),
        ),
        out_specs=(grid, grid, P(), P(), P()),
        check_vma=False,
    )
```
